32 devices in a mesh: grp: 4 (over y, core), dev: 8 (over z, x).
Axes of the slice: x: 2, y: 2, z: 4, core: 2. Of those that a mesh axis runs over, the one named last changes fastest.
Arguments:
- colloc: bfloat16 [3072, 8000], P('dev', 'grp'), may hold values from -3 to 3
- block_colloc: bfloat16 [1024, 8000], P('dev', 'grp'), may hold values from -3 to 3
- factor: float32 [3072, 8192], P('dev', 'grp'), may hold values from -4.8 to 4.8
- block_factor: float32 [1024, 8192], P('dev', 'grp'), may hold values from -0.25 to 0.25
Outputs:
- block_lower: float32 [1024, 1024], P('dev')
- panel_lower: float32 [8, 384, 1024], P('dev', 'grp')
The draws below stay inside these ranges and needn't reach their ends.
All inputs are finite; a program needn't handle non-finite values.
Results may differ from the reference program's by a relative error of at most 0.0003.
Values may be sent and summed in bfloat16 or wider, within the bound.
No kernel may reach another device: no remote copies, remote signals or barrier semaphores. Data moves between devices by JAX's collectives and lax.ppermute only.
A program may use at most 64 MiB of HBM per device.

```python
import math
import jax
import jax.numpy as jnp
from jax import lax

NORB = 8000
PANEL_COLUMNS = 1024
FINISHED_COLUMNS = 8192
RB = 384
BANDS = 8
ROWS = 3072


NOISE_SHARE = 0.1


LOW_SCALE = 1.2


def orbital_terms(key):
    centers = jax.random.uniform(jax.random.fold_in(key, 7), (NORB,), jnp.float32, 0.0, 1.0)
    scales = jnp.exp(jax.random.uniform(jax.random.fold_in(key, 8), (NORB,), jnp.float32, -1.5, 1.5))
    amplitude = jnp.clip(jax.random.normal(jax.random.fold_in(key, 9), (NORB,), jnp.float32), -2.5, 2.5)
    return (centers, scales, amplitude)


def collocation(key, count_of_rows, salt_value):
    starting_key = jax.random.fold_in(key, salt_value)
    position_key, noise_key, row_key = jax.random.split(starting_key, 3)
    centers, scales, amplitude = orbital_terms(key)
    kernel_width = min(24.0 / PANEL_COLUMNS, 0.08)
    positions = jax.random.uniform(position_key, (count_of_rows, 1), jnp.float32, 0.0, 1.0)
    offset = positions - centers[None, :]
    offset = offset - jnp.floor(offset + 0.5)
    smooth = jnp.exp(-offset * offset / (2.0 * kernel_width * kernel_width)) * amplitude[None, :]
    smooth_scale = math.sqrt((1.0 - NOISE_SHARE) / (NORB * 3.3393 * kernel_width * 1.7724539))
    noise_scale = math.sqrt(NOISE_SHARE / (NORB * 3.3393))
    noise_part = jnp.clip(jax.random.normal(noise_key, (count_of_rows, NORB), jnp.float32), -5.0, 5.0)
    row_scales = jnp.exp(jax.random.uniform(row_key, (count_of_rows, 1), jnp.float32, -0.2231, 0.2231))
    value_entries = row_scales * scales[None, :] * (smooth_scale * smooth + noise_scale * noise_part)
    return jnp.clip(value_entries, -3.0, 3.0).astype(jnp.bfloat16)


def draw_colloc(key, part):
    return collocation(key, ROWS, 11)


def draw_block_colloc(key, part):
    return collocation(key, PANEL_COLUMNS, 13)


def factor_values(key, count_of_rows, dispersion, salt_value):
    starting_key = jax.random.fold_in(key, salt_value)
    value_entries = jnp.clip(jax.random.normal(starting_key, (count_of_rows, FINISHED_COLUMNS), jnp.float32), -4.0, 4.0)
    return (dispersion * value_entries).astype(jnp.float32)


def draw_block_factor(key, part):
    dispersion = math.sqrt(0.035) / (math.sqrt(PANEL_COLUMNS) + math.sqrt(FINISHED_COLUMNS))
    return factor_values(key, PANEL_COLUMNS, dispersion, 17)


def draw_factor(key, part):
    return factor_values(key, ROWS, LOW_SCALE, 19)


def setup_inputs(seed: int = 0) -> dict:
    key_of = jax.random.split(jax.random.key(seed), 5)
    colloc = draw_colloc(jax.random.fold_in(key_of[4], 71), 0)
    block_colloc = draw_block_colloc(jax.random.fold_in(key_of[4], 71), 0)
    factor = draw_factor(jax.random.fold_in(key_of[4], 71), 0)
    block_factor = draw_block_factor(jax.random.fold_in(key_of[4], 71), 0)
    return dict(colloc=colloc, block_colloc=block_colloc, factor=factor, block_factor=block_factor)


DAMPING = 0.0625

def reference(colloc, block_colloc, factor, block_factor):
    metric_block = jnp.dot(block_colloc.astype(jnp.float32), block_colloc.T.astype(jnp.float32), preferred_element_type=jnp.float32)
    gram_low = jnp.dot(colloc.astype(jnp.float32), block_colloc.T.astype(jnp.float32), preferred_element_type=jnp.float32)
    update_block = jnp.dot(block_factor.astype(jnp.float32), block_factor.T.astype(jnp.float32), precision=lax.Precision.HIGHEST, preferred_element_type=jnp.float32)
    update_low = jnp.dot(factor.astype(jnp.float32), block_factor.T.astype(jnp.float32), precision=lax.Precision.HIGHEST, preferred_element_type=jnp.float32)
    identity = jnp.eye(PANEL_COLUMNS, dtype=jnp.float32)
    schur = metric_block * metric_block + DAMPING * identity - update_block
    cholesky_factor = jnp.linalg.cholesky(schur)
    below_rows = gram_low * gram_low - update_low
    panel_rows = lax.linalg.triangular_solve(cholesky_factor, below_rows, left_side=False, lower=True, transpose_a=True)
    return (cholesky_factor, panel_rows.reshape(BANDS, RB, PANEL_COLUMNS))
```

```python
import jax
import jax.numpy as jnp
from jax import lax
from jax.sharding import PartitionSpec as P
from jax.experimental import pallas as pl
from jax.experimental.pallas import tpu as pltpu

DAMPING = 0.0625
LANES = 128
SUBS = 8


def split(value):
    high = value.astype(jnp.bfloat16)
    low = (value - high.astype(jnp.float32)).astype(jnp.bfloat16)
    return high, low


def dot3(left, right, contract):
    (left_high, left_low), (right_high, right_low) = left, right
    dims = (contract, ((), ()))

    def one(a, b):
        return lax.dot_general(a, b, dims, preferred_element_type=jnp.float32)

    return one(left_high, right_high) + (one(left_high, right_low) + one(left_low, right_high))


NN = ((1,), (0,))
NT = ((1,), (1,))


def reciprocal(value):
    guess = pl.reciprocal(value, approx=True)
    guess = guess * (2.0 - value * guess)
    return guess * (2.0 - value * guess)


def over_lanes(value, column):
    return jnp.broadcast_to(value[:, column : column + 1], (SUBS, LANES))


def over_subs(value, row):
    return jnp.broadcast_to(value[row : row + 1, :], (SUBS, LANES))


def factor_block(block):
    lane = lax.broadcasted_iota(jnp.int32, (SUBS, LANES), 1)
    sub = lax.broadcasted_iota(jnp.int32, (SUBS, LANES), 0)
    strips = LANES // SUBS
    rows = [block[SUBS * s : SUBS * (s + 1), :] for s in range(strips)]
    upper, inverse = [], []
    for s in range(strips):
        first = SUBS * s
        pivots = (lane >= first) & (lane < first + SUBS)
        own = rows[s]
        unit = jnp.where(lane - first == sub, 1.0, jnp.where(pivots, 0.0, own))
        columns = [over_lanes(own, first + k) for k in range(SUBS)]
        kept_own, kept_unit = own, unit
        diagonal, scale = None, None
        for k in range(SUBS):
            here = sub == k
            pivot = over_subs(columns[k], k)
            share = reciprocal(pivot)
            if k == 0:
                diagonal, scale = pivot, share
            else:
                diagonal = jnp.where(here, pivot, diagonal)
                scale = jnp.where(here, share, scale)
                kept_own = jnp.where(here, own, kept_own)
                kept_unit = jnp.where(here, unit, kept_unit)
            multiplier = jnp.where(here, 0.0, columns[k] * share)
            for q in range(k + 1, SUBS):
                columns[q] = columns[q] - multiplier * over_subs(columns[q], k)
            own = own - multiplier * over_subs(own, k)
            unit = unit - multiplier * over_subs(unit, k)
        root = lax.rsqrt(diagonal)
        upper.append(jnp.where(lane >= first + sub, kept_own * root, 0.0))
        inverse.append(jnp.where(lane <= first + sub, kept_unit * root, 0.0))
        solved = unit * scale
        spread = [over_subs(solved, k) for k in range(SUBS)]
        for i in range(s + 1, strips):
            value = jnp.where(pivots, 0.0, rows[i])
            for k in range(SUBS):
                value = value - over_lanes(rows[i], first + k) * spread[k]
            rows[i] = value
    return jnp.concatenate(upper, axis=0), jnp.concatenate(inverse, axis=0)


def panel_kernel(place_ref, schur_ref, below_ref, rows_ref, panel_ref, low_ref, high_part, low_part):
    size = schur_ref.shape[0]
    blocks = size // LANES
    zero = jnp.zeros((LANES, LANES), jnp.float32)

    def part(j, n=1):
        return slice(j * LANES, (j + n) * LANES)

    def left(j, count):
        return split(low_ref[part(j), : count * LANES])

    def right(count, cols):
        return high_part[: count * LANES, cols], low_part[: count * LANES, cols]

    diagonal = schur_ref[part(0), part(0)]
    for j in range(blocks):
        rest = slice((j + 1) * LANES, size)
        upper, inverse = factor_block(diagonal)
        inverse_parts = split(inverse)
        low_ref[part(j), part(j)] = upper.T
        for i in range(j):
            low_ref[part(i), part(j)] = zero
        if j + 1 < blocks:
            ahead = schur_ref[part(j), rest]
            next_diagonal = schur_ref[part(j + 1), part(j + 1)]
            if j:
                ahead = ahead - dot3(left(j, j), right(j, rest), NN)
                next_diagonal = next_diagonal - dot3(left(j + 1, j), right(j, part(j + 1)), NN)
            row = dot3(inverse_parts, split(ahead), NN)
            row_high, row_low = split(row)
            high_part[part(j), rest] = row_high
            low_part[part(j), rest] = row_low
            for i in range(j + 1, blocks):
                low_ref[part(i), part(j)] = row[:, part(i - j - 1)].T
            first = split(low_ref[part(j + 1), part(j)])
            diagonal = next_diagonal - dot3(first, (row_high[:, :LANES], row_low[:, :LANES]), NN)
        own = below_ref[:, part(j)]
        if j:
            own = own - dot3(split(panel_ref[:, : j * LANES]), right(j, part(j)), NN)
        panel_ref[:, part(j)] = dot3(split(own), inverse_parts, NT)
    band = rows_ref.shape[0]
    start = pl.multiple_of(place_ref[0] * band, SUBS)
    rows_ref[...] = low_ref[pl.ds(start, band), :]


def factor_panel(place, schur, below, band):
    size = schur.shape[0]
    return pl.pallas_call(
        panel_kernel,
        in_specs=[
            pl.BlockSpec(memory_space=pltpu.SMEM),
            pl.BlockSpec(memory_space=pltpu.VMEM),
            pl.BlockSpec(memory_space=pltpu.VMEM),
        ],
        out_specs=[pl.BlockSpec(memory_space=pltpu.VMEM), pl.BlockSpec(memory_space=pltpu.VMEM)],
        out_shape=[
            jax.ShapeDtypeStruct((band, size), jnp.float32),
            jax.ShapeDtypeStruct(below.shape, jnp.float32),
        ],
        scratch_shapes=[
            pltpu.VMEM((size, size), jnp.float32),
            pltpu.VMEM((size, size), jnp.bfloat16),
            pltpu.VMEM((size, size), jnp.bfloat16),
        ],
        compiler_params=pltpu.CompilerParams(vmem_limit_bytes=40 * 1024 * 1024),
        name="cholesky_panel",
    )(place, schur, below)


def with_damping(gram_part, update_part, row_index, col_index):
    return (
        gram_part * gram_part
        + jnp.where(row_index == col_index, jnp.float32(DAMPING), jnp.float32(0.0))
        - update_part
    )


def on_device(colloc, block_colloc, factor, block_factor):
    grp_count = lax.axis_size("grp")
    grp_index = lax.axis_index("grp")
    dev_index = lax.axis_index("dev")
    band_rows = block_colloc.shape[0]
    panel_width = band_rows * lax.axis_size("dev")
    points = jnp.concatenate([block_colloc, colloc], axis=0)
    earlier = jnp.concatenate([block_factor, factor], axis=0)
    metric_terms = lax.dot_general(
        points,
        lax.all_gather(block_colloc, "dev", axis=0, tiled=True),
        (((1,), (1,)), ((), ())),
        preferred_element_type=jnp.float32,
    )
    update_terms = lax.dot_general(
        earlier,
        lax.all_gather(block_factor, "dev", axis=0, tiled=True),
        (((1,), (1,)), ((), ())),
        precision=lax.Precision.HIGHEST,
        preferred_element_type=jnp.float32,
    )
    gram_low, update_low = (
        lax.psum_scatter(metric_terms[band_rows:], "grp", scatter_dimension=0, tiled=True),
        lax.psum_scatter(update_terms[band_rows:], "grp", scatter_dimension=0, tiled=True),
    )
    below_rows = gram_low * gram_low - update_low
    gram_head = metric_terms[:band_rows]
    update_head = update_terms[:band_rows]
    row_index = dev_index * band_rows + lax.broadcasted_iota(jnp.int32, (band_rows, 1), 0)
    slice_width = panel_width // grp_count
    slice_index = grp_index * slice_width + lax.broadcasted_iota(jnp.int32, (1, slice_width), 1)
    gram_slice, update_slice = (
        lax.psum_scatter(gram_head, "grp", scatter_dimension=1, tiled=True),
        lax.psum_scatter(update_head, "grp", scatter_dimension=1, tiled=True),
    )
    own_slice = with_damping(gram_slice, update_slice, row_index, slice_index)
    row_slab = lax.all_gather(own_slice, "grp", axis=1, tiled=True)
    schur = lax.all_gather(row_slab, "dev", axis=0, tiled=True)
    place = jnp.reshape(dev_index, (1,)).astype(jnp.int32)
    factor_rows, panel_rows = factor_panel(place, schur, below_rows, band_rows)
    return (factor_rows, panel_rows[None])


def solution(mesh):
    placed = (P("dev", "grp"), P("dev", "grp"), P("dev", "grp"), P("dev", "grp"))
    return jax.shard_map(
        on_device,
        mesh=mesh,
        in_specs=placed,
        out_specs=(P("dev", None), P("dev", "grp", None)),
        check_vma=False,
    )
```

```python
import jax
import jax.numpy as jnp
from jax import lax
from jax.sharding import PartitionSpec as P
from jax.experimental import pallas as pl
from jax.experimental.pallas import tpu as pltpu

DAMPING = 0.0625
SCALE = 896.0
LANES = 128
SUBS = 8


def split(value):
    high = value.astype(jnp.bfloat16)
    low = (value - high.astype(jnp.float32)).astype(jnp.bfloat16)
    return high, low


def dot3(left, right, contract):
    (left_high, left_low), (right_high, right_low) = left, right
    dims = (contract, ((), ()))

    def one(a, b):
        return lax.dot_general(a, b, dims, preferred_element_type=jnp.float32)

    return one(left_high, right_high) + (one(left_high, right_low) + one(left_low, right_high))


NN = ((1,), (0,))
NT = ((1,), (1,))


def reciprocal(value):
    guess = pl.reciprocal(value, approx=True)
    guess = guess * (2.0 - value * guess)
    return guess * (2.0 - value * guess)


def over_lanes(value, column):
    return jnp.broadcast_to(value[:, column : column + 1], (SUBS, LANES))


def over_subs(value, row):
    return jnp.broadcast_to(value[row : row + 1, :], (SUBS, LANES))


def factor_block(block):
    lane = lax.broadcasted_iota(jnp.int32, (SUBS, LANES), 1)
    sub = lax.broadcasted_iota(jnp.int32, (SUBS, LANES), 0)
    strips = LANES // SUBS
    rows = [block[SUBS * s : SUBS * (s + 1), :] for s in range(strips)]
    upper, inverse = [], []
    for s in range(strips):
        first = SUBS * s
        pivots = (lane >= first) & (lane < first + SUBS)
        own = rows[s]
        unit = jnp.where(lane - first == sub, 1.0, jnp.where(pivots, 0.0, own))
        columns = [over_lanes(own, first + k) for k in range(SUBS)]
        kept_own, kept_unit = own, unit
        diagonal, scale = None, None
        for k in range(SUBS):
            here = sub == k
            pivot = over_subs(columns[k], k)
            share = reciprocal(pivot)
            if k == 0:
                diagonal, scale = pivot, share
            else:
                diagonal = jnp.where(here, pivot, diagonal)
                scale = jnp.where(here, share, scale)
                kept_own = jnp.where(here, own, kept_own)
                kept_unit = jnp.where(here, unit, kept_unit)
            multiplier = jnp.where(here, 0.0, columns[k] * share)
            for q in range(k + 1, SUBS):
                columns[q] = columns[q] - multiplier * over_subs(columns[q], k)
            own = own - multiplier * over_subs(own, k)
            unit = unit - multiplier * over_subs(unit, k)
        root = lax.rsqrt(diagonal)
        upper.append(jnp.where(lane >= first + sub, kept_own * root, 0.0))
        inverse.append(jnp.where(lane <= first + sub, kept_unit * root, 0.0))
        solved = unit * scale
        spread = [over_subs(solved, k) for k in range(SUBS)]
        for i in range(s + 1, strips):
            value = jnp.where(pivots, 0.0, rows[i])
            for k in range(SUBS):
                value = value - over_lanes(rows[i], first + k) * spread[k]
            rows[i] = value
    return jnp.concatenate(upper, axis=0), jnp.concatenate(inverse, axis=0)


def pair_table(ring):
    half = ring // 2
    owners = {}
    for z in range(ring):
        for x in range(2):
            me = 2 * z + x
            pairs = [(me, 2 * ((z - t) % ring) + x) for t in range(half + 1)]
            pairs += [(me, 2 * ((z - t) % ring) + 1 - x) for t in range(half)]
            pairs += [(2 * ((z - half) % ring) + x, 2 * z + 1 - x)]
            for slot, pair in enumerate(pairs):
                owners.setdefault(pair, (me, slot))
    return owners, 2 * half + 2


def panel_kernel(ring, place_ref, *refs):
    devices = 2 * ring
    pieces = refs[: 2 * devices]
    below_ref, rows_ref, panel_ref, schur, low_ref, high_part, low_part, arrived = refs[2 * devices :]
    dev_index, side = place_ref[0], place_ref[1]
    own_z, own_x = dev_index // 2, lax.rem(dev_index, 2)
    owners, _ = pair_table(ring)
    blocks = devices
    size = blocks * LANES
    half_rows = LANES // 2
    zero = jnp.zeros((LANES, LANES), jnp.float32)

    copies = []
    for r in range(ring):
        for q in range(2):
            who = 2 * lax.rem(own_z - r + ring, ring) + lax.rem(own_x + q, 2)
            for other in range(2):
                at = pl.multiple_of(lax.rem(side + other, 2) * half_rows, half_rows)
                number = 2 * (2 * r + q) + other
                copies.append(
                    pltpu.make_async_copy(
                        pieces[number],
                        schur.at[who, :, pl.ds(at, half_rows), :],
                        arrived.at[number],
                    )
                )
    for copy in copies:
        copy.start()
    for copy in copies:
        copy.wait()

    def schur_block(i, j):
        if (i, j) in owners:
            who, slot = owners[i, j]
            return schur[who, slot]
        who, slot = owners[j, i]
        return schur[who, slot].T

    def below_block(j):
        rel = 2 * lax.rem(own_z - j // 2 + ring, ring) + lax.rem(own_x + j % 2, 2)
        return below_ref[rel]

    def part(j, n=1):
        return slice(j * LANES, (j + n) * LANES)

    def left(j, count):
        return split(low_ref[part(j), : count * LANES])

    def right(count, cols):
        return high_part[: count * LANES, cols], low_part[: count * LANES, cols]

    diagonal = schur_block(0, 0)
    for j in range(blocks):
        rest = slice((j + 1) * LANES, size)
        upper, inverse = factor_block(diagonal)
        inverse_parts = split(inverse)
        low_ref[part(j), part(j)] = upper.T
        for i in range(j):
            low_ref[part(i), part(j)] = zero
        if j + 1 < blocks:
            ahead = jnp.concatenate([schur_block(j, i) for i in range(j + 1, blocks)], axis=1)
            next_diagonal = schur_block(j + 1, j + 1)
            if j:
                ahead = ahead - dot3(left(j, j), right(j, rest), NN)
                next_diagonal = next_diagonal - dot3(left(j + 1, j), right(j, part(j + 1)), NN)
            row = dot3(inverse_parts, split(ahead), NN)
            row_high, row_low = split(row)
            high_part[part(j), rest] = row_high
            low_part[part(j), rest] = row_low
            for i in range(j + 1, blocks):
                low_ref[part(i), part(j)] = row[:, part(i - j - 1)].T
            first = split(low_ref[part(j + 1), part(j)])
            diagonal = next_diagonal - dot3(first, (row_high[:, :LANES], row_low[:, :LANES]), NN)
        own = below_block(j)
        if j:
            own = own - dot3(split(panel_ref[:, : j * LANES]), right(j, part(j)), NN)
        panel_ref[:, part(j)] = dot3(split(own), inverse_parts, NT)
    band = rows_ref.shape[0]
    start = pl.multiple_of(dev_index * band, SUBS)
    rows_ref[...] = low_ref[pl.ds(start, band), :]


def factor_panel(ring, place, pieces, below):
    blocks, rows, _ = below.shape
    size = blocks * LANES
    slots = pieces[0].shape[0]
    in_vmem = pl.BlockSpec(memory_space=pltpu.VMEM)
    anywhere = pl.BlockSpec(memory_space=pl.ANY)

    def kernel(*refs):
        panel_kernel(ring, *refs)

    return pl.pallas_call(
        kernel,
        in_specs=[pl.BlockSpec(memory_space=pltpu.SMEM)] + [anywhere] * len(pieces) + [in_vmem],
        out_specs=[in_vmem, in_vmem],
        out_shape=[
            jax.ShapeDtypeStruct((LANES, size), jnp.float32),
            jax.ShapeDtypeStruct((rows, size), jnp.float32),
        ],
        scratch_shapes=[
            pltpu.VMEM((blocks, slots, LANES, LANES), jnp.float32),
            pltpu.VMEM((size, size), jnp.float32),
            pltpu.VMEM((size, size), jnp.bfloat16),
            pltpu.VMEM((size, size), jnp.bfloat16),
            pltpu.SemaphoreType.DMA((len(pieces),)),
        ],
        compiler_params=pltpu.CompilerParams(vmem_limit_bytes=40 * 1024 * 1024),
        name="cholesky_panel",
    )(place, *pieces, below)


def pick(value, axis, index):
    return lax.dynamic_index_in_dim(value, index, axis, keepdims=False)


def ring_step(value, ring):
    return lax.ppermute(value, "dev", [(2 * z + x, 2 * ((z + 1) % ring) + x) for z in range(ring) for x in range(2)])


def swap(value, axis, bit):
    return lax.ppermute(value, axis, [(i, i ^ bit) for i in range(lax.axis_size(axis))])


def sum_rows(value):
    count, index = lax.axis_size("grp"), lax.axis_index("grp")
    n, rows, width = value.shape
    value = value.reshape(n, count, rows // count, width)
    bit = 1
    while bit < count:
        mine = lax.rem(index // bit, 2)
        value = value.reshape(n, value.shape[1] // 2, 2, rows // count, width)
        value = pick(value, 2, mine) + swap(pick(value, 2, 1 - mine), "grp", bit)
        bit *= 2
    return value.reshape(n, rows // count, width)


def sum_half(value):
    count, index = lax.axis_size("grp"), lax.axis_index("grp")
    n, rows, width = value.shape
    side = lax.rem(index, 2)
    value = value.reshape(n, 2, rows // 2, width)
    value = pick(value, 1, side) + swap(pick(value, 1, 1 - side), "grp", 1)
    bit = 2
    while bit < count:
        value = value + swap(value, "grp", bit)
        bit *= 2
    return value


def coded(value):
    value = value * SCALE
    return (value * jnp.abs(value)).astype(jnp.float16)


def on_grid(colloc, block_colloc, factor, block_factor):
    ring = lax.axis_size("dev") // 2
    half = ring // 2
    dev_index, grp_index = lax.axis_index("dev"), lax.axis_index("grp")
    side = lax.rem(grp_index, 2)

    own = (block_colloc, coded(block_factor))
    along, across = [own], []
    for t in range(ring):
        across.append(tuple(swap(v, "dev", 1) for v in along[t]))
        if t + 1 < ring:
            along.append(tuple(ring_step(v, ring) for v in along[t]))

    def widen(value):
        value = value.astype(jnp.float32)
        root = jnp.sqrt(jnp.abs(value)) * jnp.float32(1.0 / SCALE)
        return jnp.where(value < 0.0, -root, root)

    points = jnp.concatenate([block_colloc, colloc], axis=0)
    earlier = jnp.concatenate([widen(own[1]), factor], axis=0)
    dims = (((1,), (1,)), ((), ()))

    def gram(left, right):
        return lax.dot_general(left, right, dims, preferred_element_type=jnp.float32)

    def update(left, right):
        return lax.dot_general(
            left, right, dims, precision=lax.Precision.HIGH, preferred_element_type=jnp.float32
        )

    def terms(other):
        return gram(points, other[0]), update(earlier, widen(other[1]))

    along_terms = [terms(v) for v in along]
    across_terms = [terms(v) for v in across]

    head = [v for v in along_terms[: half + 1]] + [v for v in across_terms[:half]]
    head_gram = [v[0][:LANES] for v in head] + [gram(along[half][0], across[0][0])]
    head_update = [v[1][:LANES] for v in head] + [update(widen(along[half][1]), widen(across[0][1]))]
    slots = len(head_gram)
    total = sum_half(jnp.stack(head_gram + head_update))
    slot = lax.broadcasted_iota(jnp.int32, total[:slots].shape, 0)
    row = lax.broadcasted_iota(jnp.int32, total[:slots].shape, 1) + side * total.shape[1]
    col = lax.broadcasted_iota(jnp.int32, total[:slots].shape, 2)
    damping = jnp.where((slot == 0) & (row == col), jnp.float32(DAMPING), jnp.float32(0.0))
    piece = total[:slots] * total[:slots] + damping - total[slots:]

    pieces = []
    for r in range(ring):
        for q in range(2):
            held = swap(piece, "dev", 1) if q else piece
            pieces += [held, swap(held, "grp", 1)]
        if r + 1 < ring:
            piece = ring_step(piece, ring)

    order = [v for pair in zip(along_terms, across_terms) for v in pair]
    early = [2 * t for t in range(half + 1)] + [2 * t + 1 for t in range(half)]
    late = [i for i in range(len(order)) if i not in early]
    below = [None] * len(order)
    for chosen in (early, late):
        stacked = jnp.stack([order[i][0][LANES:] for i in chosen] + [order[i][1][LANES:] for i in chosen])
        summed = sum_rows(stacked)
        part = summed[: len(chosen)] * summed[: len(chosen)] - summed[len(chosen) :]
        for n, i in enumerate(chosen):
            below[i] = part[n]
    below = jnp.stack(below)

    place = jnp.stack([dev_index, side]).astype(jnp.int32)
    factor_rows, panel_rows = factor_panel(ring, place, pieces, below)
    return factor_rows, panel_rows[None]


def whole_kernel(place_ref, schur_ref, below_ref, rows_ref, panel_ref, low_ref, high_part, low_part):
    size = schur_ref.shape[0]
    blocks = size // LANES
    zero = jnp.zeros((LANES, LANES), jnp.float32)

    def part(j, n=1):
        return slice(j * LANES, (j + n) * LANES)

    for j in range(blocks):
        cols, rest = part(j), slice((j + 1) * LANES, size)
        here = schur_ref[part(j), j * LANES :]
        own = below_ref[:, cols]
        if j:
            done = slice(0, j * LANES)
            here = here - dot3(split(low_ref[part(j), done]), (high_part[done, j * LANES :], low_part[done, j * LANES :]), NN)
            own = own - dot3(split(panel_ref[:, done]), (high_part[done, cols], low_part[done, cols]), NN)
        upper, inverse = factor_block(here[:, :LANES])
        inverse_parts = split(inverse)
        low_ref[part(j), cols] = upper.T
        for i in range(j):
            low_ref[part(i), cols] = zero
        if j + 1 < blocks:
            row = dot3(inverse_parts, split(here[:, LANES:]), NN)
            high_part[part(j), rest], low_part[part(j), rest] = split(row)
            for i in range(j + 1, blocks):
                low_ref[part(i), cols] = row[:, part(i - j - 1)].T
        panel_ref[:, cols] = dot3(split(own), inverse_parts, NT)
    band = rows_ref.shape[0]
    start = pl.multiple_of(place_ref[0] * band, SUBS)
    rows_ref[...] = low_ref[pl.ds(start, band), :]


def factor_whole(place, schur, below, band):
    size = schur.shape[0]
    in_vmem = pl.BlockSpec(memory_space=pltpu.VMEM)
    return pl.pallas_call(
        whole_kernel,
        in_specs=[pl.BlockSpec(memory_space=pltpu.SMEM), in_vmem, in_vmem],
        out_specs=[in_vmem, in_vmem],
        out_shape=[
            jax.ShapeDtypeStruct((band, size), jnp.float32),
            jax.ShapeDtypeStruct(below.shape, jnp.float32),
        ],
        scratch_shapes=[
            pltpu.VMEM((size, size), jnp.float32),
            pltpu.VMEM((size, size), jnp.bfloat16),
            pltpu.VMEM((size, size), jnp.bfloat16),
        ],
        compiler_params=pltpu.CompilerParams(vmem_limit_bytes=40 * 1024 * 1024),
        name="cholesky_whole",
    )(place, schur, below)


def on_any(colloc, block_colloc, factor, block_factor):
    grp_count, grp_index, dev_index = lax.axis_size("grp"), lax.axis_index("grp"), lax.axis_index("dev")
    band = block_colloc.shape[0]
    width = band * lax.axis_size("dev")
    points = jnp.concatenate([block_colloc, colloc], axis=0)
    earlier = jnp.concatenate([block_factor, factor], axis=0)
    dims = (((1,), (1,)), ((), ()))
    gram = lax.dot_general(
        points, lax.all_gather(block_colloc, "dev", axis=0, tiled=True), dims, preferred_element_type=jnp.float32
    )
    update = lax.dot_general(
        earlier,
        lax.all_gather(block_factor, "dev", axis=0, tiled=True),
        dims,
        precision=lax.Precision.HIGHEST,
        preferred_element_type=jnp.float32,
    )
    gram_low = lax.psum_scatter(gram[band:], "grp", scatter_dimension=0, tiled=True)
    update_low = lax.psum_scatter(update[band:], "grp", scatter_dimension=0, tiled=True)
    below = gram_low * gram_low - update_low
    slice_width = width // grp_count
    row = dev_index * band + lax.broadcasted_iota(jnp.int32, (band, slice_width), 0)
    col = grp_index * slice_width + lax.broadcasted_iota(jnp.int32, (band, slice_width), 1)
    gram_slice = lax.psum_scatter(gram[:band], "grp", scatter_dimension=1, tiled=True)
    update_slice = lax.psum_scatter(update[:band], "grp", scatter_dimension=1, tiled=True)
    damping = jnp.where(row == col, jnp.float32(DAMPING), jnp.float32(0.0))
    piece = gram_slice * gram_slice + damping - update_slice
    slab = lax.all_gather(piece, "grp", axis=1, tiled=True)
    schur = lax.all_gather(slab, "dev", axis=0, tiled=True)
    place = jnp.reshape(dev_index, (1,)).astype(jnp.int32)
    factor_rows, panel_rows = factor_whole(place, schur, below, band)
    return factor_rows, panel_rows[None]


def on_device(colloc, block_colloc, factor, block_factor):
    devices, count = lax.axis_size("dev"), lax.axis_size("grp")
    gridded = devices % 4 == 0 and block_colloc.shape[0] == LANES and count >= 2 and count & (count - 1) == 0
    form = on_grid if gridded else on_any
    return form(colloc, block_colloc, factor, block_factor)


def solution(mesh):
    placed = (P("dev", "grp"), P("dev", "grp"), P("dev", "grp"), P("dev", "grp"))
    return jax.shard_map(
        on_device,
        mesh=mesh,
        in_specs=placed,
        out_specs=(P("dev", None), P("dev", "grp", None)),
        check_vma=False,
    )
```

```python
import jax
import jax.numpy as jnp
from jax import lax
from jax.sharding import PartitionSpec as P
from jax.experimental import pallas as pl
from jax.experimental.pallas import tpu as pltpu

DAMPING = 0.0625
SCALE = 896.0
LANES = 128
SUBS = 8
NN = ((1,), (0,))
NT = ((1,), (1,))


def split(value):
    high = value.astype(jnp.bfloat16)
    low = (value - high.astype(jnp.float32)).astype(jnp.bfloat16)
    return high, low


def dot3(left, right, contract):
    (left_high, left_low), (right_high, right_low) = left, right
    dims = (contract, ((), ()))

    def one(a, b):
        return lax.dot_general(a, b, dims, preferred_element_type=jnp.float32)

    return one(left_high, right_high) + (one(left_high, right_low) + one(left_low, right_high))


def reciprocal(value):
    return pl.reciprocal(value, approx=True)


def over_lanes(value, column):
    return jnp.broadcast_to(value[:, column : column + 1], (SUBS, LANES))


def over_subs(value, row):
    return jnp.broadcast_to(value[row : row + 1, :], (SUBS, LANES))


def tree_sum(values):
    while len(values) > 1:
        values = [a + b for a, b in zip(values[::2], values[1::2])] + values[len(values) // 2 * 2 :]
    return values[0]


def factor_block(block):
    lane = lax.broadcasted_iota(jnp.int32, (SUBS, LANES), 1)
    sub = lax.broadcasted_iota(jnp.int32, (SUBS, LANES), 0)
    strips = LANES // SUBS
    rows = [block[SUBS * s : SUBS * (s + 1), :] for s in range(strips)]
    upper, inverse = [], []
    for s in range(strips):
        first = SUBS * s
        pivots = (lane >= first) & (lane < first + SUBS)
        own = rows[s]
        unit = jnp.where(lane - first == sub, 1.0, jnp.where(pivots, 0.0, own))
        columns = [over_lanes(own, first + k) for k in range(SUBS)]
        kept_own, kept_unit, diagonal = own, unit, None
        for k in range(0, SUBS, 2):
            one, two = sub == k, sub == k + 1
            both = one | two
            a, b, c = over_subs(columns[k], k), over_subs(columns[k + 1], k), over_subs(columns[k + 1], k + 1)
            det = a * c - b * b
            share = reciprocal(det)
            lead = jnp.where(one, c, jnp.where(two, -b, columns[k + 1] * b - columns[k] * c)) * share
            trail = jnp.where(one, -b, jnp.where(two, a, columns[k] * b - columns[k + 1] * a)) * share

            def swept(value):
                return jnp.where(both, 0.0, value) + (lead * over_subs(value, k) + trail * over_subs(value, k + 1))

            inverse_a = reciprocal(a)
            ratio = b * inverse_a
            second = det * inverse_a
            if k == 0:
                diagonal = jnp.where(two, second, a)
            else:
                diagonal = jnp.where(one, a, jnp.where(two, second, diagonal))
            kept_own = jnp.where(one, own, jnp.where(two, own - ratio * over_subs(own, k), kept_own))
            kept_unit = jnp.where(one, unit, jnp.where(two, unit - ratio * over_subs(unit, k), kept_unit))
            for q in range(k + 2, SUBS):
                columns[q] = swept(columns[q])
            own, unit = swept(own), swept(unit)
        root = lax.rsqrt(diagonal)
        upper.append(jnp.where(lane >= first + sub, kept_own * root, 0.0))
        inverse.append(jnp.where(lane <= first + sub, kept_unit * root, 0.0))
        spread = [over_subs(unit, k) for k in range(SUBS)]
        for i in range(s + 1, strips):
            change = tree_sum([over_lanes(rows[i], first + k) * spread[k] for k in range(SUBS)])
            rows[i] = jnp.where(pivots, 0.0, rows[i]) - change
    return jnp.concatenate(upper, axis=0), jnp.concatenate(inverse, axis=0)


def part(j, n=1):
    return slice(j * LANES, (j + n) * LANES)


def factor_rows(count, total, block_at, low_ref, high_ref, low_part_ref, inverse_refs, rest_ref):
    zero = jnp.zeros((LANES, LANES), jnp.float32)

    def left(i, first, n):
        return split(low_ref[part(i), part(first, n)])

    def right(first, n, cols):
        return high_ref[part(first, n), cols], low_part_ref[part(first, n), cols]

    diagonal = block_at(0, 0)
    remainder = {}
    for j in range(count):
        rest = slice((j + 1) * LANES, total * LANES)
        if j + 1 < total:
            ahead = jnp.concatenate([block_at(j, i) for i in range(j + 1, total)], axis=1)
            if j:
                ahead = ahead - dot3(left(j, 0, j), right(0, j, rest), NN)
        if j + 1 < count:
            next_diagonal = block_at(j + 1, j + 1)
            if j:
                next_diagonal = next_diagonal - dot3(left(j + 1, 0, j), right(0, j, part(j + 1)), NN)
        else:
            for i in range(count, total):
                cols = slice(i * LANES, total * LANES)
                value = jnp.concatenate([block_at(i, n) for n in range(i, total)], axis=1)
                if j:
                    value = value - dot3(left(i, 0, j), right(0, j, cols), NN)
                remainder[i] = value
        upper, inverse = factor_block(diagonal)
        inverse_parts = split(inverse)
        for ref, value in zip(inverse_refs, inverse_parts):
            ref[part(j), :] = value
        low_ref[part(j), part(j)] = upper.T
        for i in range(j):
            low_ref[part(i), part(j)] = zero
        if j + 1 < total:
            row = dot3(inverse_parts, split(ahead), NN)
            row_parts = split(row)
            high_ref[part(j), rest], low_part_ref[part(j), rest] = row_parts
            for i in range(j + 1, total):
                low_ref[part(i), part(j)] = row[:, part(i - j - 1)].T
        if j + 1 < count:
            first = tuple(v[:, :LANES] for v in row_parts)
            diagonal = next_diagonal - dot3(left(j + 1, j, 1), first, NN)
    for i in range(count, total):
        cols = slice(i * LANES, total * LANES)
        value = remainder[i] - dot3(left(i, count - 1, 1), right(count - 1, 1, cols), NN)
        rest_ref[part(i - count), part(i - count, total - i)] = value


def first_kernel(ring, count, place_ref, *refs):
    devices = 2 * ring
    pieces = refs[: 2 * devices]
    rows_ref, high_ref, low_part_ref, inverse_high, inverse_low, rest_ref, schur, low_ref, arrived = refs[2 * devices :]
    dev_index, side = place_ref[0], place_ref[1]
    own_z, own_x = dev_index // 2, lax.rem(dev_index, 2)
    half_rows = LANES // 2
    copies = []
    for r in range(ring):
        for q in range(2):
            who = 2 * lax.rem(own_z - r + ring, ring) + lax.rem(own_x + q, 2)
            for other in range(2):
                at = pl.multiple_of(lax.rem(side + other, 2) * half_rows, half_rows)
                number = 2 * (2 * r + q) + other
                copies.append(
                    pltpu.make_async_copy(
                        pieces[number], schur.at[who, :, pl.ds(at, half_rows), :], arrived.at[number]
                    )
                )
    for copy in copies:
        copy.start()
    for copy in copies:
        copy.wait()

    owners, _ = pair_table(ring)

    def block_at(i, j):
        found = []
        for who, slot in owners.get((i, j), ()):
            found.append(schur[who, slot])
        if i != j:
            for who, slot in owners.get((j, i), ()):
                found.append(schur[who, slot].T)
        return tree_sum(found)

    factor_rows(count, devices, block_at, low_ref, high_ref, low_part_ref, (inverse_high, inverse_low), rest_ref)
    start = pl.multiple_of(dev_index * LANES, LANES)
    rows_ref[...] = low_ref[pl.ds(start, LANES), :]


def second_kernel(place_ref, start_ref, rows_ref, out_ref, high_ref, low_part_ref, inverse_high, inverse_low, low_ref):
    count = start_ref.shape[0] // LANES
    done = rows_ref.shape[1]

    def block_at(i, j):
        return start_ref[part(i), part(j)]

    factor_rows(count, count, block_at, low_ref, high_ref, low_part_ref, (inverse_high, inverse_low), None)
    out_ref[:, :done] = rows_ref[...]
    dev_index = place_ref[0]
    row = dev_index * LANES - done
    at = pl.multiple_of(jnp.maximum(row, 0), LANES)
    out_ref[:, done:] = jnp.where(row >= 0, low_ref[pl.ds(at, LANES), :], 0.0)


def solve_kernel(ring, early, late, place_ref, early_ref, late_ref, *refs):
    first, second, (panel_ref, held) = refs[:4], refs[4:8], refs[8:]
    blocks = 2 * ring
    own_z, own_x = place_ref[0] // 2, lax.rem(place_ref[0], 2)
    for ref, places in ((early_ref, early), (late_ref, late)):
        for n, place in enumerate(places):
            who = 2 * lax.rem(own_z - place // 2 + ring, ring) + lax.rem(own_x + place % 2, 2)
            held[who] = ref[n]
    below = jnp.concatenate([held[i] for i in range(blocks)], axis=1)
    count = first[0].shape[0] // LANES
    for j in range(blocks):
        high, low, inverse_high, inverse_low = first if j < count else second
        n, skip = (j, 0) if j < count else (j - count, count)
        value = dot3(split(below[:, :LANES]), (inverse_high[part(n), :], inverse_low[part(n), :]), NT)
        panel_ref[:, part(j)] = value
        if j + 1 < blocks:
            rest = slice((j + 1 - skip) * LANES, (blocks - skip) * LANES)
            parts = split(value)
            below = below[:, LANES:] - dot3(parts, (high[part(n), rest], low[part(n), rest]), NN)


IN_VMEM = pl.BlockSpec(memory_space=pltpu.VMEM)
IN_SMEM = pl.BlockSpec(memory_space=pltpu.SMEM)
ANYWHERE = pl.BlockSpec(memory_space=pl.ANY)


def params():
    return pltpu.CompilerParams(vmem_limit_bytes=40 * 1024 * 1024)


def effort(steps):
    return pl.CostEstimate(flops=steps * 40_000_000, bytes_accessed=0, transcendentals=0)


def factor_shapes(count, total):
    tall, wide = count * LANES, total * LANES
    return [
        jax.ShapeDtypeStruct((tall, wide), jnp.bfloat16),
        jax.ShapeDtypeStruct((tall, wide), jnp.bfloat16),
        jax.ShapeDtypeStruct((tall, LANES), jnp.bfloat16),
        jax.ShapeDtypeStruct((tall, LANES), jnp.bfloat16),
    ]


def factor_first(ring, count, place, pieces):
    blocks = 2 * ring
    slots = pieces[0].shape[0]

    def kernel(*refs):
        first_kernel(ring, count, *refs)

    left = (blocks - count) * LANES
    return pl.pallas_call(
        kernel,
        in_specs=[IN_SMEM] + [ANYWHERE] * len(pieces),
        out_specs=[IN_VMEM] * 6,
        out_shape=[jax.ShapeDtypeStruct((LANES, count * LANES), jnp.float32)]
        + factor_shapes(count, blocks)
        + [jax.ShapeDtypeStruct((left, left), jnp.float32)],
        scratch_shapes=[
            pltpu.VMEM((blocks, slots, LANES, LANES), jnp.float32),
            pltpu.VMEM((blocks * LANES, count * LANES), jnp.float32),
            pltpu.SemaphoreType.DMA((len(pieces),)),
        ],
        compiler_params=params(),
        cost_estimate=effort(count * LANES),
        name="cholesky_first",
    )(place, *pieces)


def factor_second(place, start, rows):
    size = start.shape[0]
    count = size // LANES
    return pl.pallas_call(
        second_kernel,
        in_specs=[IN_SMEM, IN_VMEM, IN_VMEM],
        out_specs=[IN_VMEM] * 5,
        out_shape=[jax.ShapeDtypeStruct((LANES, rows.shape[1] + size), jnp.float32)] + factor_shapes(count, count),
        scratch_shapes=[pltpu.VMEM((size, size), jnp.float32)],
        compiler_params=params(),
        cost_estimate=effort(size),
        name="cholesky_second",
    )(place, start, rows)


def solve_panel(ring, early, late, place, below_early, below_late, first, second):
    rows, blocks = below_early.shape[1], 2 * ring

    def kernel(*refs):
        solve_kernel(ring, early, late, *refs)

    return pl.pallas_call(
        kernel,
        in_specs=[IN_SMEM] + [IN_VMEM] * 10,
        out_specs=IN_VMEM,
        out_shape=jax.ShapeDtypeStruct((rows, blocks * LANES), jnp.float32),
        scratch_shapes=[pltpu.VMEM((blocks, rows, LANES), jnp.float32)],
        compiler_params=params(),
        cost_estimate=effort(LANES),
        name="panel_solve",
    )(place, below_early, below_late, *first, *second)


def pair_table(ring):
    half = ring // 2
    owners = {}
    for z in range(ring):
        for x in range(2):
            me, across = 2 * z + x, 2 * z + 1 - x

            def back(t):
                return 2 * ((z - t) % ring) + x

            pairs = [(me, me)] + [(me, back(t)) for t in range(1, half)]
            pairs += [(across, back(t)) for t in range(1, half)]
            pairs += [(me, across), (me, back(half)), (across, back(half))]
            for slot, pair in enumerate(pairs):
                owners.setdefault(pair, []).append((me, slot))
    return owners, 2 * half + 2


def pick(value, axis, index):
    return lax.dynamic_index_in_dim(value, index, axis, keepdims=False)


def ring_step(value, ring, chosen=None):
    steps = [(2 * z + x, 2 * ((z + 1) % ring) + x) for z in range(ring) for x in range(2)]
    return lax.ppermute(value, "dev", [s for s in steps if chosen is None or chosen(s[1] // 2)])


def swap(value, axis, bit, chosen=None):
    steps = [(i, i ^ bit) for i in range(lax.axis_size(axis))]
    return lax.ppermute(value, axis, [s for s in steps if chosen is None or chosen(s[1] // 2)])


def after(value, *first):
    return lax.optimization_barrier((value, *first))[0]


def halve(value, bit):
    mine = lax.rem(lax.axis_index("grp") // bit, 2)
    return pick(value, 1, mine) + swap(pick(value, 1, 1 - mine), "grp", bit)


def parts_for(value):
    count, index = lax.axis_size("grp"), lax.axis_index("grp")
    n, rows, width = value.shape
    value = value.reshape(n, count, rows // count, width)
    return [pick(value, 1, index ^ k) for k in range(count)]


def exchanged(parts):
    return [parts[0]] + [swap(v, "grp", k) for k, v in enumerate(parts) if k]


def sum_half(value):
    n, rows, width = value.shape
    value = halve(value.reshape(n, 2, rows // 2, width), 1)
    bit = 2
    while bit < lax.axis_size("grp"):
        value = value + swap(value, "grp", bit)
        bit *= 2
    return value


def coded(value):
    value = value * SCALE
    return (value * jnp.abs(value)).astype(jnp.float16)


def widen(value):
    value = value.astype(jnp.float32)
    root = jnp.sqrt(jnp.abs(value)) * jnp.float32(1.0 / SCALE)
    return jnp.where(value < 0.0, -root, root)


DIMS = (((1,), (1,)), ((), ()))


def gram(left, right):
    return lax.dot_general(left, right, DIMS, preferred_element_type=jnp.float32)


def update(left, right):
    return lax.dot_general(left, right, DIMS, precision=lax.Precision.HIGH, preferred_element_type=jnp.float32)


def on_grid(colloc, block_colloc, factor, block_factor):
    ring = lax.axis_size("dev") // 2
    half = ring // 2
    dev_index, grp_index = lax.axis_index("dev"), lax.axis_index("grp")
    own_z, own_x, side = dev_index // 2, lax.rem(dev_index, 2), lax.rem(grp_index, 2)
    upper_z, first_x = own_z >= half, own_x == 0

    def is_upper(z):
        return z >= half

    def is_lower(z):
        return z < half

    def step(v):
        return ring_step(v, ring)

    def cross(v):
        return swap(v, "dev", 1)

    colloc_along, factor_along = [block_colloc], [coded(block_factor)]
    colloc_across, factor_across = [cross(block_colloc)], [cross(factor_along[0])]
    for t in range(1, half):
        colloc_along.append(step(colloc_along[-1]))
        factor_along.append(step(factor_along[-1]))
    colloc_first, factor_first_part = (
        ring_step(colloc_along[-1], ring, is_upper),
        ring_step(factor_along[-1], ring, is_lower),
    )
    for t in range(1, half):
        factor_across.append(cross(factor_along[t]))
        colloc_across.append(cross(colloc_along[t]))

    own_factor = widen(factor_along[0])
    across_factor = widen(factor_across[0])
    corner_colloc = jnp.concatenate([block_colloc, colloc_across[0]], axis=0)
    corner_factor = jnp.concatenate([own_factor, across_factor], axis=0)
    head_gram = [gram(block_colloc, block_colloc)]
    head_update = [update(own_factor, own_factor)]
    middle = [
        (gram(corner_colloc, colloc_along[t]), update(corner_factor, widen(factor_along[t]))) for t in range(1, half)
    ]
    for rows in (slice(0, LANES), slice(LANES, 2 * LANES)):
        head_gram += [v[0][rows] for v in middle]
        head_update += [v[1][rows] for v in middle]
    facing = jnp.where(first_x, gram(block_colloc, colloc_across[0]), update(own_factor, across_factor))
    far = gram(corner_colloc, colloc_first) + update(corner_factor, widen(factor_first_part))
    full = len(head_gram)
    total = sum_half(jnp.stack(head_gram + head_update + [facing, far[:LANES], far[LANES:]]))
    row = lax.broadcasted_iota(jnp.int32, total.shape[1:], 0) + side * total.shape[1]
    col = lax.broadcasted_iota(jnp.int32, total.shape[1:], 1)
    damping = jnp.where(row == col, jnp.float32(DAMPING), jnp.float32(0.0))
    slots = [total[n] * total[n] - total[full + n] for n in range(full)]
    slots[0] = slots[0] + damping
    for n, squared in ((2 * full, first_x), (2 * full + 1, upper_z), (2 * full + 2, upper_z)):
        slots.append(jnp.where(squared, total[n] * total[n], -total[n]))
    piece = jnp.stack(slots)

    colloc_second, factor_second_part = (
        ring_step(colloc_along[-1], ring, is_lower),
        ring_step(factor_along[-1], ring, is_upper),
    )
    colloc_across_parts = [swap(colloc_first, "dev", 1, is_upper), swap(colloc_second, "dev", 1, is_lower)]
    factor_across_parts = [swap(factor_first_part, "dev", 1, is_lower), swap(factor_second_part, "dev", 1, is_upper)]
    colloc_along.append(jnp.where(upper_z, colloc_first, colloc_second))
    factor_along.append(jnp.where(upper_z, factor_second_part, factor_first_part))
    colloc_across.append(jnp.where(upper_z, *colloc_across_parts))
    factor_across.append(jnp.where(upper_z, factor_across_parts[1], factor_across_parts[0]))

    hops = [piece]
    for r in range(1, ring):
        hops.append(step(hops[-1]))
    pieces = []
    for hop in hops:
        crossed = cross(hop)
        pieces += [hop, swap(hop, "grp", 1), crossed, swap(crossed, "grp", 1)]

    for t in range(half + 1, ring):
        colloc_along.append(step(colloc_along[-1]))
        factor_along.append(step(after(factor_along[-1], hops[half])))
        colloc_across.append(cross(colloc_along[-1]))
        factor_across.append(cross(factor_along[-1]))

    def low_terms(colloc_rows, factor_rows):
        return gram(colloc, colloc_rows), update(factor, widen(factor_rows))

    def stacked(terms):
        return jnp.stack([v[0] for v in terms] + [v[1] for v in terms])

    def ended(parts, first):
        summed = tree_sum(after(parts, first))
        n = summed.shape[0] // 2
        return summed[:n] * summed[:n] - summed[n:]

    blocks = [pair for t in range(ring) for pair in ((colloc_along[t], factor_along[t]), (colloc_across[t], factor_across[t]))]
    soon, early, late = list(range(2 * half - 1)), [2 * half - 1, 2 * half], list(range(2 * half + 1, 2 * ring))
    terms = [low_terms(*blocks[i]) for i in soon]
    terms += [low_terms(*after(blocks[i], hops[1])) for i in early]
    parts_early = parts_for(stacked(terms))
    sums_early = exchanged(parts_early)

    place = jnp.stack([dev_index, side]).astype(jnp.int32)
    pieces[0] = after(pieces[0], parts_early)
    rows, *first, start = factor_first(ring, ring, place, pieces)

    terms = [low_terms(*v) for v in after([blocks[i] for i in late], start)]
    parts_late = parts_for(stacked(terms))
    sums_late = exchanged(parts_late)
    factor_out, *second = factor_second(place, after(start, parts_late), rows)
    below_early, below_late = ended(sums_early, factor_out), ended(sums_late, factor_out)
    panel = solve_panel(ring, soon + early, late, place, below_early, below_late, first, second)
    return factor_out, panel[None]


def whole_kernel(place_ref, schur_ref, below_ref, rows_ref, panel_ref, low_ref, high_part, low_part):
    size = schur_ref.shape[0]
    blocks = size // LANES
    zero = jnp.zeros((LANES, LANES), jnp.float32)

    def part(j, n=1):
        return slice(j * LANES, (j + n) * LANES)

    for j in range(blocks):
        cols, rest = part(j), slice((j + 1) * LANES, size)
        here = schur_ref[part(j), j * LANES :]
        own = below_ref[:, cols]
        if j:
            done = slice(0, j * LANES)
            here = here - dot3(split(low_ref[part(j), done]), (high_part[done, j * LANES :], low_part[done, j * LANES :]), NN)
            own = own - dot3(split(panel_ref[:, done]), (high_part[done, cols], low_part[done, cols]), NN)
        upper, inverse = factor_block(here[:, :LANES])
        inverse_parts = split(inverse)
        low_ref[part(j), cols] = upper.T
        for i in range(j):
            low_ref[part(i), cols] = zero
        if j + 1 < blocks:
            row = dot3(inverse_parts, split(here[:, LANES:]), NN)
            high_part[part(j), rest], low_part[part(j), rest] = split(row)
            for i in range(j + 1, blocks):
                low_ref[part(i), cols] = row[:, part(i - j - 1)].T
        panel_ref[:, cols] = dot3(split(own), inverse_parts, NT)
    band = rows_ref.shape[0]
    start = pl.multiple_of(place_ref[0] * band, SUBS)
    rows_ref[...] = low_ref[pl.ds(start, band), :]


def factor_whole(place, schur, below, band):
    size = schur.shape[0]
    in_vmem = pl.BlockSpec(memory_space=pltpu.VMEM)
    return pl.pallas_call(
        whole_kernel,
        in_specs=[pl.BlockSpec(memory_space=pltpu.SMEM), in_vmem, in_vmem],
        out_specs=[in_vmem, in_vmem],
        out_shape=[
            jax.ShapeDtypeStruct((band, size), jnp.float32),
            jax.ShapeDtypeStruct(below.shape, jnp.float32),
        ],
        scratch_shapes=[
            pltpu.VMEM((size, size), jnp.float32),
            pltpu.VMEM((size, size), jnp.bfloat16),
            pltpu.VMEM((size, size), jnp.bfloat16),
        ],
        compiler_params=pltpu.CompilerParams(vmem_limit_bytes=40 * 1024 * 1024),
        name="cholesky_whole",
    )(place, schur, below)


def on_any(colloc, block_colloc, factor, block_factor):
    grp_count, grp_index, dev_index = lax.axis_size("grp"), lax.axis_index("grp"), lax.axis_index("dev")
    band = block_colloc.shape[0]
    width = band * lax.axis_size("dev")
    points = jnp.concatenate([block_colloc, colloc], axis=0)
    earlier = jnp.concatenate([block_factor, factor], axis=0)
    dims = (((1,), (1,)), ((), ()))
    gram = lax.dot_general(
        points, lax.all_gather(block_colloc, "dev", axis=0, tiled=True), dims, preferred_element_type=jnp.float32
    )
    update = lax.dot_general(
        earlier,
        lax.all_gather(block_factor, "dev", axis=0, tiled=True),
        dims,
        precision=lax.Precision.HIGHEST,
        preferred_element_type=jnp.float32,
    )
    gram_low = lax.psum_scatter(gram[band:], "grp", scatter_dimension=0, tiled=True)
    update_low = lax.psum_scatter(update[band:], "grp", scatter_dimension=0, tiled=True)
    below = gram_low * gram_low - update_low
    slice_width = width // grp_count
    row = dev_index * band + lax.broadcasted_iota(jnp.int32, (band, slice_width), 0)
    col = grp_index * slice_width + lax.broadcasted_iota(jnp.int32, (band, slice_width), 1)
    gram_slice = lax.psum_scatter(gram[:band], "grp", scatter_dimension=1, tiled=True)
    update_slice = lax.psum_scatter(update[:band], "grp", scatter_dimension=1, tiled=True)
    damping = jnp.where(row == col, jnp.float32(DAMPING), jnp.float32(0.0))
    piece = gram_slice * gram_slice + damping - update_slice
    slab = lax.all_gather(piece, "grp", axis=1, tiled=True)
    schur = lax.all_gather(slab, "dev", axis=0, tiled=True)
    place = jnp.reshape(dev_index, (1,)).astype(jnp.int32)
    factor_rows, panel_rows = factor_whole(place, schur, below, band)
    return factor_rows, panel_rows[None]


def on_device(colloc, block_colloc, factor, block_factor):
    devices, count = lax.axis_size("dev"), lax.axis_size("grp")
    gridded = devices % 4 == 0 and devices >= 8 and block_colloc.shape[0] == LANES and count >= 2 and count & (count - 1) == 0
    form = on_grid if gridded else on_any
    return form(colloc, block_colloc, factor, block_factor)


def solution(mesh):
    placed = (P("dev", "grp"), P("dev", "grp"), P("dev", "grp"), P("dev", "grp"))
    return jax.shard_map(
        on_device,
        mesh=mesh,
        in_specs=placed,
        out_specs=(P("dev", None), P("dev", "grp", None)),
        check_vma=False,
    )
```

```python
import functools
import jax
import jax.numpy as jnp
from jax import lax
from jax.sharding import PartitionSpec as P
from jax.experimental import pallas as pl
from jax.experimental.pallas import tpu as pltpu

DAMPING = 0.0625
SCALE = 896.0
LANES = 128
SUBS = 8
NT = ((1,), (1,))


def split(value):
    high = value.astype(jnp.bfloat16)
    low = (value - high.astype(jnp.float32)).astype(jnp.bfloat16)
    return high, low


def dot3(left, right):
    (left_high, left_low), (right_high, right_low) = left, right
    return lax.dot_general(
        jnp.concatenate([left_high, left_high, left_low], axis=1),
        jnp.concatenate([right_high, right_low, right_high], axis=1),
        (NT, ((), ())),
        preferred_element_type=jnp.float32,
    )


def reciprocal(value):
    return pl.reciprocal(value, approx=True)


def over_lanes(value, column):
    return jnp.broadcast_to(value[:, column : column + 1], (SUBS, LANES))


def over_subs(value, row):
    return jnp.broadcast_to(value[row : row + 1, :], (SUBS, LANES))


def tree_sum(values):
    while len(values) > 1:
        values = [a + b for a, b in zip(values[::2], values[1::2])] + values[len(values) // 2 * 2 :]
    return values[0]


def factor_block(block):
    lane = lax.broadcasted_iota(jnp.int32, (SUBS, LANES), 1)
    sub = lax.broadcasted_iota(jnp.int32, (SUBS, LANES), 0)
    strips = LANES // SUBS
    rows = [block[SUBS * s : SUBS * (s + 1), :] for s in range(strips)]
    upper, inverse = [], []
    for s in range(strips):
        first = SUBS * s
        pivots = (lane >= first) & (lane < first + SUBS)
        own = rows[s]
        unit = jnp.where(lane - first == sub, 1.0, jnp.where(pivots, 0.0, own))
        columns = [over_lanes(own, first + k) for k in range(SUBS)]
        kept_own, kept_unit, diagonal = own, unit, None
        for k in range(0, SUBS, 2):
            one, two = sub == k, sub == k + 1
            both = one | two
            a, b, c = over_subs(columns[k], k), over_subs(columns[k + 1], k), over_subs(columns[k + 1], k + 1)
            det = a * c - b * b
            share = reciprocal(det)
            lead = jnp.where(one, c, jnp.where(two, -b, columns[k + 1] * b - columns[k] * c)) * share
            trail = jnp.where(one, -b, jnp.where(two, a, columns[k] * b - columns[k + 1] * a)) * share

            def swept(value):
                return jnp.where(both, 0.0, value) + (lead * over_subs(value, k) + trail * over_subs(value, k + 1))

            inverse_a = reciprocal(a)
            ratio = b * inverse_a
            second = det * inverse_a
            if k == 0:
                diagonal = jnp.where(two, second, a)
            else:
                diagonal = jnp.where(one, a, jnp.where(two, second, diagonal))
            kept_own = jnp.where(one, own, jnp.where(two, own - ratio * over_subs(own, k), kept_own))
            kept_unit = jnp.where(one, unit, jnp.where(two, unit - ratio * over_subs(unit, k), kept_unit))
            for q in range(k + 2, SUBS):
                columns[q] = swept(columns[q])
            own, unit = swept(own), swept(unit)
        root = lax.rsqrt(diagonal)
        upper.append(jnp.where(lane >= first + sub, kept_own * root, 0.0))
        inverse.append(jnp.where(lane <= first + sub, kept_unit * root, 0.0))
        spread = [over_subs(unit, k) for k in range(SUBS)]
        for i in range(s + 1, strips):
            change = tree_sum([over_lanes(rows[i], first + k) * spread[k] for k in range(SUBS)])
            rows[i] = jnp.where(pivots, 0.0, rows[i]) - change
    return jnp.concatenate(upper, axis=0), jnp.concatenate(inverse, axis=0)


def part(j, n=1):
    return slice(j * LANES, (j + n) * LANES)


def factor_columns(count, total, block_at, low_ref, high_ref, low_part_ref, inverse_refs, rest_ref):
    zero = jnp.zeros((LANES, LANES), jnp.float32)

    def held(rows, first, n):
        return high_ref[rows, part(first, n)], low_part_ref[rows, part(first, n)]

    def column_at(i, n):
        value = jnp.concatenate([block_at(m, i) for m in range(i, total)], axis=0)
        return value - dot3(held(part(i, total - i), 0, n), held(part(i), 0, n)) if n else value

    diagonal = block_at(0, 0)
    for j in range(count):
        below = slice((j + 1) * LANES, total * LANES)
        if j + 1 < total:
            ahead = column_at(j, j)[LANES:]
        if j + 1 < count:
            next_diagonal = block_at(j + 1, j + 1)
            if j:
                next_diagonal = next_diagonal - dot3(held(part(j + 1), 0, j), held(part(j + 1), 0, j))
        elif rest_ref is not None:
            remainder = [column_at(i, j) for i in range(count, total)]
        upper, inverse = factor_block(diagonal)
        inverse_parts = split(inverse)
        for ref, value in zip(inverse_refs, inverse_parts):
            ref[part(j), :] = value
        low_ref[part(j), part(j)] = upper.T
        for i in range(j):
            low_ref[part(i), part(j)] = zero
        if j + 1 < total:
            column = dot3(split(ahead), inverse_parts)
            low_ref[below, part(j)] = column
            column_parts = split(column)
            high_ref[below, part(j)], low_part_ref[below, part(j)] = column_parts
        if j + 1 < count:
            first = tuple(v[:LANES] for v in column_parts)
            diagonal = next_diagonal - dot3(first, first)
    for i in range(count, total):
        value = remainder[i - count] - dot3(held(part(i, total - i), count - 1, 1), held(part(i), count - 1, 1))
        rest_ref[part(i - count, total - i), part(i - count)] = value


def first_kernel(ring, count, place_ref, *refs):
    devices = 2 * ring
    pieces = refs[: 2 * devices]
    rows_ref, high_ref, low_part_ref, inverse_high, inverse_low, rest_ref, schur, low_ref, arrived = refs[2 * devices :]
    dev_index, side = place_ref[0], place_ref[1]
    own_z, own_x = dev_index // 2, lax.rem(dev_index, 2)
    half_rows = LANES // 2
    copies = []
    for r in range(ring):
        for q in range(2):
            who = 2 * lax.rem(own_z - r + ring, ring) + lax.rem(own_x + q, 2)
            for other in range(2):
                at = pl.multiple_of(lax.rem(side + other, 2) * half_rows, half_rows)
                number = 2 * (2 * r + q) + other
                copies.append(
                    pltpu.make_async_copy(
                        pieces[number], schur.at[who, :, pl.ds(at, half_rows), :], arrived.at[number]
                    )
                )
    for copy in copies:
        copy.start()
    for copy in copies:
        copy.wait()
    owners, _ = pair_table(ring)

    def block_at(i, j):
        return tree_sum([schur[who, slot] for who, slot in owners[i, j]])

    factor_columns(count, devices, block_at, low_ref, high_ref, low_part_ref, (inverse_high, inverse_low), rest_ref)
    start = pl.multiple_of(dev_index * LANES, LANES)
    rows_ref[...] = low_ref[pl.ds(start, LANES), :]


def second_kernel(place_ref, start_ref, rows_ref, out_ref, high_ref, low_part_ref, inverse_high, inverse_low, low_ref):
    count = start_ref.shape[0] // LANES
    done = rows_ref.shape[1]

    def block_at(i, j):
        return start_ref[part(i), part(j)]

    factor_columns(count, count, block_at, low_ref, high_ref, low_part_ref, (inverse_high, inverse_low), None)
    out_ref[:, :done] = rows_ref[...]
    row = place_ref[0] * LANES - done
    at = pl.multiple_of(jnp.maximum(row, 0), LANES)
    out_ref[:, done:] = jnp.where(row >= 0, low_ref[pl.ds(at, LANES), :], 0.0)


def solve_kernel(ring, count, groups, place_ref, *refs):
    sums = refs[: count * len(groups)]
    first, second = refs[len(sums) : len(sums) + 4], refs[len(sums) + 4 : len(sums) + 8]
    panel_ref, held = refs[len(sums) + 8 :]
    blocks = 2 * ring
    own_z, own_x = place_ref[0] // 2, lax.rem(place_ref[0], 2)
    for m, places in enumerate(groups):
        group = sums[count * m : count * (m + 1)]
        for n, place in enumerate(places):
            who = 2 * lax.rem(own_z - place // 2 + ring, ring) + lax.rem(own_x + place % 2, 2)
            gram_sum = tree_sum([ref[n] for ref in group])
            held[who] = gram_sum * gram_sum - tree_sum([ref[len(places) + n] for ref in group])
    below = jnp.concatenate([held[i] for i in range(blocks)], axis=1)
    half = first[0].shape[1] // LANES
    for j in range(blocks):
        high, low, inverse_high, inverse_low = first if j < half else second
        n, skip = (j, 0) if j < half else (j - half, half)
        value = dot3(split(below[:, :LANES]), (inverse_high[part(n), :], inverse_low[part(n), :]))
        panel_ref[:, part(j)] = value
        if j + 1 < blocks:
            rest = slice((j + 1 - skip) * LANES, (blocks - skip) * LANES)
            below = below[:, LANES:] - dot3(split(value), (high[rest, part(n)], low[rest, part(n)]))


def head_kernel(ring, place_ref, own, across, own_t, across_t, own_f, across_f, *refs):
    half = ring // 2
    middle, out_ref = refs[:-1], refs[-1]
    own_z, first_x = place_ref[0] // 2, lax.rem(place_ref[0], 2) == 0
    full = 2 * half - 1
    own_parts, across_parts = split(own_f[...]), split(across_f[...])

    def product(left, right):
        return jnp.dot(left[...], right[...], preferred_element_type=jnp.float32)

    out_ref[0] = product(own, own_t)
    out_ref[full] = dot3(own_parts, own_parts)
    for t in range(1, half):
        right_t, right_parts = middle[2 * t - 2], split(middle[2 * t - 1][...])
        values = product(own, right_t), product(across, right_t)
        values += dot3(own_parts, right_parts), dot3(across_parts, right_parts)
        slots = t, half - 1 + t, full + t, full + half - 1 + t
        for slot, value in zip(slots, values):
            out_ref[slot] = jnp.where(own_z >= t, value, value.T)

    @pl.when(first_x)
    def _():
        out_ref[2 * full] = product(own, across_t).T

    @pl.when(jnp.logical_not(first_x))
    def _():
        out_ref[2 * full] = dot3(own_parts, across_parts)


def far_kernel(ring, place_ref, done, own, across, own_f, across_f, far_t, far_f, keep_ref, send_ref, held):
    half = ring // 2
    n = done.shape[0]
    rows = LANES // 2
    own_z, side = place_ref[0] // 2, place_ref[1]

    @pl.when(own_z >= half)
    def _():
        for m, left in enumerate((own, across)):
            held[m] = jnp.dot(left[...], far_t[...], preferred_element_type=jnp.float32)

    @pl.when(own_z < half)
    def _():
        right = split(far_f[...])
        for m, left in enumerate((own_f, across_f)):
            held[m] = dot3(split(left[...]), right).T

    for ref, at in ((keep_ref, side * rows), (send_ref, (1 - side) * rows)):
        here = pl.ds(pl.multiple_of(at, rows), rows)
        ref[:n] = done[:, here, :]
        ref[n:] = held[:, here, :]


def piece_kernel(ring, place_ref, one_ref, two_ref, out_ref):
    half = ring // 2
    full = 2 * half - 1
    dev_index, side = place_ref[0], place_ref[1]
    _, rows, width = out_ref.shape
    row = lax.broadcasted_iota(jnp.int32, (rows, width), 0) + side * rows
    col = lax.broadcasted_iota(jnp.int32, (rows, width), 1)
    for n in range(full):
        gram_sum = one_ref[n] + two_ref[n]
        value = gram_sum * gram_sum - (one_ref[full + n] + two_ref[full + n])
        out_ref[n] = value + jnp.where(row == col, DAMPING, 0.0) if n == 0 else value
    squared = lax.rem(dev_index, 2) == 0, dev_index // 2 >= half, dev_index // 2 >= half
    for n, is_gram in enumerate(squared):
        value = one_ref[2 * full + n] + two_ref[2 * full + n]
        out_ref[full + n] = jnp.where(is_gram, value * value, -value)


def low_kernel(count, place_ref, colloc, factor, *refs):
    blocks = (len(refs) - count - 3) // 2
    held, high, low = refs[-3:]
    outs = refs[2 * blocks : 2 * blocks + count]
    rows = colloc.shape[0] // count
    high[...], low[...] = split(factor[...])
    for n in range(blocks):
        value = jnp.dot(colloc[...], refs[2 * n][...], preferred_element_type=jnp.float32)
        held[n] = value.reshape(count, rows, LANES)
        value = dot3((high[...], low[...]), split(refs[2 * n + 1][...]))
        held[blocks + n] = value.reshape(count, rows, LANES)
    for k, ref in enumerate(outs):
        for n in range(2 * blocks):
            ref[n] = held[n, place_ref[2] ^ k]


IN_VMEM = pl.BlockSpec(memory_space=pltpu.VMEM)
IN_SMEM = pl.BlockSpec(memory_space=pltpu.SMEM)
ANYWHERE = pl.BlockSpec(memory_space=pl.ANY)


def params():
    return pltpu.CompilerParams(vmem_limit_bytes=40 * 1024 * 1024)


def effort(steps):
    return pl.CostEstimate(flops=steps * 40_000_000, bytes_accessed=0, transcendentals=0)


def factor_shapes(count, total):
    part_shape = jax.ShapeDtypeStruct((total * LANES, count * LANES), jnp.bfloat16)
    inverse_shape = jax.ShapeDtypeStruct((count * LANES, LANES), jnp.bfloat16)
    return [part_shape, part_shape, inverse_shape, inverse_shape]


def factor_first(ring, count, place, pieces):
    blocks = 2 * ring
    slots = pieces[0].shape[0]
    left = (blocks - count) * LANES
    return pl.pallas_call(
        functools.partial(first_kernel, ring, count),
        in_specs=[IN_SMEM] + [ANYWHERE] * len(pieces),
        out_specs=[IN_VMEM] * 6,
        out_shape=[jax.ShapeDtypeStruct((LANES, count * LANES), jnp.float32)]
        + factor_shapes(count, blocks)
        + [jax.ShapeDtypeStruct((left, left), jnp.float32)],
        scratch_shapes=[
            pltpu.VMEM((blocks, slots, LANES, LANES), jnp.float32),
            pltpu.VMEM((blocks * LANES, count * LANES), jnp.float32),
            pltpu.SemaphoreType.DMA((len(pieces),)),
        ],
        compiler_params=params(),
        cost_estimate=effort(count * LANES),
        name="cholesky_first",
    )(place, *pieces)


def factor_second(place, start, rows):
    size = start.shape[0]
    count = size // LANES
    return pl.pallas_call(
        second_kernel,
        in_specs=[IN_SMEM, IN_VMEM, IN_VMEM],
        out_specs=[IN_VMEM] * 5,
        out_shape=[jax.ShapeDtypeStruct((LANES, rows.shape[1] + size), jnp.float32)] + factor_shapes(count, count),
        scratch_shapes=[pltpu.VMEM((size, size), jnp.float32)],
        compiler_params=params(),
        cost_estimate=effort(size),
        name="cholesky_second",
    )(place, start, rows)


def solve_panel(ring, place, groups, sums, first, second):
    count, rows, blocks = len(sums[0]), sums[0][0].shape[1], 2 * ring
    flat = [v for group in sums for v in group]
    return pl.pallas_call(
        functools.partial(solve_kernel, ring, count, groups),
        in_specs=[IN_SMEM] + [IN_VMEM] * (len(flat) + 8),
        out_specs=IN_VMEM,
        out_shape=jax.ShapeDtypeStruct((rows, blocks * LANES), jnp.float32),
        scratch_shapes=[pltpu.VMEM((blocks, rows, LANES), jnp.float32)],
        compiler_params=params(),
        cost_estimate=effort(LANES),
        name="panel_solve",
    )(place, *flat, *first, *second)


def head_products(ring, place, *operands):
    return pl.pallas_call(
        functools.partial(head_kernel, ring),
        in_specs=[IN_SMEM] + [IN_VMEM] * len(operands),
        out_specs=IN_VMEM,
        out_shape=jax.ShapeDtypeStruct((4 * (ring // 2) - 1, LANES, LANES), jnp.float32),
        compiler_params=params(),
        cost_estimate=effort(64),
        name="head_products",
    )(place, *operands)


def far_products(ring, place, done, *operands):
    shape = (done.shape[0] + 2, LANES // 2, LANES)
    return pl.pallas_call(
        functools.partial(far_kernel, ring),
        in_specs=[IN_SMEM] + [IN_VMEM] * (1 + len(operands)),
        out_specs=[IN_VMEM] * 2,
        out_shape=[jax.ShapeDtypeStruct(shape, jnp.float32)] * 2,
        scratch_shapes=[pltpu.VMEM((2, LANES, LANES), jnp.float32)],
        compiler_params=params(),
        cost_estimate=effort(32),
        name="far_products",
    )(place, done, *operands)


def schur_piece(ring, place, one, two):
    return pl.pallas_call(
        functools.partial(piece_kernel, ring),
        in_specs=[IN_SMEM] + [IN_VMEM] * 2,
        out_specs=IN_VMEM,
        out_shape=jax.ShapeDtypeStruct((2 * (ring // 2) + 2, *one.shape[1:]), jnp.float32),
        compiler_params=params(),
        cost_estimate=effort(16),
        name="schur_piece",
    )(place, one, two)


def low_products(count, place, colloc, factor, blocks):
    rows = colloc.shape[0] // count
    flat = [v for pair in blocks for v in pair]
    n = len(flat)
    return pl.pallas_call(
        functools.partial(low_kernel, count),
        in_specs=[IN_SMEM] + [IN_VMEM] * (2 + n),
        out_specs=[IN_VMEM] * count,
        out_shape=[jax.ShapeDtypeStruct((n, rows, LANES), jnp.float32)] * count,
        scratch_shapes=[
            pltpu.VMEM((n, count, rows, LANES), jnp.float32),
            pltpu.VMEM(factor.shape, jnp.bfloat16),
            pltpu.VMEM(factor.shape, jnp.bfloat16),
        ],
        compiler_params=params(),
        cost_estimate=effort(24 * n),
        name="low_products",
    )(place, colloc, factor, *flat)


def pair_table(ring):
    half = ring // 2
    owners = {}
    for z in range(ring):
        for x in range(2):
            me, across = 2 * z + x, 2 * z + 1 - x

            def back(t):
                return 2 * ((z - t) % ring) + x

            pairs = [(me, me)] + [(me, back(t)) for t in range(1, half)]
            pairs += [(across, back(t)) for t in range(1, half)]
            pairs += [(me, across), (me, back(half)), (across, back(half))]
            for slot, pair in enumerate(pairs):
                owners.setdefault((max(pair), min(pair)), []).append((me, slot))
    return owners, 2 * half + 2


def pick(value, axis, index):
    return lax.dynamic_index_in_dim(value, index, axis, keepdims=False)


def ring_step(value, ring, chosen=None):
    steps = [(2 * z + x, 2 * ((z + 1) % ring) + x) for z in range(ring) for x in range(2)]
    return lax.ppermute(value, "dev", [s for s in steps if chosen is None or chosen(s[1] // 2)])


def swap(value, axis, bit, chosen=None):
    steps = [(i, i ^ bit) for i in range(lax.axis_size(axis))]
    return lax.ppermute(value, axis, [s for s in steps if chosen is None or chosen(s[1] // 2)])


def after(value, *first):
    return lax.optimization_barrier((value, *first))[0]


def exchanged(parts):
    return [parts[0]] + [swap(v, "grp", k) for k, v in enumerate(parts) if k]


def coded(value):
    value = value * SCALE
    return (value * jnp.abs(value)).astype(jnp.float16)


def widen(value):
    value = value.astype(jnp.float32)
    root = jnp.sqrt(jnp.abs(value)) * jnp.float32(1.0 / SCALE)
    return jnp.where(value < 0.0, -root, root)


def on_grid(colloc, block_colloc, factor, block_factor):
    ring, count = lax.axis_size("dev") // 2, lax.axis_size("grp")
    half = ring // 2
    dev_index, grp_index = lax.axis_index("dev"), lax.axis_index("grp")
    upper_z = dev_index // 2 >= half
    place = jnp.stack([dev_index, lax.rem(grp_index, 2), grp_index]).astype(jnp.int32)

    def is_upper(z):
        return z >= half

    def is_lower(z):
        return z < half

    def step(v):
        return ring_step(v, ring)

    def cross(v):
        return swap(v, "dev", 1)

    colloc_along = [block_colloc.T]
    colloc_across = [cross(colloc_along[0])]
    colloc_along.append(step(colloc_along[0]))
    factor_along = [coded(block_factor)]
    factor_along.append(step(factor_along[0]))
    factor_across = [cross(factor_along[0])]
    for t in range(2, half):
        colloc_along.append(step(colloc_along[-1]))
        factor_along.append(step(factor_along[-1]))
    colloc_first, factor_first_part = (
        ring_step(colloc_along[-1], ring, is_upper),
        ring_step(factor_along[-1], ring, is_lower),
    )

    own_factor, across_factor = widen(factor_along[0]), widen(factor_across[0])
    across_rows = colloc_across[0].T
    middle = [v for t in range(1, half) for v in (colloc_along[t], widen(factor_along[t]))]
    done = head_products(
        ring, place, block_colloc, across_rows, colloc_along[0], colloc_across[0], own_factor, across_factor, *middle
    )
    keep, send = far_products(
        ring,
        place,
        done,
        block_colloc,
        across_rows,
        own_factor,
        across_factor,
        after(colloc_first, done),
        widen(factor_first_part),
    )
    total = keep + swap(send, "grp", 1)
    bit = 2
    while 2 * bit < count:
        total = total + swap(total, "grp", bit)
        bit *= 2
    other = swap(total, "grp", bit)

    for t in range(1, half):
        held = after((colloc_along[t], factor_along[t]), send)
        colloc_across.append(cross(held[0]))
        factor_across.append(cross(held[1]))
    held = after((colloc_along[-1], factor_along[-1]), send)
    colloc_second = ring_step(held[0], ring, is_lower)
    factor_second_part = ring_step(held[1], ring, is_upper)

    piece = schur_piece(ring, place, total, other)
    hops = [piece]
    for r in range(1, ring):
        hops.append(step(hops[-1]))
    pieces = []
    for hop in hops:
        crossed = cross(hop)
        pieces += [hop, swap(hop, "grp", 1), crossed, swap(crossed, "grp", 1)]

    colloc_along.append(jnp.where(upper_z, colloc_first, after(colloc_second, piece)))
    factor_along.append(jnp.where(upper_z, after(factor_second_part, piece), factor_first_part))
    colloc_across.append(cross(colloc_along[half]))
    factor_across.append(cross(factor_along[half]))

    for t in range(half + 1, ring):
        held = after((colloc_along[-1], factor_along[-1]), hops[half])
        colloc_along.append(step(held[0]))
        factor_along.append(step(held[1]))
        colloc_across.append(cross(colloc_along[-1]))
        factor_across.append(cross(factor_along[-1]))

    blocks = []
    for t in range(ring):
        blocks += [(colloc_along[t], factor_along[t]), (colloc_across[t], factor_across[t])]

    def low_parts(chosen, first):
        chosen = after([blocks[i] for i in chosen], first)
        return low_products(count, place, colloc, factor, [(v[0], widen(v[1])) for v in chosen])

    early, late = list(range(2 * half + 1)), list(range(2 * half + 1, 2 * ring))
    parts_early = low_parts(early, hops[1])
    sums_early = exchanged(parts_early)
    pieces[0] = after(pieces[0], parts_early)
    rows, *first, start = factor_first(ring, ring, place, pieces)

    parts_late = low_parts(late, start)
    sums_late = exchanged(parts_late)
    factor_out, *second = factor_second(place, after(start, parts_late), rows)
    sums = after([sums_early, sums_late], factor_out)
    panel = solve_panel(ring, place, [early, late], sums, first, second)
    return factor_out, panel[None]


def whole_kernel(place_ref, schur_ref, below_ref, rows_ref, panel_ref, low_ref, high_part, low_part, inverse_high, inverse_low):
    blocks = schur_ref.shape[0] // LANES

    def block_at(i, j):
        return schur_ref[part(i), part(j)]

    factor_columns(blocks, blocks, block_at, low_ref, high_part, low_part, (inverse_high, inverse_low), None)
    for j in range(blocks):
        own = below_ref[:, part(j)]
        if j:
            done = part(0, j)
            own = own - dot3(split(panel_ref[:, done]), (high_part[part(j), done], low_part[part(j), done]))
        panel_ref[:, part(j)] = dot3(split(own), (inverse_high[part(j), :], inverse_low[part(j), :]))
    band = rows_ref.shape[0]
    start = pl.multiple_of(place_ref[0] * band, SUBS)
    rows_ref[...] = low_ref[pl.ds(start, band), :]


def factor_whole(place, schur, below, band):
    size = schur.shape[0]
    return pl.pallas_call(
        whole_kernel,
        in_specs=[IN_SMEM, IN_VMEM, IN_VMEM],
        out_specs=[IN_VMEM, IN_VMEM],
        out_shape=[
            jax.ShapeDtypeStruct((band, size), jnp.float32),
            jax.ShapeDtypeStruct(below.shape, jnp.float32),
        ],
        scratch_shapes=[
            pltpu.VMEM((size, size), jnp.float32),
            pltpu.VMEM((size, size), jnp.bfloat16),
            pltpu.VMEM((size, size), jnp.bfloat16),
            pltpu.VMEM((size, LANES), jnp.bfloat16),
            pltpu.VMEM((size, LANES), jnp.bfloat16),
        ],
        compiler_params=params(),
        name="cholesky_whole",
    )(place, schur, below)


def on_any(colloc, block_colloc, factor, block_factor):
    grp_count, grp_index, dev_index = lax.axis_size("grp"), lax.axis_index("grp"), lax.axis_index("dev")
    band = block_colloc.shape[0]
    width = band * lax.axis_size("dev")
    points = jnp.concatenate([block_colloc, colloc], axis=0)
    earlier = jnp.concatenate([block_factor, factor], axis=0)
    dims = (((1,), (1,)), ((), ()))
    gram = lax.dot_general(
        points, lax.all_gather(block_colloc, "dev", axis=0, tiled=True), dims, preferred_element_type=jnp.float32
    )
    update = lax.dot_general(
        earlier,
        lax.all_gather(block_factor, "dev", axis=0, tiled=True),
        dims,
        precision=lax.Precision.HIGHEST,
        preferred_element_type=jnp.float32,
    )
    gram_low = lax.psum_scatter(gram[band:], "grp", scatter_dimension=0, tiled=True)
    update_low = lax.psum_scatter(update[band:], "grp", scatter_dimension=0, tiled=True)
    below = gram_low * gram_low - update_low
    slice_width = width // grp_count
    row = dev_index * band + lax.broadcasted_iota(jnp.int32, (band, slice_width), 0)
    col = grp_index * slice_width + lax.broadcasted_iota(jnp.int32, (band, slice_width), 1)
    gram_slice = lax.psum_scatter(gram[:band], "grp", scatter_dimension=1, tiled=True)
    update_slice = lax.psum_scatter(update[:band], "grp", scatter_dimension=1, tiled=True)
    damping = jnp.where(row == col, jnp.float32(DAMPING), jnp.float32(0.0))
    piece = gram_slice * gram_slice + damping - update_slice
    slab = lax.all_gather(piece, "grp", axis=1, tiled=True)
    schur = lax.all_gather(slab, "dev", axis=0, tiled=True)
    place = jnp.reshape(dev_index, (1,)).astype(jnp.int32)
    factor_rows, panel_rows = factor_whole(place, schur, below, band)
    return factor_rows, panel_rows[None]


def on_device(colloc, block_colloc, factor, block_factor):
    devices, count = lax.axis_size("dev"), lax.axis_size("grp")
    gridded = devices % 4 == 0 and devices >= 8 and block_colloc.shape[0] == LANES and count >= 2 and count & (count - 1) == 0
    form = on_grid if gridded else on_any
    return form(colloc, block_colloc, factor, block_factor)


def solution(mesh):
    placed = (P("dev", "grp"), P("dev", "grp"), P("dev", "grp"), P("dev", "grp"))
    return jax.shard_map(
        on_device,
        mesh=mesh,
        in_specs=placed,
        out_specs=(P("dev", None), P("dev", "grp", None)),
        check_vma=False,
    )
```

```python
import functools
import jax
import jax.numpy as jnp
from jax import lax
from jax.sharding import PartitionSpec as P
from jax.experimental import pallas as pl
from jax.experimental.pallas import tpu as pltpu

DAMPING = 0.0625
SCALE = 896.0
LANES = 128
SUBS = 8
NT = ((1,), (1,))


def split(value):
    high = value.astype(jnp.bfloat16)
    low = (value - high.astype(jnp.float32)).astype(jnp.bfloat16)
    return high, low


def dot3(left, right):
    (left_high, left_low), (right_high, right_low) = left, right
    return lax.dot_general(
        jnp.concatenate([left_high, left_high, left_low], axis=1),
        jnp.concatenate([right_high, right_low, right_high], axis=1),
        (NT, ((), ())),
        preferred_element_type=jnp.float32,
    )


def reciprocal(value):
    return pl.reciprocal(value, approx=True)


def over_lanes(value, column):
    return jnp.broadcast_to(value[:, column : column + 1], (SUBS, LANES))


def over_subs(value, row):
    return jnp.broadcast_to(value[row : row + 1, :], (SUBS, LANES))


def tree_sum(values):
    while len(values) > 1:
        values = [a + b for a, b in zip(values[::2], values[1::2])] + values[len(values) // 2 * 2 :]
    return values[0]


def factor_block(block):
    lane = lax.broadcasted_iota(jnp.int32, (SUBS, LANES), 1)
    sub = lax.broadcasted_iota(jnp.int32, (SUBS, LANES), 0)
    strips = LANES // SUBS
    rows = [block[SUBS * s : SUBS * (s + 1), :] for s in range(strips)]
    upper, inverse = [], []
    for s in range(strips):
        first = SUBS * s
        pivots = (lane >= first) & (lane < first + SUBS)
        own = rows[s]
        unit = jnp.where(lane - first == sub, 1.0, jnp.where(pivots, 0.0, own))
        columns = [over_lanes(own, first + k) for k in range(SUBS)]
        kept_own, kept_unit, diagonal = own, unit, None
        for k in range(0, SUBS, 2):
            one, two = sub == k, sub == k + 1
            both = one | two
            a, b, c = over_subs(columns[k], k), over_subs(columns[k + 1], k), over_subs(columns[k + 1], k + 1)
            det = a * c - b * b
            share = reciprocal(det)
            lead = jnp.where(one, c, jnp.where(two, -b, columns[k + 1] * b - columns[k] * c)) * share
            trail = jnp.where(one, -b, jnp.where(two, a, columns[k] * b - columns[k + 1] * a)) * share

            def swept(value):
                return jnp.where(both, 0.0, value) + (lead * over_subs(value, k) + trail * over_subs(value, k + 1))

            inverse_a = reciprocal(a)
            ratio = b * inverse_a
            second = det * inverse_a
            if k == 0:
                diagonal = jnp.where(two, second, a)
            else:
                diagonal = jnp.where(one, a, jnp.where(two, second, diagonal))
            kept_own = jnp.where(one, own, jnp.where(two, own - ratio * over_subs(own, k), kept_own))
            kept_unit = jnp.where(one, unit, jnp.where(two, unit - ratio * over_subs(unit, k), kept_unit))
            for q in range(k + 2, SUBS):
                columns[q] = swept(columns[q])
            own, unit = swept(own), swept(unit)
        root = lax.rsqrt(diagonal)
        upper.append(jnp.where(lane >= first + sub, kept_own * root, 0.0))
        inverse.append(jnp.where(lane <= first + sub, kept_unit * root, 0.0))
        spread = [over_subs(unit, k) for k in range(SUBS)]
        for i in range(s + 1, strips):
            change = tree_sum([over_lanes(rows[i], first + k) * spread[k] for k in range(SUBS)])
            rows[i] = jnp.where(pivots, 0.0, rows[i]) - change
    return jnp.concatenate(upper, axis=0), jnp.concatenate(inverse, axis=0)


def part(j, n=1):
    return slice(j * LANES, (j + n) * LANES)


def factor_columns(count, total, block_at, low_ref, high_ref, low_part_ref, inverse_refs, rest_ref):
    zero = jnp.zeros((LANES, LANES), jnp.float32)

    def held(rows, first, n):
        return high_ref[rows, part(first, n)], low_part_ref[rows, part(first, n)]

    def column_at(i, n):
        value = jnp.concatenate([block_at(m, i) for m in range(i, total)], axis=0)
        return value - dot3(held(part(i, total - i), 0, n), held(part(i), 0, n)) if n else value

    diagonal = block_at(0, 0)
    for j in range(count):
        below = slice((j + 1) * LANES, total * LANES)
        if j + 1 < total:
            ahead = column_at(j, j)[LANES:]
        if j + 1 < count:
            next_diagonal = block_at(j + 1, j + 1)
            if j:
                next_diagonal = next_diagonal - dot3(held(part(j + 1), 0, j), held(part(j + 1), 0, j))
        elif rest_ref is not None:
            remainder = [column_at(i, j) for i in range(count, total)]
        upper, inverse = factor_block(diagonal)
        inverse_parts = split(inverse)
        for ref, value in zip(inverse_refs, inverse_parts):
            ref[part(j), :] = value
        low_ref[part(j), part(j)] = upper.T
        for i in range(j):
            low_ref[part(i), part(j)] = zero
        if j + 1 < total:
            column = dot3(split(ahead), inverse_parts)
            low_ref[below, part(j)] = column
            column_parts = split(column)
            high_ref[below, part(j)], low_part_ref[below, part(j)] = column_parts
        if j + 1 < count:
            first = tuple(v[:LANES] for v in column_parts)
            diagonal = next_diagonal - dot3(first, first)
    for i in range(count, total):
        value = remainder[i - count] - dot3(held(part(i, total - i), count - 1, 1), held(part(i), count - 1, 1))
        rest_ref[part(i - count, total - i), part(i - count)] = value


def first_kernel(ring, count, place_ref, *refs):
    devices = 2 * ring
    pieces = refs[: 2 * devices]
    rows_ref, high_ref, low_part_ref, inverse_high, inverse_low, rest_ref, schur, low_ref, arrived = refs[2 * devices :]
    dev_index, side = place_ref[0], place_ref[1]
    own_z, own_x = dev_index // 2, lax.rem(dev_index, 2)
    half_rows = LANES // 2
    copies = []
    for r in range(ring):
        for q in range(2):
            who = 2 * lax.rem(own_z - r + ring, ring) + lax.rem(own_x + q, 2)
            for other in range(2):
                at = pl.multiple_of(lax.rem(side + other, 2) * half_rows, half_rows)
                number = 2 * (2 * r + q) + other
                copies.append(
                    pltpu.make_async_copy(
                        pieces[number], schur.at[who, :, pl.ds(at, half_rows), :], arrived.at[number]
                    )
                )
    for copy in copies:
        copy.start()
    for copy in copies:
        copy.wait()
    owners, _ = pair_table(ring)

    def block_at(i, j):
        return tree_sum([schur[who, slot] for who, slot in owners[i, j]])

    factor_columns(count, devices, block_at, low_ref, high_ref, low_part_ref, (inverse_high, inverse_low), rest_ref)
    start = pl.multiple_of(dev_index * LANES, LANES)
    rows_ref[...] = low_ref[pl.ds(start, LANES), :]


def second_kernel(place_ref, start_ref, rows_ref, out_ref, high_ref, low_part_ref, inverse_high, inverse_low, low_ref):
    count = start_ref.shape[0] // LANES
    done = rows_ref.shape[1]

    def block_at(i, j):
        return start_ref[part(i), part(j)]

    factor_columns(count, count, block_at, low_ref, high_ref, low_part_ref, (inverse_high, inverse_low), None)
    out_ref[:, :done] = rows_ref[...]
    row = place_ref[0] * LANES - done
    at = pl.multiple_of(jnp.maximum(row, 0), LANES)
    out_ref[:, done:] = jnp.where(row >= 0, low_ref[pl.ds(at, LANES), :], 0.0)


def solve_kernel(ring, groups, place_ref, *refs):
    sums = refs[: sum(summands for _, summands in groups)]
    first, second, (panel_ref, held) = refs[len(sums) :][:4], refs[len(sums) :][4:8], refs[len(sums) :][8:]
    blocks = 2 * ring
    own_z, own_x = place_ref[0] // 2, lax.rem(place_ref[0], 2)
    for places, summands in groups:
        group, sums = sums[:summands], sums[summands:]
        for n, place in enumerate(places):
            who = 2 * lax.rem(own_z - place // 2 + ring, ring) + lax.rem(own_x + place % 2, 2)
            gram_sum = tree_sum([ref[n] for ref in group])
            held[who] = gram_sum * gram_sum - tree_sum([ref[len(places) + n] for ref in group])
    below = jnp.concatenate([held[i] for i in range(blocks)], axis=1)
    half = first[0].shape[1] // LANES
    for j in range(blocks):
        high, low, inverse_high, inverse_low = first if j < half else second
        n, skip = (j, 0) if j < half else (j - half, half)
        value = dot3(split(below[:, :LANES]), (inverse_high[part(n), :], inverse_low[part(n), :]))
        panel_ref[:, part(j)] = value
        if j + 1 < blocks:
            rest = slice((j + 1 - skip) * LANES, (blocks - skip) * LANES)
            below = below[:, LANES:] - dot3(split(value), (high[rest, part(n)], low[rest, part(n)]))


def head_kernel(ring, place_ref, own, across, own_t, across_t, own_f, across_f, *refs):
    half = ring // 2
    middle, out_ref = refs[:-1], refs[-1]
    own_z, first_x = place_ref[0] // 2, lax.rem(place_ref[0], 2) == 0
    full = 2 * half - 1
    own_parts, across_parts = split(own_f[...]), split(across_f[...])

    def product(left, right):
        return jnp.dot(left[...], right[...], preferred_element_type=jnp.float32)

    out_ref[0] = product(own, own_t)
    out_ref[full] = dot3(own_parts, own_parts)
    for t in range(1, half):
        right_t, right_parts = middle[2 * t - 2], split(middle[2 * t - 1][...])
        values = product(own, right_t), product(across, right_t)
        values += dot3(own_parts, right_parts), dot3(across_parts, right_parts)
        slots = t, half - 1 + t, full + t, full + half - 1 + t
        for slot, value in zip(slots, values):
            out_ref[slot] = jnp.where(own_z >= t, value, value.T)

    @pl.when(first_x)
    def _():
        out_ref[2 * full] = product(own, across_t).T

    @pl.when(jnp.logical_not(first_x))
    def _():
        out_ref[2 * full] = dot3(own_parts, across_parts)


def far_kernel(ring, place_ref, done, own, across, own_f, across_f, far_t, far_f, keep_ref, send_ref, held):
    half = ring // 2
    n = done.shape[0]
    rows = LANES // 2
    own_z, side = place_ref[0] // 2, place_ref[1]

    @pl.when(own_z >= half)
    def _():
        for m, left in enumerate((own, across)):
            held[m] = jnp.dot(left[...], far_t[...], preferred_element_type=jnp.float32)

    @pl.when(own_z < half)
    def _():
        right = split(far_f[...])
        for m, left in enumerate((own_f, across_f)):
            held[m] = dot3(split(left[...]), right).T

    for ref, at in ((keep_ref, side * rows), (send_ref, (1 - side) * rows)):
        here = pl.ds(pl.multiple_of(at, rows), rows)
        ref[:n] = done[:, here, :]
        ref[n:] = held[:, here, :]


def piece_kernel(ring, place_ref, one_ref, two_ref, out_ref):
    half = ring // 2
    full = 2 * half - 1
    dev_index, side = place_ref[0], place_ref[1]
    _, rows, width = out_ref.shape
    row = lax.broadcasted_iota(jnp.int32, (rows, width), 0) + side * rows
    col = lax.broadcasted_iota(jnp.int32, (rows, width), 1)
    for n in range(full):
        gram_sum = one_ref[n] + two_ref[n]
        value = gram_sum * gram_sum - (one_ref[full + n] + two_ref[full + n])
        out_ref[n] = value + jnp.where(row == col, DAMPING, 0.0) if n == 0 else value
    squared = lax.rem(dev_index, 2) == 0, dev_index // 2 >= half, dev_index // 2 >= half
    for n, is_gram in enumerate(squared):
        value = one_ref[2 * full + n] + two_ref[2 * full + n]
        out_ref[full + n] = jnp.where(is_gram, value * value, -value)


def low_kernel(count, before, place_ref, colloc, factor, *refs):
    blocks = (len(refs) - count - 3 - (count if before else 0)) // 2
    high, low, held = refs[-3:]
    outs = refs[-3 - count : -3]
    earlier = refs[2 * blocks : 2 * blocks + count] if before else ()
    rows = colloc.shape[0] // count
    high[...], low[...] = split(factor[...])
    right = jnp.concatenate([refs[2 * n][...] for n in range(blocks)], axis=1)
    value = jnp.dot(colloc[...], right, preferred_element_type=jnp.float32)
    for n in range(blocks):
        held[n] = value[:, part(n)].reshape(count, rows, LANES)
    right = jnp.concatenate([refs[2 * n + 1][...] for n in range(blocks)], axis=0)
    value = dot3((high[...], low[...]), split(right))
    for n in range(blocks):
        held[blocks + n] = value[:, part(n)].reshape(count, rows, LANES)
    for k, ref in enumerate(outs):
        for n in range(before):
            ref[n] = earlier[k][n]
            ref[before + blocks + n] = earlier[k][before + n]
        for n in range(blocks):
            ref[before + n] = held[n, place_ref[2] ^ k]
            ref[2 * before + blocks + n] = held[blocks + n, place_ref[2] ^ k]


IN_VMEM = pl.BlockSpec(memory_space=pltpu.VMEM)
IN_SMEM = pl.BlockSpec(memory_space=pltpu.SMEM)
ANYWHERE = pl.BlockSpec(memory_space=pl.ANY)


def params():
    return pltpu.CompilerParams(vmem_limit_bytes=40 * 1024 * 1024)


def effort(steps):
    return pl.CostEstimate(flops=steps * 40_000_000, bytes_accessed=0, transcendentals=0)


def factor_shapes(count, total):
    part_shape = jax.ShapeDtypeStruct((total * LANES, count * LANES), jnp.bfloat16)
    inverse_shape = jax.ShapeDtypeStruct((count * LANES, LANES), jnp.bfloat16)
    return [part_shape, part_shape, inverse_shape, inverse_shape]


def factor_first(ring, count, place, pieces):
    blocks = 2 * ring
    slots = pieces[0].shape[0]
    left = (blocks - count) * LANES
    return pl.pallas_call(
        functools.partial(first_kernel, ring, count),
        in_specs=[IN_SMEM] + [ANYWHERE] * len(pieces),
        out_specs=[IN_VMEM] * 6,
        out_shape=[jax.ShapeDtypeStruct((LANES, count * LANES), jnp.float32)]
        + factor_shapes(count, blocks)
        + [jax.ShapeDtypeStruct((left, left), jnp.float32)],
        scratch_shapes=[
            pltpu.VMEM((blocks, slots, LANES, LANES), jnp.float32),
            pltpu.VMEM((blocks * LANES, count * LANES), jnp.float32),
            pltpu.SemaphoreType.DMA((len(pieces),)),
        ],
        compiler_params=params(),
        cost_estimate=effort(count * LANES),
        name="cholesky_first",
    )(place, *pieces)


def factor_second(place, start, rows):
    size = start.shape[0]
    count = size // LANES
    return pl.pallas_call(
        second_kernel,
        in_specs=[IN_SMEM, IN_VMEM, IN_VMEM],
        out_specs=[IN_VMEM] * 5,
        out_shape=[jax.ShapeDtypeStruct((LANES, rows.shape[1] + size), jnp.float32)] + factor_shapes(count, count),
        scratch_shapes=[pltpu.VMEM((size, size), jnp.float32)],
        compiler_params=params(),
        cost_estimate=effort(size),
        name="cholesky_second",
    )(place, start, rows)


def solve_panel(ring, place, groups, sums, first, second):
    rows, blocks = sums[0][0].shape[1], 2 * ring
    flat = [v for group in sums for v in group]
    groups = [(places, len(group)) for places, group in zip(groups, sums)]
    return pl.pallas_call(
        functools.partial(solve_kernel, ring, groups),
        in_specs=[IN_SMEM] + [IN_VMEM] * (len(flat) + 8),
        out_specs=IN_VMEM,
        out_shape=jax.ShapeDtypeStruct((rows, blocks * LANES), jnp.float32),
        scratch_shapes=[pltpu.VMEM((blocks, rows, LANES), jnp.float32)],
        compiler_params=params(),
        cost_estimate=effort(LANES),
        name="panel_solve",
    )(place, *flat, *first, *second)


def head_products(ring, place, *operands):
    return pl.pallas_call(
        functools.partial(head_kernel, ring),
        in_specs=[IN_SMEM] + [IN_VMEM] * len(operands),
        out_specs=IN_VMEM,
        out_shape=jax.ShapeDtypeStruct((4 * (ring // 2) - 1, LANES, LANES), jnp.float32),
        compiler_params=params(),
        cost_estimate=effort(64),
        name="head_products",
    )(place, *operands)


def far_products(ring, place, done, *operands):
    shape = (done.shape[0] + 2, LANES // 2, LANES)
    return pl.pallas_call(
        functools.partial(far_kernel, ring),
        in_specs=[IN_SMEM] + [IN_VMEM] * (1 + len(operands)),
        out_specs=[IN_VMEM] * 2,
        out_shape=[jax.ShapeDtypeStruct(shape, jnp.float32)] * 2,
        scratch_shapes=[pltpu.VMEM((2, LANES, LANES), jnp.float32)],
        compiler_params=params(),
        cost_estimate=effort(32),
        name="far_products",
    )(place, done, *operands)


def schur_piece(ring, place, one, two):
    return pl.pallas_call(
        functools.partial(piece_kernel, ring),
        in_specs=[IN_SMEM] + [IN_VMEM] * 2,
        out_specs=IN_VMEM,
        out_shape=jax.ShapeDtypeStruct((2 * (ring // 2) + 2, *one.shape[1:]), jnp.float32),
        compiler_params=params(),
        cost_estimate=effort(16),
        name="schur_piece",
    )(place, one, two)


def low_products(count, place, colloc, factor, blocks, earlier=()):
    rows = colloc.shape[0] // count
    before = earlier[0].shape[0] // 2 if earlier else 0
    flat = [v for pair in blocks for v in pair] + list(earlier)
    n = 2 * len(blocks)
    return pl.pallas_call(
        functools.partial(low_kernel, count, before),
        in_specs=[IN_SMEM] + [IN_VMEM] * (2 + len(flat)),
        out_specs=[IN_VMEM] * count,
        out_shape=[jax.ShapeDtypeStruct((2 * before + n, rows, LANES), jnp.float32)] * count,
        scratch_shapes=[
            pltpu.VMEM(factor.shape, jnp.bfloat16),
            pltpu.VMEM(factor.shape, jnp.bfloat16),
            pltpu.VMEM((n, count, rows, LANES), jnp.float32),
        ],
        compiler_params=params(),
        cost_estimate=effort(24 * n),
        name="low_products",
    )(place, colloc, factor, *flat)


def pair_table(ring):
    half = ring // 2
    owners = {}
    for z in range(ring):
        for x in range(2):
            me, across = 2 * z + x, 2 * z + 1 - x

            def back(t):
                return 2 * ((z - t) % ring) + x

            pairs = [(me, me)] + [(me, back(t)) for t in range(1, half)]
            pairs += [(across, back(t)) for t in range(1, half)]
            pairs += [(me, across), (me, back(half)), (across, back(half))]
            for slot, pair in enumerate(pairs):
                owners.setdefault((max(pair), min(pair)), []).append((me, slot))
    return owners, 2 * half + 2


def pick(value, axis, index):
    return lax.dynamic_index_in_dim(value, index, axis, keepdims=False)


def ring_step(value, ring, chosen=None):
    steps = [(2 * z + x, 2 * ((z + 1) % ring) + x) for z in range(ring) for x in range(2)]
    return lax.ppermute(value, "dev", [s for s in steps if chosen is None or chosen(s[1] // 2)])


def swap(value, axis, bit, chosen=None):
    steps = [(i, i ^ bit) for i in range(lax.axis_size(axis))]
    return lax.ppermute(value, axis, [s for s in steps if chosen is None or chosen(s[1] // 2)])


def after(value, *first):
    return lax.optimization_barrier((value, *first))[0]


def exchanged(parts):
    return [parts[0]] + [swap(v, "grp", k) for k, v in enumerate(parts) if k]


def halved(parts):
    own, bit = [parts[0]], 1
    while len(parts) > 1:
        received = [swap(v, "grp", bit) for v in parts[1::2]]
        own.append(received[0])
        parts = [parts[0]] + [v + w for v, w in zip(parts[2::2], received[1:])]
        bit *= 2
    return own


def coded(value):
    value = value * SCALE
    return (value * jnp.abs(value)).astype(jnp.float16)


def widen(value):
    value = value.astype(jnp.float32)
    root = jnp.sqrt(jnp.abs(value)) * jnp.float32(1.0 / SCALE)
    return jnp.where(value < 0.0, -root, root)


def on_grid(colloc, block_colloc, factor, block_factor):
    ring, count = lax.axis_size("dev") // 2, lax.axis_size("grp")
    half = ring // 2
    dev_index, grp_index = lax.axis_index("dev"), lax.axis_index("grp")
    upper_z = dev_index // 2 >= half
    place = jnp.stack([dev_index, lax.rem(grp_index, 2), grp_index]).astype(jnp.int32)

    def is_upper(z):
        return z >= half

    def is_lower(z):
        return z < half

    def step(v):
        return ring_step(v, ring)

    def cross(v):
        return swap(v, "dev", 1)

    colloc_along = [block_colloc.T]
    colloc_across = [cross(colloc_along[0])]
    colloc_along.append(step(colloc_along[0]))
    factor_along = [coded(block_factor)]
    factor_along.append(step(factor_along[0]))
    factor_across = [cross(factor_along[0])]
    for t in range(2, half):
        colloc_along.append(step(colloc_along[-1]))
        factor_along.append(step(factor_along[-1]))
    colloc_first, factor_first_part = (
        ring_step(colloc_along[-1], ring, is_upper),
        ring_step(factor_along[-1], ring, is_lower),
    )

    own_factor, across_factor = widen(factor_along[0]), widen(factor_across[0])
    across_rows = colloc_across[0].T
    middle = [v for t in range(1, half) for v in (colloc_along[t], widen(factor_along[t]))]
    done = head_products(
        ring, place, block_colloc, across_rows, colloc_along[0], colloc_across[0], own_factor, across_factor, *middle
    )
    keep, send = far_products(
        ring,
        place,
        done,
        block_colloc,
        across_rows,
        own_factor,
        across_factor,
        after(colloc_first, done),
        widen(factor_first_part),
    )
    total = keep + swap(send, "grp", 1)
    bit = 2
    while 2 * bit < count:
        total = total + swap(total, "grp", bit)
        bit *= 2
    other = swap(total, "grp", bit)

    def low_parts(chosen, first, earlier=()):
        chosen = after(chosen, first)
        return low_products(count, place, colloc, factor, [(v[0], widen(v[1])) for v in chosen], earlier)

    for t in range(1, half):
        colloc_across.append(cross(colloc_along[t]))
        factor_across.append(cross(factor_along[t]))
    held = after((colloc_along[-1], factor_along[-1]), send)
    colloc_second = ring_step(held[0], ring, is_lower)
    factor_second_part = ring_step(held[1], ring, is_upper)
    held = after((colloc_first, factor_first_part), total)
    colloc_across_first = swap(held[0], "dev", 1, is_upper)
    factor_across_first = swap(held[1], "dev", 1, is_lower)

    def blocks_at(t):
        return [(colloc_along[t], factor_along[t]), (colloc_across[t], factor_across[t])]

    soon = [v for t in range(half) for v in blocks_at(t)][: 2 * half - 1]
    parts_soon = low_parts(soon, total)

    piece = schur_piece(ring, place, total, other)
    hops = [piece]
    for r in range(1, ring):
        hops.append(step(hops[-1]))
    crossed = [cross(hop) for hop in hops]
    pieces = []
    for hop, over in zip(hops, crossed):
        pieces += [hop, swap(hop, "grp", 1), over, swap(over, "grp", 1)]

    held = after((colloc_second, factor_second_part), hops[1])
    colloc_across_second = swap(held[0], "dev", 1, is_lower)
    factor_across_second = swap(held[1], "dev", 1, is_upper)
    factor_along.append(jnp.where(upper_z, held[1], factor_first_part))
    colloc_along.append(jnp.where(upper_z, colloc_first, held[0]))

    held = after((colloc_across_second, factor_across_second), hops[half])
    colloc_across.append(jnp.where(upper_z, colloc_across_first, held[0]))
    factor_across.append(jnp.where(upper_z, held[1], factor_across_first))
    for t in range(half + 1, ring):
        factor_along.append(step(factor_along[-1]))
        colloc_along.append(step(after(colloc_along[-1], hops[half])))
        factor_across.append(cross(after(factor_along[-1], hops[-1])))
        colloc_across.append(step(after(colloc_across[-1], hops[-1])))

    parts_early = low_parts([blocks_at(half - 1)[1], blocks_at(half)[0]], hops[half], parts_soon)
    sums_early = halved(parts_early)
    pieces[0] = after(pieces[0], parts_early)
    rows, *first, start = factor_first(ring, ring, place, pieces)

    late = [blocks_at(half)[1]] + [v for t in range(half + 1, ring) for v in blocks_at(t)]
    parts_late = low_parts(late, start)
    sums_late = exchanged(parts_late)
    factor_out, *second = factor_second(place, after(start, parts_late), rows)
    sums = after([sums_early, sums_late], factor_out)
    groups = [list(range(2 * half + 1)), list(range(2 * half + 1, 2 * ring))]
    panel = solve_panel(ring, place, groups, sums, first, second)
    return factor_out, panel[None]


def whole_kernel(place_ref, schur_ref, below_ref, rows_ref, panel_ref, low_ref, high_part, low_part, inverse_high, inverse_low):
    blocks = schur_ref.shape[0] // LANES

    def block_at(i, j):
        return schur_ref[part(i), part(j)]

    factor_columns(blocks, blocks, block_at, low_ref, high_part, low_part, (inverse_high, inverse_low), None)
    for j in range(blocks):
        own = below_ref[:, part(j)]
        if j:
            done = part(0, j)
            own = own - dot3(split(panel_ref[:, done]), (high_part[part(j), done], low_part[part(j), done]))
        panel_ref[:, part(j)] = dot3(split(own), (inverse_high[part(j), :], inverse_low[part(j), :]))
    band = rows_ref.shape[0]
    start = pl.multiple_of(place_ref[0] * band, SUBS)
    rows_ref[...] = low_ref[pl.ds(start, band), :]


def factor_whole(place, schur, below, band):
    size = schur.shape[0]
    return pl.pallas_call(
        whole_kernel,
        in_specs=[IN_SMEM, IN_VMEM, IN_VMEM],
        out_specs=[IN_VMEM, IN_VMEM],
        out_shape=[
            jax.ShapeDtypeStruct((band, size), jnp.float32),
            jax.ShapeDtypeStruct(below.shape, jnp.float32),
        ],
        scratch_shapes=[
            pltpu.VMEM((size, size), jnp.float32),
            pltpu.VMEM((size, size), jnp.bfloat16),
            pltpu.VMEM((size, size), jnp.bfloat16),
            pltpu.VMEM((size, LANES), jnp.bfloat16),
            pltpu.VMEM((size, LANES), jnp.bfloat16),
        ],
        compiler_params=params(),
        name="cholesky_whole",
    )(place, schur, below)


def on_any(colloc, block_colloc, factor, block_factor):
    grp_count, grp_index, dev_index = lax.axis_size("grp"), lax.axis_index("grp"), lax.axis_index("dev")
    band = block_colloc.shape[0]
    width = band * lax.axis_size("dev")
    points = jnp.concatenate([block_colloc, colloc], axis=0)
    earlier = jnp.concatenate([block_factor, factor], axis=0)
    dims = (((1,), (1,)), ((), ()))
    gram = lax.dot_general(
        points, lax.all_gather(block_colloc, "dev", axis=0, tiled=True), dims, preferred_element_type=jnp.float32
    )
    update = lax.dot_general(
        earlier,
        lax.all_gather(block_factor, "dev", axis=0, tiled=True),
        dims,
        precision=lax.Precision.HIGHEST,
        preferred_element_type=jnp.float32,
    )
    gram_low = lax.psum_scatter(gram[band:], "grp", scatter_dimension=0, tiled=True)
    update_low = lax.psum_scatter(update[band:], "grp", scatter_dimension=0, tiled=True)
    below = gram_low * gram_low - update_low
    slice_width = width // grp_count
    row = dev_index * band + lax.broadcasted_iota(jnp.int32, (band, slice_width), 0)
    col = grp_index * slice_width + lax.broadcasted_iota(jnp.int32, (band, slice_width), 1)
    gram_slice = lax.psum_scatter(gram[:band], "grp", scatter_dimension=1, tiled=True)
    update_slice = lax.psum_scatter(update[:band], "grp", scatter_dimension=1, tiled=True)
    damping = jnp.where(row == col, jnp.float32(DAMPING), jnp.float32(0.0))
    piece = gram_slice * gram_slice + damping - update_slice
    slab = lax.all_gather(piece, "grp", axis=1, tiled=True)
    schur = lax.all_gather(slab, "dev", axis=0, tiled=True)
    place = jnp.reshape(dev_index, (1,)).astype(jnp.int32)
    factor_rows, panel_rows = factor_whole(place, schur, below, band)
    return factor_rows, panel_rows[None]


def on_device(colloc, block_colloc, factor, block_factor):
    devices, count = lax.axis_size("dev"), lax.axis_size("grp")
    gridded = devices % 4 == 0 and devices >= 8 and block_colloc.shape[0] == LANES and count >= 2 and count & (count - 1) == 0
    form = on_grid if gridded else on_any
    return form(colloc, block_colloc, factor, block_factor)


def solution(mesh):
    placed = (P("dev", "grp"), P("dev", "grp"), P("dev", "grp"), P("dev", "grp"))
    return jax.shard_map(
        on_device,
        mesh=mesh,
        in_specs=placed,
        out_specs=(P("dev", None), P("dev", "grp", None)),
        check_vma=False,
    )
```

```python
import functools
import jax
import jax.numpy as jnp
from jax import lax
from jax.sharding import PartitionSpec as P
from jax.experimental import pallas as pl
from jax.experimental.pallas import tpu as pltpu

DAMPING = 0.0625
SCALE = 896.0
VALUE_SCALE = 16384.0
LANES = 128
SUBS = 8
NT = ((1,), (1,))


def split(value):
    high = value.astype(jnp.bfloat16)
    low = (value - high.astype(jnp.float32)).astype(jnp.bfloat16)
    return high, low


def dot3(left, right):
    (left_high, left_low), (right_high, right_low) = left, right
    return lax.dot_general(
        jnp.concatenate([left_high, left_high, left_low], axis=1),
        jnp.concatenate([right_high, right_low, right_high], axis=1),
        (NT, ((), ())),
        preferred_element_type=jnp.float32,
    )


def reciprocal(value):
    return pl.reciprocal(value, approx=True)


def over_lanes(value, column):
    return jnp.broadcast_to(value[:, column : column + 1], (SUBS, LANES))


def over_subs(value, row):
    return jnp.broadcast_to(value[row : row + 1, :], (SUBS, LANES))


def tree_sum(values):
    while len(values) > 1:
        values = [a + b for a, b in zip(values[::2], values[1::2])] + values[len(values) // 2 * 2 :]
    return values[0]


def factor_block(block):
    lane = lax.broadcasted_iota(jnp.int32, (SUBS, LANES), 1)
    sub = lax.broadcasted_iota(jnp.int32, (SUBS, LANES), 0)
    strips = LANES // SUBS
    rows = [block[SUBS * s : SUBS * (s + 1), :] for s in range(strips)]
    upper, inverse = [], []
    for s in range(strips):
        first = SUBS * s
        pivots = (lane >= first) & (lane < first + SUBS)
        own = rows[s]
        unit = jnp.where(lane - first == sub, 1.0, jnp.where(pivots, 0.0, own))
        columns = [over_lanes(own, first + k) for k in range(SUBS)]
        kept_own, kept_unit, diagonal = own, unit, None
        for k in range(0, SUBS, 2):
            one, two = sub == k, sub == k + 1
            both = one | two
            a, b, c = over_subs(columns[k], k), over_subs(columns[k + 1], k), over_subs(columns[k + 1], k + 1)
            det = a * c - b * b
            share = reciprocal(det)
            lead = jnp.where(one, c, jnp.where(two, -b, columns[k + 1] * b - columns[k] * c)) * share
            trail = jnp.where(one, -b, jnp.where(two, a, columns[k] * b - columns[k + 1] * a)) * share

            def swept(value):
                return jnp.where(both, 0.0, value) + (lead * over_subs(value, k) + trail * over_subs(value, k + 1))

            inverse_a = reciprocal(a)
            ratio = b * inverse_a
            second = det * inverse_a
            if k == 0:
                diagonal = jnp.where(two, second, a)
            else:
                diagonal = jnp.where(one, a, jnp.where(two, second, diagonal))
            kept_own = jnp.where(one, own, jnp.where(two, own - ratio * over_subs(own, k), kept_own))
            kept_unit = jnp.where(one, unit, jnp.where(two, unit - ratio * over_subs(unit, k), kept_unit))
            for q in range(k + 2, SUBS):
                columns[q] = swept(columns[q])
            own, unit = swept(own), swept(unit)
        root = lax.rsqrt(diagonal)
        upper.append(jnp.where(lane >= first + sub, kept_own * root, 0.0))
        inverse.append(jnp.where(lane <= first + sub, kept_unit * root, 0.0))
        spread = [over_subs(unit, k) for k in range(SUBS)]
        for i in range(s + 1, strips):
            change = tree_sum([over_lanes(rows[i], first + k) * spread[k] for k in range(SUBS)])
            rows[i] = jnp.where(pivots, 0.0, rows[i]) - change
    return jnp.concatenate(upper, axis=0), jnp.concatenate(inverse, axis=0)


def part(j, n=1):
    return slice(j * LANES, (j + n) * LANES)


def factor_columns(count, total, block_at, low_ref, high_ref, low_part_ref, inverse_refs, rest_ref):
    zero = jnp.zeros((LANES, LANES), jnp.float32)

    def held(rows, first, n):
        return high_ref[rows, part(first, n)], low_part_ref[rows, part(first, n)]

    def column_at(i, n):
        value = jnp.concatenate([block_at(m, i) for m in range(i, total)], axis=0)
        return value - dot3(held(part(i, total - i), 0, n), held(part(i), 0, n)) if n else value

    diagonal = block_at(0, 0)
    for j in range(count):
        below = slice((j + 1) * LANES, total * LANES)
        if j + 1 < total:
            ahead = column_at(j, j)[LANES:]
        if j + 1 < count:
            next_diagonal = block_at(j + 1, j + 1)
            if j:
                next_diagonal = next_diagonal - dot3(held(part(j + 1), 0, j), held(part(j + 1), 0, j))
        elif rest_ref is not None:
            remainder = [column_at(i, j) for i in range(count, total)]
        upper, inverse = factor_block(diagonal)
        inverse_parts = split(inverse)
        for ref, value in zip(inverse_refs, inverse_parts):
            ref[part(j), :] = value
        low_ref[part(j), part(j)] = upper.T
        for i in range(j):
            low_ref[part(i), part(j)] = zero
        if j + 1 < total:
            column = dot3(split(ahead), inverse_parts)
            low_ref[below, part(j)] = column
            column_parts = split(column)
            high_ref[below, part(j)], low_part_ref[below, part(j)] = column_parts
        if j + 1 < count:
            first = tuple(v[:LANES] for v in column_parts)
            diagonal = next_diagonal - dot3(first, first)
    for i in range(count, total):
        value = remainder[i - count] - dot3(held(part(i, total - i), count - 1, 1), held(part(i), count - 1, 1))
        rest_ref[part(i - count, total - i), part(i - count)] = value


def first_kernel(ring, count, place_ref, *refs):
    devices = 2 * ring
    pieces = refs[: 2 * devices]
    rows_ref, high_ref, low_part_ref, inverse_high, inverse_low, rest_ref, schur, low_ref, arrived = refs[2 * devices :]
    dev_index, side = place_ref[0], place_ref[1]
    own_z, own_x = dev_index // 2, lax.rem(dev_index, 2)
    half_rows = LANES // 2
    copies = []
    for r in range(ring):
        for q in range(2):
            who = 2 * lax.rem(own_z - r + ring, ring) + lax.rem(own_x + q, 2)
            for other in range(2):
                at = pl.multiple_of(lax.rem(side + other, 2) * half_rows, half_rows)
                number = 2 * (2 * r + q) + other
                copies.append(
                    pltpu.make_async_copy(
                        pieces[number], schur.at[who, :, pl.ds(at, half_rows), :], arrived.at[number]
                    )
                )
    for copy in copies:
        copy.start()
    for copy in copies:
        copy.wait()
    owners, _ = pair_table(ring)

    def block_at(i, j):
        return tree_sum([schur[who, slot] for who, slot in owners[i, j]])

    factor_columns(count, devices, block_at, low_ref, high_ref, low_part_ref, (inverse_high, inverse_low), rest_ref)
    start = pl.multiple_of(dev_index * LANES, LANES)
    rows_ref[...] = low_ref[pl.ds(start, LANES), :]


def second_kernel(place_ref, start_ref, rows_ref, out_ref, high_ref, low_part_ref, inverse_high, inverse_low, low_ref):
    count = start_ref.shape[0] // LANES
    done = rows_ref.shape[1]

    def block_at(i, j):
        return start_ref[part(i), part(j)]

    factor_columns(count, count, block_at, low_ref, high_ref, low_part_ref, (inverse_high, inverse_low), None)
    out_ref[:, :done] = rows_ref[...]
    row = place_ref[0] * LANES - done
    at = pl.multiple_of(jnp.maximum(row, 0), LANES)
    out_ref[:, done:] = jnp.where(row >= 0, low_ref[pl.ds(at, LANES), :], 0.0)


def solve_kernel(ring, groups, place_ref, *refs):
    sums = refs[: sum(summands for _, summands in groups)]
    first, second, (panel_ref, held) = refs[len(sums) :][:4], refs[len(sums) :][4:8], refs[len(sums) :][8:]
    blocks = 2 * ring
    own_z, own_x = place_ref[0] // 2, lax.rem(place_ref[0], 2)
    for places, summands in groups:
        group, sums = sums[:summands], sums[summands:]
        for n, place in enumerate(places):
            who = 2 * lax.rem(own_z - place // 2 + ring, ring) + lax.rem(own_x + place % 2, 2)
            gram_sum = tree_sum([ref[n] for ref in group])
            held[who] = gram_sum * gram_sum - tree_sum([ref[len(places) + n] for ref in group])
    below = jnp.concatenate([held[i] for i in range(blocks)], axis=1)
    half = first[0].shape[1] // LANES
    for j in range(blocks):
        high, low, inverse_high, inverse_low = first if j < half else second
        n, skip = (j, 0) if j < half else (j - half, half)
        value = dot3(split(below[:, :LANES]), (inverse_high[part(n), :], inverse_low[part(n), :]))
        panel_ref[:, part(j)] = value
        if j + 1 < blocks:
            rest = slice((j + 1 - skip) * LANES, (blocks - skip) * LANES)
            below = below[:, LANES:] - dot3(split(value), (high[rest, part(n)], low[rest, part(n)]))


def gram_of(left, right):
    return lax.dot_general(left, right, (NT, ((), ())), preferred_element_type=jnp.float32)


def head_kernel(ring, place_ref, own, across, own_f, across_f, *refs):
    half = ring // 2
    middle, out_ref = refs[:-1], refs[-1]
    own_z, first_x = place_ref[0] // 2, lax.rem(place_ref[0], 2) == 0
    full = 2 * half - 1
    own_parts, across_parts = split(own_f[...]), split(across_f[...])
    out_ref[0] = gram_of(own[...], own[...])
    out_ref[full] = dot3(own_parts, own_parts)
    for t in range(1, half):
        right, right_parts = middle[2 * t - 2][...], split(middle[2 * t - 1][...])
        values = gram_of(own[...], right), gram_of(across[...], right)
        values += dot3(own_parts, right_parts), dot3(across_parts, right_parts)
        slots = t, half - 1 + t, full + t, full + half - 1 + t
        for slot, value in zip(slots, values):
            out_ref[slot] = jnp.where(own_z >= t, value, value.T)

    @pl.when(first_x)
    def _():
        out_ref[2 * full] = gram_of(across[...], own[...])

    @pl.when(jnp.logical_not(first_x))
    def _():
        out_ref[2 * full] = dot3(own_parts, across_parts)


def far_kernel(ring, place_ref, done, own, across, own_f, across_f, far, far_f, keep_ref, send_ref, held):
    half = ring // 2
    n = done.shape[0]
    rows = LANES // 2
    own_z, side = place_ref[0] // 2, place_ref[1]

    @pl.when(own_z >= half)
    def _():
        for m, left in enumerate((own, across)):
            held[m] = gram_of(left[...], far[...])

    @pl.when(own_z < half)
    def _():
        right = split(far_f[...])
        for m, left in enumerate((own_f, across_f)):
            held[m] = dot3(split(left[...]), right).T

    for ref, at in ((keep_ref, side * rows), (send_ref, (1 - side) * rows)):
        here = pl.ds(pl.multiple_of(at, rows), rows)
        ref[:n] = done[:, here, :]
        ref[n:] = held[:, here, :]


def piece_kernel(ring, place_ref, one_ref, two_ref, out_ref):
    half = ring // 2
    full = 2 * half - 1
    dev_index, side = place_ref[0], place_ref[1]
    _, rows, width = out_ref.shape
    row = lax.broadcasted_iota(jnp.int32, (rows, width), 0) + side * rows
    col = lax.broadcasted_iota(jnp.int32, (rows, width), 1)
    for n in range(full):
        gram_sum = one_ref[n] + two_ref[n]
        value = gram_sum * gram_sum - (one_ref[full + n] + two_ref[full + n])
        out_ref[n] = value + jnp.where(row == col, DAMPING, 0.0) if n == 0 else value
    squared = lax.rem(dev_index, 2) == 0, dev_index // 2 >= half, dev_index // 2 >= half
    for n, is_gram in enumerate(squared):
        value = one_ref[2 * full + n] + two_ref[2 * full + n]
        out_ref[full + n] = jnp.where(is_gram, value * value, -value)


def low_kernel(count, before, place_ref, colloc, factor, *refs):
    blocks = (len(refs) - count - 3 - (count if before else 0)) // 2
    high, low, held = refs[-3:]
    outs = refs[-3 - count : -3]
    earlier = refs[2 * blocks : 2 * blocks + count] if before else ()
    rows = colloc.shape[0] // count
    high[...], low[...] = split(factor[...])
    right = jnp.concatenate([refs[2 * n][...] for n in range(blocks)], axis=0)
    value = gram_of(colloc[...], right)
    for n in range(blocks):
        held[n] = value[:, part(n)].reshape(count, rows, LANES)
    right = jnp.concatenate([refs[2 * n + 1][...] for n in range(blocks)], axis=0)
    value = dot3((high[...], low[...]), split(right))
    for n in range(blocks):
        held[blocks + n] = value[:, part(n)].reshape(count, rows, LANES)
    for k, ref in enumerate(outs):
        for n in range(before):
            ref[n] = earlier[k][n]
            ref[before + blocks + n] = earlier[k][before + n]
        for n in range(blocks):
            ref[before + n] = held[n, place_ref[2] ^ k]
            ref[2 * before + blocks + n] = held[blocks + n, place_ref[2] ^ k]


IN_VMEM = pl.BlockSpec(memory_space=pltpu.VMEM)
IN_SMEM = pl.BlockSpec(memory_space=pltpu.SMEM)
ANYWHERE = pl.BlockSpec(memory_space=pl.ANY)


def params():
    return pltpu.CompilerParams(vmem_limit_bytes=40 * 1024 * 1024)


def effort(steps):
    return pl.CostEstimate(flops=steps * 40_000_000, bytes_accessed=0, transcendentals=0)


def factor_shapes(count, total):
    part_shape = jax.ShapeDtypeStruct((total * LANES, count * LANES), jnp.bfloat16)
    inverse_shape = jax.ShapeDtypeStruct((count * LANES, LANES), jnp.bfloat16)
    return [part_shape, part_shape, inverse_shape, inverse_shape]


def factor_first(ring, count, place, pieces):
    blocks = 2 * ring
    slots = pieces[0].shape[0]
    left = (blocks - count) * LANES
    return pl.pallas_call(
        functools.partial(first_kernel, ring, count),
        in_specs=[IN_SMEM] + [ANYWHERE] * len(pieces),
        out_specs=[IN_VMEM] * 6,
        out_shape=[jax.ShapeDtypeStruct((LANES, count * LANES), jnp.float32)]
        + factor_shapes(count, blocks)
        + [jax.ShapeDtypeStruct((left, left), jnp.float32)],
        scratch_shapes=[
            pltpu.VMEM((blocks, slots, LANES, LANES), jnp.float32),
            pltpu.VMEM((blocks * LANES, count * LANES), jnp.float32),
            pltpu.SemaphoreType.DMA((len(pieces),)),
        ],
        compiler_params=params(),
        cost_estimate=effort(count * LANES),
        name="cholesky_first",
    )(place, *pieces)


def factor_second(place, start, rows):
    size = start.shape[0]
    count = size // LANES
    return pl.pallas_call(
        second_kernel,
        in_specs=[IN_SMEM, IN_VMEM, IN_VMEM],
        out_specs=[IN_VMEM] * 5,
        out_shape=[jax.ShapeDtypeStruct((LANES, rows.shape[1] + size), jnp.float32)] + factor_shapes(count, count),
        scratch_shapes=[pltpu.VMEM((size, size), jnp.float32)],
        compiler_params=params(),
        cost_estimate=effort(size),
        name="cholesky_second",
    )(place, start, rows)


def solve_panel(ring, place, groups, sums, first, second):
    rows, blocks = sums[0][0].shape[1], 2 * ring
    flat = [v for group in sums for v in group]
    groups = [(places, len(group)) for places, group in zip(groups, sums)]
    return pl.pallas_call(
        functools.partial(solve_kernel, ring, groups),
        in_specs=[IN_SMEM] + [IN_VMEM] * (len(flat) + 8),
        out_specs=IN_VMEM,
        out_shape=jax.ShapeDtypeStruct((rows, blocks * LANES), jnp.float32),
        scratch_shapes=[pltpu.VMEM((blocks, rows, LANES), jnp.float32)],
        compiler_params=params(),
        cost_estimate=effort(LANES),
        name="panel_solve",
    )(place, *flat, *first, *second)


def head_products(ring, place, *operands):
    return pl.pallas_call(
        functools.partial(head_kernel, ring),
        in_specs=[IN_SMEM] + [IN_VMEM] * len(operands),
        out_specs=IN_VMEM,
        out_shape=jax.ShapeDtypeStruct((4 * (ring // 2) - 1, LANES, LANES), jnp.float32),
        compiler_params=params(),
        cost_estimate=effort(64),
        name="head_products",
    )(place, *operands)


def far_products(ring, place, done, *operands):
    shape = (done.shape[0] + 2, LANES // 2, LANES)
    return pl.pallas_call(
        functools.partial(far_kernel, ring),
        in_specs=[IN_SMEM] + [IN_VMEM] * (1 + len(operands)),
        out_specs=[IN_VMEM] * 2,
        out_shape=[jax.ShapeDtypeStruct(shape, jnp.float32)] * 2,
        scratch_shapes=[pltpu.VMEM((2, LANES, LANES), jnp.float32)],
        compiler_params=params(),
        cost_estimate=effort(32),
        name="far_products",
    )(place, done, *operands)


def schur_piece(ring, place, one, two):
    return pl.pallas_call(
        functools.partial(piece_kernel, ring),
        in_specs=[IN_SMEM] + [IN_VMEM] * 2,
        out_specs=IN_VMEM,
        out_shape=jax.ShapeDtypeStruct((2 * (ring // 2) + 2, *one.shape[1:]), jnp.float32),
        compiler_params=params(),
        cost_estimate=effort(16),
        name="schur_piece",
    )(place, one, two)


def low_products(count, place, colloc, factor, blocks, earlier=()):
    rows = colloc.shape[0] // count
    before = earlier[0].shape[0] // 2 if earlier else 0
    flat = [v for pair in blocks for v in pair] + list(earlier)
    n = 2 * len(blocks)
    return pl.pallas_call(
        functools.partial(low_kernel, count, before),
        in_specs=[IN_SMEM] + [IN_VMEM] * (2 + len(flat)),
        out_specs=[IN_VMEM] * count,
        out_shape=[jax.ShapeDtypeStruct((2 * before + n, rows, LANES), jnp.float32)] * count,
        scratch_shapes=[
            pltpu.VMEM(factor.shape, jnp.bfloat16),
            pltpu.VMEM(factor.shape, jnp.bfloat16),
            pltpu.VMEM((n, count, rows, LANES), jnp.float32),
        ],
        compiler_params=params(),
        cost_estimate=effort(24 * n),
        name="low_products",
    )(place, colloc, factor, *flat)


def pair_table(ring):
    half = ring // 2
    owners = {}
    for z in range(ring):
        for x in range(2):
            me, across = 2 * z + x, 2 * z + 1 - x

            def back(t):
                return 2 * ((z - t) % ring) + x

            pairs = [(me, me)] + [(me, back(t)) for t in range(1, half)]
            pairs += [(across, back(t)) for t in range(1, half)]
            pairs += [(me, across), (me, back(half)), (across, back(half))]
            for slot, pair in enumerate(pairs):
                owners.setdefault((max(pair), min(pair)), []).append((me, slot))
    return owners, 2 * half + 2


def pick(value, axis, index):
    return lax.dynamic_index_in_dim(value, index, axis, keepdims=False)


def ring_step(value, ring, chosen=None):
    steps = [(2 * z + x, 2 * ((z + 1) % ring) + x) for z in range(ring) for x in range(2)]
    return lax.ppermute(value, "dev", [s for s in steps if chosen is None or chosen(s[1] // 2)])


def swap(value, axis, bit, chosen=None):
    steps = [(i, i ^ bit) for i in range(lax.axis_size(axis))]
    return lax.ppermute(value, axis, [s for s in steps if chosen is None or chosen(s[1] // 2)])


def after(value, *first):
    return lax.optimization_barrier((value, *first))[0]


def exchanged(parts):
    return [parts[0]] + [swap(v, "grp", k) for k, v in enumerate(parts) if k]


def halved(parts):
    own, bit = [parts[0]], 1
    while len(parts) > 1:
        received = [swap(v, "grp", bit) for v in parts[1::2]]
        own.append(received[0])
        parts = [parts[0]] + [v + w for v, w in zip(parts[2::2], received[1:])]
        bit *= 2
    return own


def coded(colloc_rows, factor_rows):
    width = max(colloc_rows.shape[1], factor_rows.shape[1])
    width += -width % LANES
    factor_rows = factor_rows * SCALE
    parts = (colloc_rows.astype(jnp.float32) * VALUE_SCALE, factor_rows * jnp.abs(factor_rows))
    return jnp.stack([padded(v.astype(jnp.float16), width) for v in parts])


def padded(value, width):
    return jnp.pad(value, ((0, 0), (0, width - value.shape[1])))


def narrow(value):
    return (value.astype(jnp.float32) * jnp.float32(1.0 / VALUE_SCALE)).astype(jnp.bfloat16)


def widen(value):
    value = value.astype(jnp.float32)
    root = jnp.sqrt(jnp.abs(value)) * jnp.float32(1.0 / SCALE)
    return jnp.where(value < 0.0, -root, root)


def on_grid(colloc, block_colloc, factor, block_factor):
    ring, count = lax.axis_size("dev") // 2, lax.axis_size("grp")
    half = ring // 2
    dev_index, grp_index = lax.axis_index("dev"), lax.axis_index("grp")
    own_z = dev_index // 2
    place = jnp.stack([dev_index, lax.rem(grp_index, 2), grp_index]).astype(jnp.int32)

    def is_upper(t):
        return lax.rem(own_z - t + ring, ring) >= half

    def step(v):
        return ring_step(v, ring)

    def cross(v):
        return swap(v, "dev", 1)

    own = coded(block_colloc, block_factor)
    width = own.shape[2]
    wide_colloc, wide_factor = padded(colloc, width), padded(factor, width)

    def opened(v):
        return narrow(v[0]), widen(v[1])

    along, across = [own], [cross(own)]
    for t in range(1, half):
        along.append(step(along[-1]))
        across.append(cross(along[-1]))
    next_upper = is_upper(-1)
    first = step(pick(along[-1], 0, jnp.where(next_upper, 0, 1)))

    open_along = [opened(v) for v in along]
    open_across = [opened(across[0])]
    middle = [v for pair in open_along[1:] for v in pair]
    done = head_products(
        ring, place, open_along[0][0], open_across[0][0], open_along[0][1], open_across[0][1], *middle
    )
    last = after(first, done)
    keep, send = far_products(
        ring,
        place,
        done,
        open_along[0][0],
        open_across[0][0],
        open_along[0][1],
        open_across[0][1],
        narrow(last),
        widen(last),
    )
    total = keep + swap(send, "grp", 1)
    bit = 2
    while 2 * bit < count:
        total = total + swap(total, "grp", bit)
        bit *= 2
    other = swap(total, "grp", bit)

    second = step(pick(after(along[-1], send), 0, jnp.where(next_upper, 1, 0)))
    across_first = cross(after(first, send))

    def low_parts(chosen, earlier=()):
        return low_products(count, place, wide_colloc, wide_factor, chosen, earlier)

    soon = [open_along[0], open_across[0], *open_along[1:]]
    parts_soon = low_parts(after(soon, total))

    piece = schur_piece(ring, place, total, after(other, across[1:]))
    hops = [piece, after(step(piece), first, across_first, second)]
    hops.append(step(hops[-1]))
    across_second = cross(after(second, hops[1]))
    far_along = [(step(after(first, hops[0])), None)]
    for r in range(3, ring):
        hops.append(after(step(hops[-1]), across_second, far_along[0][0]))
    crossed = [cross(hop) for hop in hops]
    pieces = []
    for hop, over in zip(hops, crossed):
        pieces += [hop, swap(hop, "grp", 1), over, swap(over, "grp", 1)]

    def joined(t, one, two):
        upper = is_upper(t - half)
        return narrow(jnp.where(upper, one, two)), widen(jnp.where(upper, two, one))

    far_along[0] = (far_along[0][0], step(after(second, hops[half])))
    far_across = [(across_first, across_second)]
    for t in range(half + 1, ring):
        if t > half + 1:
            far_along.append(tuple(step(v) for v in far_along[-1]))
        one = cross(after(far_along[-1][0], hops[-1]))
        far_across.append((one, step(after(far_across[-1][1], hops[-1]))))

    held = after([v for t in range(1, half) for v in (across[t],)] + [first, second], hops[-1])
    early = [opened(v) for v in held[:-2]] + [joined(half, *held[-2:])]
    parts_early = low_parts(early, parts_soon)
    sums_early = halved(parts_early)
    pieces[0] = after(pieces[0], parts_early)
    rows, *first_factor, start = factor_first(ring, ring, place, pieces)

    far_along, far_across = after((far_along, far_across), start)
    late = [joined(half + t, *v) for t, v in enumerate(far_across)]
    late += [joined(half + 1 + t, *v) for t, v in enumerate(far_along)]
    parts_late = low_parts(late)
    sums_late = exchanged(parts_late)
    factor_out, *second_factor = factor_second(place, after(start, parts_late), rows)
    sums = after([sums_early, sums_late], factor_out)
    places_early = [0, 1] + [2 * t for t in range(1, half)] + [2 * t + 1 for t in range(1, half)] + [2 * half]
    places_late = [2 * t + 1 for t in range(half, ring)] + [2 * t for t in range(half + 1, ring)]
    panel = solve_panel(ring, place, [places_early, places_late], sums, first_factor, second_factor)
    return factor_out, panel[None]


def whole_kernel(place_ref, schur_ref, below_ref, rows_ref, panel_ref, low_ref, high_part, low_part, inverse_high, inverse_low):
    blocks = schur_ref.shape[0] // LANES

    def block_at(i, j):
        return schur_ref[part(i), part(j)]

    factor_columns(blocks, blocks, block_at, low_ref, high_part, low_part, (inverse_high, inverse_low), None)
    for j in range(blocks):
        own = below_ref[:, part(j)]
        if j:
            done = part(0, j)
            own = own - dot3(split(panel_ref[:, done]), (high_part[part(j), done], low_part[part(j), done]))
        panel_ref[:, part(j)] = dot3(split(own), (inverse_high[part(j), :], inverse_low[part(j), :]))
    band = rows_ref.shape[0]
    start = pl.multiple_of(place_ref[0] * band, SUBS)
    rows_ref[...] = low_ref[pl.ds(start, band), :]


def factor_whole(place, schur, below, band):
    size = schur.shape[0]
    return pl.pallas_call(
        whole_kernel,
        in_specs=[IN_SMEM, IN_VMEM, IN_VMEM],
        out_specs=[IN_VMEM, IN_VMEM],
        out_shape=[
            jax.ShapeDtypeStruct((band, size), jnp.float32),
            jax.ShapeDtypeStruct(below.shape, jnp.float32),
        ],
        scratch_shapes=[
            pltpu.VMEM((size, size), jnp.float32),
            pltpu.VMEM((size, size), jnp.bfloat16),
            pltpu.VMEM((size, size), jnp.bfloat16),
            pltpu.VMEM((size, LANES), jnp.bfloat16),
            pltpu.VMEM((size, LANES), jnp.bfloat16),
        ],
        compiler_params=params(),
        name="cholesky_whole",
    )(place, schur, below)


def on_any(colloc, block_colloc, factor, block_factor):
    grp_count, grp_index, dev_index = lax.axis_size("grp"), lax.axis_index("grp"), lax.axis_index("dev")
    band = block_colloc.shape[0]
    width = band * lax.axis_size("dev")
    points = jnp.concatenate([block_colloc, colloc], axis=0)
    earlier = jnp.concatenate([block_factor, factor], axis=0)
    dims = (((1,), (1,)), ((), ()))
    gram = lax.dot_general(
        points, lax.all_gather(block_colloc, "dev", axis=0, tiled=True), dims, preferred_element_type=jnp.float32
    )
    update = lax.dot_general(
        earlier,
        lax.all_gather(block_factor, "dev", axis=0, tiled=True),
        dims,
        precision=lax.Precision.HIGHEST,
        preferred_element_type=jnp.float32,
    )
    gram_low = lax.psum_scatter(gram[band:], "grp", scatter_dimension=0, tiled=True)
    update_low = lax.psum_scatter(update[band:], "grp", scatter_dimension=0, tiled=True)
    below = gram_low * gram_low - update_low
    slice_width = width // grp_count
    row = dev_index * band + lax.broadcasted_iota(jnp.int32, (band, slice_width), 0)
    col = grp_index * slice_width + lax.broadcasted_iota(jnp.int32, (band, slice_width), 1)
    gram_slice = lax.psum_scatter(gram[:band], "grp", scatter_dimension=1, tiled=True)
    update_slice = lax.psum_scatter(update[:band], "grp", scatter_dimension=1, tiled=True)
    damping = jnp.where(row == col, jnp.float32(DAMPING), jnp.float32(0.0))
    piece = gram_slice * gram_slice + damping - update_slice
    slab = lax.all_gather(piece, "grp", axis=1, tiled=True)
    schur = lax.all_gather(slab, "dev", axis=0, tiled=True)
    place = jnp.reshape(dev_index, (1,)).astype(jnp.int32)
    factor_rows, panel_rows = factor_whole(place, schur, below, band)
    return factor_rows, panel_rows[None]


def on_device(colloc, block_colloc, factor, block_factor):
    devices, count = lax.axis_size("dev"), lax.axis_size("grp")
    gridded = devices % 4 == 0 and devices >= 8 and block_colloc.shape[0] == LANES and count >= 2 and count & (count - 1) == 0
    form = on_grid if gridded else on_any
    return form(colloc, block_colloc, factor, block_factor)


def solution(mesh):
    placed = (P("dev", "grp"), P("dev", "grp"), P("dev", "grp"), P("dev", "grp"))
    return jax.shard_map(
        on_device,
        mesh=mesh,
        in_specs=placed,
        out_specs=(P("dev", None), P("dev", "grp", None)),
        check_vma=False,
    )
```

```python
import functools
import jax
import jax.numpy as jnp
from jax import lax
from jax.sharding import PartitionSpec as P
from jax.experimental import pallas as pl
from jax.experimental.pallas import tpu as pltpu

DAMPING = 0.0625
SCALE = 896.0
VALUE_SCALE = 16384.0
LANES = 128
SUBS = 8
NT = ((1,), (1,))


def split(value):
    high = value.astype(jnp.bfloat16)
    low = (value - high.astype(jnp.float32)).astype(jnp.bfloat16)
    return high, low


def dot3(left, right):
    (left_high, left_low), (right_high, right_low) = left, right
    return lax.dot_general(
        jnp.concatenate([left_high, left_high, left_low], axis=1),
        jnp.concatenate([right_high, right_low, right_high], axis=1),
        (NT, ((), ())),
        preferred_element_type=jnp.float32,
    )


def reciprocal(value):
    return pl.reciprocal(value, approx=True)


def over_lanes(value, column):
    return jnp.broadcast_to(value[:, column : column + 1], (SUBS, LANES))


def over_subs(value, row):
    return jnp.broadcast_to(value[row : row + 1, :], (SUBS, LANES))


def tree_sum(values):
    while len(values) > 1:
        values = [a + b for a, b in zip(values[::2], values[1::2])] + values[len(values) // 2 * 2 :]
    return values[0]


def factor_block(block):
    lane = lax.broadcasted_iota(jnp.int32, (SUBS, LANES), 1)
    sub = lax.broadcasted_iota(jnp.int32, (SUBS, LANES), 0)
    strips = LANES // SUBS
    rows = [block[SUBS * s : SUBS * (s + 1), :] for s in range(strips)]
    upper, inverse = [], []
    for s in range(strips):
        first = SUBS * s
        pivots = (lane >= first) & (lane < first + SUBS)
        own = rows[s]
        unit = jnp.where(lane - first == sub, 1.0, jnp.where(pivots, 0.0, own))
        columns = [over_lanes(own, first + k) for k in range(SUBS)]
        kept_own, kept_unit, diagonal = own, unit, None
        for k in range(0, SUBS, 2):
            one, two = sub == k, sub == k + 1
            both = one | two
            a, b, c = over_subs(columns[k], k), over_subs(columns[k + 1], k), over_subs(columns[k + 1], k + 1)
            det = a * c - b * b
            share = reciprocal(det)
            lead = jnp.where(one, c, jnp.where(two, -b, columns[k + 1] * b - columns[k] * c)) * share
            trail = jnp.where(one, -b, jnp.where(two, a, columns[k] * b - columns[k + 1] * a)) * share

            def swept(value):
                return jnp.where(both, 0.0, value) + (lead * over_subs(value, k) + trail * over_subs(value, k + 1))

            inverse_a = reciprocal(a)
            ratio = b * inverse_a
            second = det * inverse_a
            if k == 0:
                diagonal = jnp.where(two, second, a)
            else:
                diagonal = jnp.where(one, a, jnp.where(two, second, diagonal))
            kept_own = jnp.where(one, own, jnp.where(two, own - ratio * over_subs(own, k), kept_own))
            kept_unit = jnp.where(one, unit, jnp.where(two, unit - ratio * over_subs(unit, k), kept_unit))
            for q in range(k + 2, SUBS):
                columns[q] = swept(columns[q])
            own, unit = swept(own), swept(unit)
        root = lax.rsqrt(diagonal)
        upper.append(jnp.where(lane >= first + sub, kept_own * root, 0.0))
        inverse.append(jnp.where(lane <= first + sub, kept_unit * root, 0.0))
        spread = [over_subs(unit, k) for k in range(SUBS)]
        for i in range(s + 1, strips):
            change = tree_sum([over_lanes(rows[i], first + k) * spread[k] for k in range(SUBS)])
            rows[i] = jnp.where(pivots, 0.0, rows[i]) - change
    return jnp.concatenate(upper, axis=0), jnp.concatenate(inverse, axis=0)


def part(j, n=1):
    return slice(j * LANES, (j + n) * LANES)


def factor_columns(count, total, block_at, low_ref, high_ref, low_part_ref, inverse_refs, rest_ref):
    zero = jnp.zeros((LANES, LANES), jnp.float32)

    def held(rows, first, n):
        return high_ref[rows, part(first, n)], low_part_ref[rows, part(first, n)]

    def column_at(i, n):
        value = jnp.concatenate([block_at(m, i) for m in range(i, total)], axis=0)
        return value - dot3(held(part(i, total - i), 0, n), held(part(i), 0, n)) if n else value

    diagonal = block_at(0, 0)
    for j in range(count):
        below = slice((j + 1) * LANES, total * LANES)
        if j + 1 < total:
            ahead = column_at(j, j)[LANES:]
        if j + 1 < count:
            next_diagonal = block_at(j + 1, j + 1)
            if j:
                next_diagonal = next_diagonal - dot3(held(part(j + 1), 0, j), held(part(j + 1), 0, j))
        elif rest_ref is not None:
            remainder = [column_at(i, j) for i in range(count, total)]
        upper, inverse = factor_block(diagonal)
        inverse_parts = split(inverse)
        for ref, value in zip(inverse_refs, inverse_parts):
            ref[part(j), :] = value
        low_ref[part(j), part(j)] = upper.T
        for i in range(j):
            low_ref[part(i), part(j)] = zero
        if j + 1 < total:
            column = dot3(split(ahead), inverse_parts)
            low_ref[below, part(j)] = column
            column_parts = split(column)
            high_ref[below, part(j)], low_part_ref[below, part(j)] = column_parts
        if j + 1 < count:
            first = tuple(v[:LANES] for v in column_parts)
            diagonal = next_diagonal - dot3(first, first)
    for i in range(count, total):
        value = remainder[i - count] - dot3(held(part(i, total - i), count - 1, 1), held(part(i), count - 1, 1))
        rest_ref[part(i - count, total - i), part(i - count)] = value


def first_kernel(ring, count, place_ref, *refs):
    devices = 2 * ring
    pieces = refs[: 2 * devices]
    rows_ref, high_ref, low_part_ref, inverse_high, inverse_low, rest_ref, schur, low_ref, arrived = refs[2 * devices :]
    dev_index, side = place_ref[0], place_ref[1]
    own_z, own_x = dev_index // 2, lax.rem(dev_index, 2)
    half_rows = LANES // 2
    copies = []
    for r in range(ring):
        for q in range(2):
            who = 2 * lax.rem(own_z - r + ring, ring) + lax.rem(own_x + q, 2)
            for other in range(2):
                at = pl.multiple_of(lax.rem(side + other, 2) * half_rows, half_rows)
                number = 2 * (2 * r + q) + other
                copies.append(
                    pltpu.make_async_copy(
                        pieces[number], schur.at[who, :, pl.ds(at, half_rows), :], arrived.at[number]
                    )
                )
    for copy in copies:
        copy.start()
    for copy in copies:
        copy.wait()
    owners, _ = pair_table(ring)

    def block_at(i, j):
        return tree_sum([schur[who, slot] for who, slot in owners[i, j]])

    factor_columns(count, devices, block_at, low_ref, high_ref, low_part_ref, (inverse_high, inverse_low), rest_ref)
    start = pl.multiple_of(dev_index * LANES, LANES)
    rows_ref[...] = low_ref[pl.ds(start, LANES), :]


def more_kernel(count, place_ref, start_ref, rows_ref, out_ref, high_ref, low_part_ref, inverse_high, inverse_low, *refs):
    rest_ref, low_ref = refs if len(refs) == 2 else (None, *refs)
    total = start_ref.shape[0] // LANES
    done = rows_ref.shape[1]
    skipped = place_ref[3] - total

    def block_at(i, j):
        return start_ref[part(i), part(j)]

    factor_columns(count, total, block_at, low_ref, high_ref, low_part_ref, (inverse_high, inverse_low), rest_ref)
    out_ref[:, :done] = rows_ref[...]
    row = (place_ref[0] - skipped) * LANES
    at = pl.multiple_of(jnp.maximum(row, 0), LANES)
    out_ref[:, done:] = jnp.where(row >= 0, low_ref[pl.ds(at, LANES), :], 0.0)


def solve_kernel(ring, groups, place_ref, *refs):
    sums = refs[: sum(summands for _, summands in groups)]
    *parts, panel_ref, held = refs[len(sums) :]
    blocks = 2 * ring
    own_z, own_x = place_ref[0] // 2, lax.rem(place_ref[0], 2)
    for places, summands in groups:
        group, sums = sums[:summands], sums[summands:]
        for n, place in enumerate(places):
            who = 2 * lax.rem(own_z - place // 2 + ring, ring) + lax.rem(own_x + place % 2, 2)
            gram_sum = tree_sum([ref[n] for ref in group])
            held[who] = gram_sum * gram_sum - tree_sum([ref[len(places) + n] for ref in group])
    below = jnp.concatenate([held[i] for i in range(blocks)], axis=1)
    columns = []
    while parts:
        group, parts = parts[:4], parts[4:]
        columns += [(group, n, len(columns)) for n in range(group[0].shape[1] // LANES)]
    for j in range(blocks):
        (high, low, inverse_high, inverse_low), n, skip = columns[j]
        value = dot3(split(below[:, :LANES]), (inverse_high[part(n), :], inverse_low[part(n), :]))
        panel_ref[:, part(j)] = value
        if j + 1 < blocks:
            rest = slice((j + 1 - skip) * LANES, (blocks - skip) * LANES)
            below = below[:, LANES:] - dot3(split(value), (high[rest, part(n)], low[rest, part(n)]))


def gram_of(left, right):
    return lax.dot_general(left, right, (NT, ((), ())), preferred_element_type=jnp.float32)


def head_kernel(ring, place_ref, own, across, own_f, across_f, *refs):
    half = ring // 2
    middle, out_ref = refs[:-1], refs[-1]
    own_z, first_x = place_ref[0] // 2, lax.rem(place_ref[0], 2) == 0
    full = 2 * half - 1
    own_parts, across_parts = split(own_f[...]), split(across_f[...])
    out_ref[0] = gram_of(own[...], own[...])
    out_ref[full] = dot3(own_parts, own_parts)
    for t in range(1, half):
        right, right_parts = middle[2 * t - 2][...], split(middle[2 * t - 1][...])
        values = gram_of(own[...], right), gram_of(across[...], right)
        values += dot3(own_parts, right_parts), dot3(across_parts, right_parts)
        slots = t, half - 1 + t, full + t, full + half - 1 + t
        for slot, value in zip(slots, values):
            out_ref[slot] = jnp.where(own_z >= t, value, value.T)

    @pl.when(first_x)
    def _():
        out_ref[2 * full] = gram_of(across[...], own[...])

    @pl.when(jnp.logical_not(first_x))
    def _():
        out_ref[2 * full] = dot3(own_parts, across_parts)


def far_kernel(ring, place_ref, done, own, across, own_f, across_f, far, far_f, keep_ref, send_ref, held):
    half = ring // 2
    n = done.shape[0]
    rows = LANES // 2
    own_z, side = place_ref[0] // 2, place_ref[1]

    @pl.when(own_z >= half)
    def _():
        for m, left in enumerate((own, across)):
            held[m] = gram_of(left[...], far[...])

    @pl.when(own_z < half)
    def _():
        right = split(far_f[...])
        for m, left in enumerate((own_f, across_f)):
            held[m] = dot3(split(left[...]), right).T

    for ref, at in ((keep_ref, side * rows), (send_ref, (1 - side) * rows)):
        here = pl.ds(pl.multiple_of(at, rows), rows)
        ref[:n] = done[:, here, :]
        ref[n:] = held[:, here, :]


def piece_kernel(ring, place_ref, one_ref, two_ref, out_ref):
    half = ring // 2
    full = 2 * half - 1
    dev_index, side = place_ref[0], place_ref[1]
    _, rows, width = out_ref.shape
    row = lax.broadcasted_iota(jnp.int32, (rows, width), 0) + side * rows
    col = lax.broadcasted_iota(jnp.int32, (rows, width), 1)
    for n in range(full):
        gram_sum = one_ref[n] + two_ref[n]
        value = gram_sum * gram_sum - (one_ref[full + n] + two_ref[full + n])
        out_ref[n] = value + jnp.where(row == col, DAMPING, 0.0) if n == 0 else value
    squared = lax.rem(dev_index, 2) == 0, dev_index // 2 >= half, dev_index // 2 >= half
    for n, is_gram in enumerate(squared):
        value = one_ref[2 * full + n] + two_ref[2 * full + n]
        out_ref[full + n] = jnp.where(is_gram, value * value, -value)


def low_kernel(count, before, place_ref, colloc, factor, *refs):
    blocks = (len(refs) - count - 3 - (count if before else 0)) // 2
    high, low, held = refs[-3:]
    outs = refs[-3 - count : -3]
    earlier = refs[2 * blocks : 2 * blocks + count] if before else ()
    rows = colloc.shape[0] // count
    high[...], low[...] = split(factor[...])
    right = jnp.concatenate([refs[2 * n][...] for n in range(blocks)], axis=0)
    value = gram_of(colloc[...], right)
    for n in range(blocks):
        held[n] = value[:, part(n)].reshape(count, rows, LANES)
    right = jnp.concatenate([refs[2 * n + 1][...] for n in range(blocks)], axis=0)
    value = dot3((high[...], low[...]), split(right))
    for n in range(blocks):
        held[blocks + n] = value[:, part(n)].reshape(count, rows, LANES)
    for k, ref in enumerate(outs):
        for n in range(before):
            ref[n] = earlier[k][n]
            ref[before + blocks + n] = earlier[k][before + n]
        for n in range(blocks):
            ref[before + n] = held[n, place_ref[2] ^ k]
            ref[2 * before + blocks + n] = held[blocks + n, place_ref[2] ^ k]


IN_VMEM = pl.BlockSpec(memory_space=pltpu.VMEM)
IN_SMEM = pl.BlockSpec(memory_space=pltpu.SMEM)
ANYWHERE = pl.BlockSpec(memory_space=pl.ANY)


def params():
    return pltpu.CompilerParams(vmem_limit_bytes=40 * 1024 * 1024)


def effort(steps):
    return pl.CostEstimate(flops=steps * 40_000_000, bytes_accessed=0, transcendentals=0)


def factor_shapes(count, total):
    part_shape = jax.ShapeDtypeStruct((total * LANES, count * LANES), jnp.bfloat16)
    inverse_shape = jax.ShapeDtypeStruct((count * LANES, LANES), jnp.bfloat16)
    return [part_shape, part_shape, inverse_shape, inverse_shape]


def factor_first(ring, count, place, pieces):
    blocks = 2 * ring
    slots = pieces[0].shape[0]
    left = (blocks - count) * LANES
    return pl.pallas_call(
        functools.partial(first_kernel, ring, count),
        in_specs=[IN_SMEM] + [ANYWHERE] * len(pieces),
        out_specs=[IN_VMEM] * 6,
        out_shape=[jax.ShapeDtypeStruct((LANES, count * LANES), jnp.float32)]
        + factor_shapes(count, blocks)
        + [jax.ShapeDtypeStruct((left, left), jnp.float32)],
        scratch_shapes=[
            pltpu.VMEM((blocks, slots, LANES, LANES), jnp.float32),
            pltpu.VMEM((blocks * LANES, count * LANES), jnp.float32),
            pltpu.SemaphoreType.DMA((len(pieces),)),
        ],
        compiler_params=params(),
        cost_estimate=effort(count * LANES // 2),
        name="cholesky_first",
    )(place, *pieces)


def factor_more(place, start, rows, count):
    total = start.shape[0] // LANES
    rest = [jax.ShapeDtypeStruct(((total - count) * LANES,) * 2, jnp.float32)] if count < total else []
    return pl.pallas_call(
        functools.partial(more_kernel, count),
        in_specs=[IN_SMEM, IN_VMEM, IN_VMEM],
        out_specs=[IN_VMEM] * (5 + len(rest)),
        out_shape=[jax.ShapeDtypeStruct((LANES, rows.shape[1] + count * LANES), jnp.float32)]
        + factor_shapes(count, total)
        + rest,
        scratch_shapes=[pltpu.VMEM((total * LANES, count * LANES), jnp.float32)],
        compiler_params=params(),
        cost_estimate=effort(count * LANES),
        name="cholesky_more",
    )(place, start, rows)


def solve_panel(ring, place, groups, sums, factors):
    rows, blocks = sums[0][0].shape[1], 2 * ring
    flat = [v for group in sums for v in group]
    groups = [(places, len(group)) for places, group in zip(groups, sums)]
    return pl.pallas_call(
        functools.partial(solve_kernel, ring, groups),
        in_specs=[IN_SMEM] + [IN_VMEM] * (len(flat) + 4 * len(factors)),
        out_specs=IN_VMEM,
        out_shape=jax.ShapeDtypeStruct((rows, blocks * LANES), jnp.float32),
        scratch_shapes=[pltpu.VMEM((blocks, rows, LANES), jnp.float32)],
        compiler_params=params(),
        cost_estimate=effort(LANES),
        name="panel_solve",
    )(place, *flat, *(v for group in factors for v in group))


def head_products(ring, place, *operands):
    return pl.pallas_call(
        functools.partial(head_kernel, ring),
        in_specs=[IN_SMEM] + [IN_VMEM] * len(operands),
        out_specs=IN_VMEM,
        out_shape=jax.ShapeDtypeStruct((4 * (ring // 2) - 1, LANES, LANES), jnp.float32),
        compiler_params=params(),
        cost_estimate=effort(64),
        name="head_products",
    )(place, *operands)


def far_products(ring, place, done, *operands):
    shape = (done.shape[0] + 2, LANES // 2, LANES)
    return pl.pallas_call(
        functools.partial(far_kernel, ring),
        in_specs=[IN_SMEM] + [IN_VMEM] * (1 + len(operands)),
        out_specs=[IN_VMEM] * 2,
        out_shape=[jax.ShapeDtypeStruct(shape, jnp.float32)] * 2,
        scratch_shapes=[pltpu.VMEM((2, LANES, LANES), jnp.float32)],
        compiler_params=params(),
        cost_estimate=effort(32),
        name="far_products",
    )(place, done, *operands)


def schur_piece(ring, place, one, two):
    return pl.pallas_call(
        functools.partial(piece_kernel, ring),
        in_specs=[IN_SMEM] + [IN_VMEM] * 2,
        out_specs=IN_VMEM,
        out_shape=jax.ShapeDtypeStruct((2 * (ring // 2) + 2, *one.shape[1:]), jnp.float32),
        compiler_params=params(),
        cost_estimate=effort(16),
        name="schur_piece",
    )(place, one, two)


def low_products(count, place, colloc, factor, blocks, earlier=()):
    rows = colloc.shape[0] // count
    before = earlier[0].shape[0] // 2 if earlier else 0
    flat = [v for pair in blocks for v in pair] + list(earlier)
    n = 2 * len(blocks)
    return pl.pallas_call(
        functools.partial(low_kernel, count, before),
        in_specs=[IN_SMEM] + [IN_VMEM] * (2 + len(flat)),
        out_specs=[IN_VMEM] * count,
        out_shape=[jax.ShapeDtypeStruct((2 * before + n, rows, LANES), jnp.float32)] * count,
        scratch_shapes=[
            pltpu.VMEM(factor.shape, jnp.bfloat16),
            pltpu.VMEM(factor.shape, jnp.bfloat16),
            pltpu.VMEM((n, count, rows, LANES), jnp.float32),
        ],
        compiler_params=params(),
        cost_estimate=effort(24 * n),
        name="low_products",
    )(place, colloc, factor, *flat)


def pair_table(ring):
    half = ring // 2
    owners = {}
    for z in range(ring):
        for x in range(2):
            me, across = 2 * z + x, 2 * z + 1 - x

            def back(t):
                return 2 * ((z - t) % ring) + x

            pairs = [(me, me)] + [(me, back(t)) for t in range(1, half)]
            pairs += [(across, back(t)) for t in range(1, half)]
            pairs += [(me, across), (me, back(half)), (across, back(half))]
            for slot, pair in enumerate(pairs):
                owners.setdefault((max(pair), min(pair)), []).append((me, slot))
    return owners, 2 * half + 2


def pick(value, axis, index):
    return lax.dynamic_index_in_dim(value, index, axis, keepdims=False)


def ring_step(value, ring, chosen=None):
    steps = [(2 * z + x, 2 * ((z + 1) % ring) + x) for z in range(ring) for x in range(2)]
    return lax.ppermute(value, "dev", [s for s in steps if chosen is None or chosen(s[1] // 2)])


def swap(value, axis, bit, chosen=None):
    steps = [(i, i ^ bit) for i in range(lax.axis_size(axis))]
    return lax.ppermute(value, axis, [s for s in steps if chosen is None or chosen(s[1] // 2)])


def after(value, *first):
    return lax.optimization_barrier((value, *first))[0]


def exchanged(parts):
    return [parts[0]] + [swap(v, "grp", k) for k, v in enumerate(parts) if k]


def halved(parts):
    own, bit = [parts[0]], 1
    while len(parts) > 1:
        received = [swap(v, "grp", bit) for v in parts[1::2]]
        own.append(received[0])
        parts = [parts[0]] + [v + w for v, w in zip(parts[2::2], received[1:])]
        bit *= 2
    return own


def coded(colloc_rows, factor_rows):
    width = max(colloc_rows.shape[1], factor_rows.shape[1])
    width += -width % LANES
    factor_rows = factor_rows * SCALE
    parts = (colloc_rows.astype(jnp.float32) * VALUE_SCALE, factor_rows * jnp.abs(factor_rows))
    return jnp.stack([padded(v.astype(jnp.float16), width) for v in parts])


def padded(value, width):
    return jnp.pad(value, ((0, 0), (0, width - value.shape[1])))


def narrow(value):
    return (value.astype(jnp.float32) * jnp.float32(1.0 / VALUE_SCALE)).astype(jnp.bfloat16)


def widen(value):
    value = value.astype(jnp.float32)
    root = jnp.sqrt(jnp.abs(value)) * jnp.float32(1.0 / SCALE)
    return jnp.where(value < 0.0, -root, root)


def on_grid(colloc, block_colloc, factor, block_factor):
    ring, count = lax.axis_size("dev") // 2, lax.axis_size("grp")
    half = ring // 2
    dev_index, grp_index = lax.axis_index("dev"), lax.axis_index("grp")
    own_z = dev_index // 2
    place = jnp.stack([dev_index, lax.rem(grp_index, 2), grp_index, 2 * ring]).astype(jnp.int32)

    def is_upper(t):
        return lax.rem(own_z - t + ring, ring) >= half

    def step(v):
        return ring_step(v, ring)

    def cross(v):
        return swap(v, "dev", 1)

    own = coded(block_colloc, block_factor)
    width = own.shape[2]

    def opened(v):
        return narrow(v[0]), widen(v[1])

    along, across = [own], [cross(own)]
    for t in range(1, half):
        along.append(step(along[-1]))
        across.append(cross(along[-1]))
    next_upper = is_upper(-1)
    first = step(pick(along[-1], 0, jnp.where(next_upper, 0, 1)))
    second = step(after(pick(along[-1], 0, jnp.where(next_upper, 1, 0)), first))

    open_along = [opened(v) for v in along]
    open_across = [opened(across[0])]
    wide_colloc, wide_factor = padded(colloc, width), padded(factor, width)
    open_along[0] = after(open_along[0], wide_colloc)
    middle = [v for pair in open_along[1:] for v in pair]
    done = head_products(
        ring, place, open_along[0][0], open_across[0][0], open_along[0][1], open_across[0][1], *middle
    )
    last = after(first, done)
    keep, send = far_products(
        ring,
        place,
        done,
        open_along[0][0],
        open_across[0][0],
        open_along[0][1],
        open_across[0][1],
        narrow(last),
        widen(last),
    )
    total = keep + swap(send, "grp", 1)
    bit = 2
    while 2 * bit < count:
        total = total + swap(total, "grp", bit)
        bit *= 2
    other = swap(total, "grp", bit)

    across_first = cross(after(first, send))

    def low_parts(chosen, earlier=()):
        return low_products(count, place, wide_colloc, wide_factor, chosen, earlier)

    soon = [open_along[0], open_across[0], *open_along[1:]]
    parts_soon = low_parts(after(soon, total))

    piece = schur_piece(ring, place, total, after(other, across[1:], parts_soon))
    hops, crossed, pairs = [piece], [cross(piece)], []
    for r in range(1, ring):
        due = (second,) if r == 1 else (across_first, crossed[r - 2])
        hops.append(after(step(hops[-1]), *due))
        pairs.append((swap(hops[r - 1], "grp", 1), swap(crossed[r - 1], "grp", 1)))
        crossed.append(cross(after(hops[-1], *(pairs[-2] if r > 1 else ()))))
    pairs.append((swap(hops[-1], "grp", 1), swap(crossed[-1], "grp", 1)))
    across_second = cross(after(second, hops[1]))
    far_along = [(step(after(first, hops[0])), None)]
    pieces = [v for hop, over, pair in zip(hops, crossed, pairs) for v in (hop, pair[0], over, pair[1])]

    def joined(t, one, two):
        upper = is_upper(t - half)
        return narrow(jnp.where(upper, one, two)), widen(jnp.where(upper, two, one))

    far_along[0] = (far_along[0][0], step(after(second, hops[half])))
    far_across = [(across_first, across_second)]
    for t in range(half + 1, ring):
        if t > half + 1:
            far_along.append(tuple(step(v) for v in far_along[-1]))
        one = cross(after(far_along[-1][0], hops[-1]))
        far_across.append((one, step(after(far_across[-1][1], hops[-1]))))

    held = after([v for t in range(1, half) for v in (across[t],)] + [first, second], crossed[-2])
    early = [opened(v) for v in held[:-2]] + [joined(half, *held[-2:])]
    parts_early = low_parts(early, parts_soon)
    sums_early = halved(parts_early)
    pieces[0] = after(pieces[0], parts_early, across_second, far_along[0][0])
    rows, *first_factor, start = factor_first(ring, ring, place, pieces)

    start = after(start, sums_early)
    rows, *second_factor, start = factor_more(place, start, rows, ring // 2)
    far_along, far_across = after((far_along, far_across), start)
    late = [joined(half + t, *v) for t, v in enumerate(far_across)]
    late += [joined(half + 1 + t, *v) for t, v in enumerate(far_along)]
    parts_late = low_parts(late)
    sums_late = exchanged(parts_late)
    factor_out, *third_factor = factor_more(place, after(start, parts_late), rows, ring - ring // 2)
    sums = after([sums_early, sums_late], factor_out)
    places_early = [0, 1] + [2 * t for t in range(1, half)] + [2 * t + 1 for t in range(1, half)] + [2 * half]
    places_late = [2 * t + 1 for t in range(half, ring)] + [2 * t for t in range(half + 1, ring)]
    panel = solve_panel(ring, place, [places_early, places_late], sums, [first_factor, second_factor, third_factor])
    return factor_out, panel[None]


def whole_kernel(place_ref, schur_ref, below_ref, rows_ref, panel_ref, low_ref, high_part, low_part, inverse_high, inverse_low):
    blocks = schur_ref.shape[0] // LANES

    def block_at(i, j):
        return schur_ref[part(i), part(j)]

    factor_columns(blocks, blocks, block_at, low_ref, high_part, low_part, (inverse_high, inverse_low), None)
    for j in range(blocks):
        own = below_ref[:, part(j)]
        if j:
            done = part(0, j)
            own = own - dot3(split(panel_ref[:, done]), (high_part[part(j), done], low_part[part(j), done]))
        panel_ref[:, part(j)] = dot3(split(own), (inverse_high[part(j), :], inverse_low[part(j), :]))
    band = rows_ref.shape[0]
    start = pl.multiple_of(place_ref[0] * band, SUBS)
    rows_ref[...] = low_ref[pl.ds(start, band), :]


def factor_whole(place, schur, below, band):
    size = schur.shape[0]
    return pl.pallas_call(
        whole_kernel,
        in_specs=[IN_SMEM, IN_VMEM, IN_VMEM],
        out_specs=[IN_VMEM, IN_VMEM],
        out_shape=[
            jax.ShapeDtypeStruct((band, size), jnp.float32),
            jax.ShapeDtypeStruct(below.shape, jnp.float32),
        ],
        scratch_shapes=[
            pltpu.VMEM((size, size), jnp.float32),
            pltpu.VMEM((size, size), jnp.bfloat16),
            pltpu.VMEM((size, size), jnp.bfloat16),
            pltpu.VMEM((size, LANES), jnp.bfloat16),
            pltpu.VMEM((size, LANES), jnp.bfloat16),
        ],
        compiler_params=params(),
        name="cholesky_whole",
    )(place, schur, below)


def on_any(colloc, block_colloc, factor, block_factor):
    grp_count, grp_index, dev_index = lax.axis_size("grp"), lax.axis_index("grp"), lax.axis_index("dev")
    band = block_colloc.shape[0]
    width = band * lax.axis_size("dev")
    points = jnp.concatenate([block_colloc, colloc], axis=0)
    earlier = jnp.concatenate([block_factor, factor], axis=0)
    dims = (((1,), (1,)), ((), ()))
    gram = lax.dot_general(
        points, lax.all_gather(block_colloc, "dev", axis=0, tiled=True), dims, preferred_element_type=jnp.float32
    )
    update = lax.dot_general(
        earlier,
        lax.all_gather(block_factor, "dev", axis=0, tiled=True),
        dims,
        precision=lax.Precision.HIGHEST,
        preferred_element_type=jnp.float32,
    )
    gram_low = lax.psum_scatter(gram[band:], "grp", scatter_dimension=0, tiled=True)
    update_low = lax.psum_scatter(update[band:], "grp", scatter_dimension=0, tiled=True)
    below = gram_low * gram_low - update_low
    slice_width = width // grp_count
    row = dev_index * band + lax.broadcasted_iota(jnp.int32, (band, slice_width), 0)
    col = grp_index * slice_width + lax.broadcasted_iota(jnp.int32, (band, slice_width), 1)
    gram_slice = lax.psum_scatter(gram[:band], "grp", scatter_dimension=1, tiled=True)
    update_slice = lax.psum_scatter(update[:band], "grp", scatter_dimension=1, tiled=True)
    damping = jnp.where(row == col, jnp.float32(DAMPING), jnp.float32(0.0))
    piece = gram_slice * gram_slice + damping - update_slice
    slab = lax.all_gather(piece, "grp", axis=1, tiled=True)
    schur = lax.all_gather(slab, "dev", axis=0, tiled=True)
    place = jnp.reshape(dev_index, (1,)).astype(jnp.int32)
    factor_rows, panel_rows = factor_whole(place, schur, below, band)
    return factor_rows, panel_rows[None]


def on_device(colloc, block_colloc, factor, block_factor):
    devices, count = lax.axis_size("dev"), lax.axis_size("grp")
    gridded = devices % 4 == 0 and devices >= 8 and block_colloc.shape[0] == LANES and count >= 2 and count & (count - 1) == 0
    form = on_grid if gridded else on_any
    return form(colloc, block_colloc, factor, block_factor)


def solution(mesh):
    placed = (P("dev", "grp"), P("dev", "grp"), P("dev", "grp"), P("dev", "grp"))
    return jax.shard_map(
        on_device,
        mesh=mesh,
        in_specs=placed,
        out_specs=(P("dev", None), P("dev", "grp", None)),
        check_vma=False,
    )
```

```python
import functools
import jax
import jax.numpy as jnp
from jax import lax
from jax.sharding import PartitionSpec as P
from jax.experimental import pallas as pl
from jax.experimental.pallas import tpu as pltpu

DAMPING = 0.0625
SCALE = 896.0
VALUE_SCALE = 16384.0
LANES = 128
SUBS = 8
NT = ((1,), (1,))


def split(value):
    high = value.astype(jnp.bfloat16)
    low = (value - high.astype(jnp.float32)).astype(jnp.bfloat16)
    return high, low


def dot3(left, right):
    (left_high, left_low), (right_high, right_low) = left, right
    return lax.dot_general(
        jnp.concatenate([left_high, left_high, left_low], axis=1),
        jnp.concatenate([right_high, right_low, right_high], axis=1),
        (NT, ((), ())),
        preferred_element_type=jnp.float32,
    )


def reciprocal(value):
    return pl.reciprocal(value, approx=True)


def over_lanes(value, column):
    return jnp.broadcast_to(value[:, column : column + 1], (SUBS, LANES))


def over_subs(value, row):
    return jnp.broadcast_to(value[row : row + 1, :], (SUBS, LANES))


def tree_sum(values):
    while len(values) > 1:
        values = [a + b for a, b in zip(values[::2], values[1::2])] + values[len(values) // 2 * 2 :]
    return values[0]


def factor_block(block):
    lane = lax.broadcasted_iota(jnp.int32, (SUBS, LANES), 1)
    sub = lax.broadcasted_iota(jnp.int32, (SUBS, LANES), 0)
    strips = LANES // SUBS
    rows = [block[SUBS * s : SUBS * (s + 1), :] for s in range(strips)]
    upper, inverse = [], []
    for s in range(strips):
        first = SUBS * s
        pivots = (lane >= first) & (lane < first + SUBS)
        own = rows[s]
        unit = jnp.where(lane - first == sub, 1.0, jnp.where(pivots, 0.0, own))
        columns = [over_lanes(own, first + k) for k in range(SUBS)]
        kept_own, kept_unit, diagonal = own, unit, None
        for k in range(0, SUBS, 2):
            one, two = sub == k, sub == k + 1
            both = one | two
            a, b, c = over_subs(columns[k], k), over_subs(columns[k + 1], k), over_subs(columns[k + 1], k + 1)
            det = a * c - b * b
            share = reciprocal(det)
            lead = jnp.where(one, c, jnp.where(two, -b, columns[k + 1] * b - columns[k] * c)) * share
            trail = jnp.where(one, -b, jnp.where(two, a, columns[k] * b - columns[k + 1] * a)) * share

            def swept(value):
                return jnp.where(both, 0.0, value) + (lead * over_subs(value, k) + trail * over_subs(value, k + 1))

            inverse_a = reciprocal(a)
            ratio = b * inverse_a
            second = det * inverse_a
            if k == 0:
                diagonal = jnp.where(two, second, a)
            else:
                diagonal = jnp.where(one, a, jnp.where(two, second, diagonal))
            kept_own = jnp.where(one, own, jnp.where(two, own - ratio * over_subs(own, k), kept_own))
            kept_unit = jnp.where(one, unit, jnp.where(two, unit - ratio * over_subs(unit, k), kept_unit))
            for q in range(k + 2, SUBS):
                columns[q] = swept(columns[q])
            own, unit = swept(own), swept(unit)
        root = lax.rsqrt(diagonal)
        upper.append(jnp.where(lane >= first + sub, kept_own * root, 0.0))
        inverse.append(jnp.where(lane <= first + sub, kept_unit * root, 0.0))
        spread = [over_subs(unit, k) for k in range(SUBS)]
        for i in range(s + 1, strips):
            change = tree_sum([over_lanes(rows[i], first + k) * spread[k] for k in range(SUBS)])
            rows[i] = jnp.where(pivots, 0.0, rows[i]) - change
    return jnp.concatenate(upper, axis=0), jnp.concatenate(inverse, axis=0)


def part(j, n=1):
    return slice(j * LANES, (j + n) * LANES)


def factor_columns(count, total, block_at, low_ref, high_ref, low_part_ref, inverse_refs, rest_ref):
    zero = jnp.zeros((LANES, LANES), jnp.float32)

    def held(rows, first, n):
        return high_ref[rows, part(first, n)], low_part_ref[rows, part(first, n)]

    def column_at(i, n):
        value = jnp.concatenate([block_at(m, i) for m in range(i, total)], axis=0)
        return value - dot3(held(part(i, total - i), 0, n), held(part(i), 0, n)) if n else value

    diagonal = block_at(0, 0)
    for j in range(count):
        below = slice((j + 1) * LANES, total * LANES)
        if j + 1 < total:
            ahead = column_at(j, j)[LANES:]
        if j + 1 < count:
            next_diagonal = block_at(j + 1, j + 1)
            if j:
                next_diagonal = next_diagonal - dot3(held(part(j + 1), 0, j), held(part(j + 1), 0, j))
        elif rest_ref is not None:
            remainder = [column_at(i, j) for i in range(count, total)]
        upper, inverse = factor_block(diagonal)
        inverse_parts = split(inverse)
        for ref, value in zip(inverse_refs, inverse_parts):
            ref[part(j), :] = value
        low_ref[part(j), part(j)] = upper.T
        for i in range(j):
            low_ref[part(i), part(j)] = zero
        if j + 1 < total:
            column = dot3(split(ahead), inverse_parts)
            low_ref[below, part(j)] = column
            column_parts = split(column)
            high_ref[below, part(j)], low_part_ref[below, part(j)] = column_parts
        if j + 1 < count:
            first = tuple(v[:LANES] for v in column_parts)
            diagonal = next_diagonal - dot3(first, first)
    for i in range(count, total):
        value = remainder[i - count] - dot3(held(part(i, total - i), count - 1, 1), held(part(i), count - 1, 1))
        rest_ref[part(i - count, total - i), part(i - count)] = value


def first_kernel(ring, count, place_ref, *refs):
    devices = 2 * ring
    pieces = refs[: 2 * devices]
    rows_ref, high_ref, low_part_ref, inverse_high, inverse_low, rest_ref, schur, low_ref, arrived = refs[2 * devices :]
    dev_index, side = place_ref[0], place_ref[1]
    own_z, own_x = dev_index // 2, lax.rem(dev_index, 2)
    half_rows = LANES // 2
    copies = []
    for r in range(ring):
        for q in range(2):
            who = 2 * lax.rem(own_z - r + ring, ring) + lax.rem(own_x + q, 2)
            for other in range(2):
                at = pl.multiple_of(lax.rem(side + other, 2) * half_rows, half_rows)
                number = 2 * (2 * r + q) + other
                copies.append(
                    pltpu.make_async_copy(
                        pieces[number], schur.at[who, :, pl.ds(at, half_rows), :], arrived.at[number]
                    )
                )
    for copy in copies:
        copy.start()
    for copy in copies:
        copy.wait()
    owners, _ = pair_table(ring)

    def block_at(i, j):
        return tree_sum([schur[who, slot] for who, slot in owners[i, j]])

    factor_columns(count, devices, block_at, low_ref, high_ref, low_part_ref, (inverse_high, inverse_low), rest_ref)
    start = pl.multiple_of(dev_index * LANES, LANES)
    rows_ref[...] = low_ref[pl.ds(start, LANES), :]


def more_kernel(count, place_ref, start_ref, rows_ref, out_ref, high_ref, low_part_ref, inverse_high, inverse_low, *refs):
    rest_ref, low_ref = refs if len(refs) == 2 else (None, *refs)
    total = start_ref.shape[0] // LANES
    done = rows_ref.shape[1]
    skipped = place_ref[3] - total

    def block_at(i, j):
        return start_ref[part(i), part(j)]

    factor_columns(count, total, block_at, low_ref, high_ref, low_part_ref, (inverse_high, inverse_low), rest_ref)
    out_ref[:, :done] = rows_ref[...]
    row = (place_ref[0] - skipped) * LANES
    at = pl.multiple_of(jnp.maximum(row, 0), LANES)
    out_ref[:, done:] = jnp.where(row >= 0, low_ref[pl.ds(at, LANES), :], 0.0)


def solve_kernel(ring, groups, place_ref, *refs):
    sums = refs[: sum(summands for _, summands in groups)]
    *parts, panel_ref, held = refs[len(sums) :]
    blocks = 2 * ring
    own_z, own_x = place_ref[0] // 2, lax.rem(place_ref[0], 2)
    for places, summands in groups:
        group, sums = sums[:summands], sums[summands:]
        for n, place in enumerate(places):
            who = 2 * lax.rem(own_z - place // 2 + ring, ring) + lax.rem(own_x + place % 2, 2)
            gram_sum = tree_sum([ref[n] for ref in group])
            held[who] = gram_sum * gram_sum - tree_sum([ref[len(places) + n] for ref in group])
    below = jnp.concatenate([held[i] for i in range(blocks)], axis=1)
    columns = []
    while parts:
        group, parts = parts[:4], parts[4:]
        columns += [(group, n, len(columns)) for n in range(group[0].shape[1] // LANES)]
    for j in range(blocks):
        (high, low, inverse_high, inverse_low), n, skip = columns[j]
        value = dot3(split(below[:, :LANES]), (inverse_high[part(n), :], inverse_low[part(n), :]))
        panel_ref[:, part(j)] = value
        if j + 1 < blocks:
            rest = slice((j + 1 - skip) * LANES, (blocks - skip) * LANES)
            below = below[:, LANES:] - dot3(split(value), (high[rest, part(n)], low[rest, part(n)]))


def gram_of(left, right):
    return lax.dot_general(left, right, (NT, ((), ())), preferred_element_type=jnp.float32)


def head_kernel(ring, place_ref, own, across, own_f, across_f, *refs):
    half = ring // 2
    middle, out_ref = refs[:-1], refs[-1]
    own_z, first_x = place_ref[0] // 2, lax.rem(place_ref[0], 2) == 0
    full = 2 * half - 1
    own_parts, across_parts = split(own_f[...]), split(across_f[...])
    out_ref[0] = gram_of(own[...], own[...])
    out_ref[full] = dot3(own_parts, own_parts)
    for t in range(1, half):
        right, right_parts = middle[2 * t - 2][...], split(middle[2 * t - 1][...])
        values = gram_of(own[...], right), gram_of(across[...], right)
        values += dot3(own_parts, right_parts), dot3(across_parts, right_parts)
        slots = t, half - 1 + t, full + t, full + half - 1 + t
        for slot, value in zip(slots, values):
            out_ref[slot] = jnp.where(own_z >= t, value, value.T)

    @pl.when(first_x)
    def _():
        out_ref[2 * full] = gram_of(across[...], own[...])

    @pl.when(jnp.logical_not(first_x))
    def _():
        out_ref[2 * full] = dot3(own_parts, across_parts)


def far_kernel(ring, place_ref, done, own, across, own_f, across_f, far, far_f, keep_ref, send_ref, held):
    half = ring // 2
    n = done.shape[0]
    rows = LANES // 2
    own_z, side = place_ref[0] // 2, place_ref[1]

    @pl.when(own_z >= half)
    def _():
        for m, left in enumerate((own, across)):
            held[m] = gram_of(left[...], far[...])

    @pl.when(own_z < half)
    def _():
        right = split(far_f[...])
        for m, left in enumerate((own_f, across_f)):
            held[m] = dot3(split(left[...]), right).T

    for ref, at in ((keep_ref, side * rows), (send_ref, (1 - side) * rows)):
        here = pl.ds(pl.multiple_of(at, rows), rows)
        ref[:n] = done[:, here, :]
        ref[n:] = held[:, here, :]


def piece_kernel(ring, place_ref, one_ref, two_ref, out_ref):
    half = ring // 2
    full = 2 * half - 1
    dev_index, side = place_ref[0], place_ref[1]
    _, rows, width = out_ref.shape
    row = lax.broadcasted_iota(jnp.int32, (rows, width), 0) + side * rows
    col = lax.broadcasted_iota(jnp.int32, (rows, width), 1)
    for n in range(full):
        gram_sum = one_ref[n] + two_ref[n]
        value = gram_sum * gram_sum - (one_ref[full + n] + two_ref[full + n])
        out_ref[n] = value + jnp.where(row == col, DAMPING, 0.0) if n == 0 else value
    squared = lax.rem(dev_index, 2) == 0, dev_index // 2 >= half, dev_index // 2 >= half
    for n, is_gram in enumerate(squared):
        value = one_ref[2 * full + n] + two_ref[2 * full + n]
        out_ref[full + n] = jnp.where(is_gram, value * value, -value)


def low_kernel(count, before, place_ref, colloc, factor, *refs):
    blocks = (len(refs) - count - 3 - (count if before else 0)) // 2
    high, low, held = refs[-3:]
    outs = refs[-3 - count : -3]
    earlier = refs[2 * blocks : 2 * blocks + count] if before else ()
    rows = colloc.shape[0] // count
    high[...], low[...] = split(factor[...])
    right = jnp.concatenate([refs[2 * n][...] for n in range(blocks)], axis=0)
    value = gram_of(colloc[...], right)
    for n in range(blocks):
        held[n] = value[:, part(n)].reshape(count, rows, LANES)
    right = jnp.concatenate([refs[2 * n + 1][...] for n in range(blocks)], axis=0)
    value = dot3((high[...], low[...]), split(right))
    for n in range(blocks):
        held[blocks + n] = value[:, part(n)].reshape(count, rows, LANES)
    for k, ref in enumerate(outs):
        for n in range(before):
            ref[n] = earlier[k][n]
            ref[before + blocks + n] = earlier[k][before + n]
        for n in range(blocks):
            ref[before + n] = held[n, place_ref[2] ^ k]
            ref[2 * before + blocks + n] = held[blocks + n, place_ref[2] ^ k]


IN_VMEM = pl.BlockSpec(memory_space=pltpu.VMEM)
IN_SMEM = pl.BlockSpec(memory_space=pltpu.SMEM)
ANYWHERE = pl.BlockSpec(memory_space=pl.ANY)


def params(mebibytes=16):
    return pltpu.CompilerParams(vmem_limit_bytes=mebibytes * 1024 * 1024)


def effort(steps):
    return pl.CostEstimate(flops=steps * 40_000_000, bytes_accessed=0, transcendentals=0)


def factor_shapes(count, total):
    part_shape = jax.ShapeDtypeStruct((total * LANES, count * LANES), jnp.bfloat16)
    inverse_shape = jax.ShapeDtypeStruct((count * LANES, LANES), jnp.bfloat16)
    return [part_shape, part_shape, inverse_shape, inverse_shape]


def factor_first(ring, count, place, pieces):
    blocks = 2 * ring
    slots = pieces[0].shape[0]
    left = (blocks - count) * LANES
    return pl.pallas_call(
        functools.partial(first_kernel, ring, count),
        in_specs=[IN_SMEM] + [ANYWHERE] * len(pieces),
        out_specs=[IN_VMEM] * 6,
        out_shape=[jax.ShapeDtypeStruct((LANES, count * LANES), jnp.float32)]
        + factor_shapes(count, blocks)
        + [jax.ShapeDtypeStruct((left, left), jnp.float32)],
        scratch_shapes=[
            pltpu.VMEM((blocks, slots, LANES, LANES), jnp.float32),
            pltpu.VMEM((blocks * LANES, count * LANES), jnp.float32),
            pltpu.SemaphoreType.DMA((len(pieces),)),
        ],
        compiler_params=params(),
        cost_estimate=effort(count * LANES),
        name="cholesky_first",
    )(place, *pieces)


def factor_more(place, start, rows, count, steps):
    total = start.shape[0] // LANES
    rest = [jax.ShapeDtypeStruct(((total - count) * LANES,) * 2, jnp.float32)] if count < total else []
    return pl.pallas_call(
        functools.partial(more_kernel, count),
        in_specs=[IN_SMEM, IN_VMEM, IN_VMEM],
        out_specs=[IN_VMEM] * (5 + len(rest)),
        out_shape=[jax.ShapeDtypeStruct((LANES, rows.shape[1] + count * LANES), jnp.float32)]
        + factor_shapes(count, total)
        + rest,
        scratch_shapes=[pltpu.VMEM((total * LANES, count * LANES), jnp.float32)],
        compiler_params=params(),
        cost_estimate=effort(count * steps),
        name="cholesky_more",
    )(place, start, rows)


def solve_panel(ring, place, groups, sums, factors):
    rows, blocks = sums[0][0].shape[1], 2 * ring
    flat = [v for group in sums for v in group]
    groups = [(places, len(group)) for places, group in zip(groups, sums)]
    return pl.pallas_call(
        functools.partial(solve_kernel, ring, groups),
        in_specs=[IN_SMEM] + [IN_VMEM] * (len(flat) + 4 * len(factors)),
        out_specs=IN_VMEM,
        out_shape=jax.ShapeDtypeStruct((rows, blocks * LANES), jnp.float32),
        scratch_shapes=[pltpu.VMEM((blocks, rows, LANES), jnp.float32)],
        compiler_params=params(),
        cost_estimate=effort(LANES),
        name="panel_solve",
    )(place, *flat, *(v for group in factors for v in group))


def head_products(ring, place, *operands):
    return pl.pallas_call(
        functools.partial(head_kernel, ring),
        in_specs=[IN_SMEM] + [IN_VMEM] * len(operands),
        out_specs=IN_VMEM,
        out_shape=jax.ShapeDtypeStruct((4 * (ring // 2) - 1, LANES, LANES), jnp.float32),
        compiler_params=params(),
        cost_estimate=effort(64),
        name="head_products",
    )(place, *operands)


def far_products(ring, place, done, *operands):
    shape = (done.shape[0] + 2, LANES // 2, LANES)
    return pl.pallas_call(
        functools.partial(far_kernel, ring),
        in_specs=[IN_SMEM] + [IN_VMEM] * (1 + len(operands)),
        out_specs=[IN_VMEM] * 2,
        out_shape=[jax.ShapeDtypeStruct(shape, jnp.float32)] * 2,
        scratch_shapes=[pltpu.VMEM((2, LANES, LANES), jnp.float32)],
        compiler_params=params(),
        cost_estimate=effort(32),
        name="far_products",
    )(place, done, *operands)


def schur_piece(ring, place, one, two):
    return pl.pallas_call(
        functools.partial(piece_kernel, ring),
        in_specs=[IN_SMEM] + [IN_VMEM] * 2,
        out_specs=IN_VMEM,
        out_shape=jax.ShapeDtypeStruct((2 * (ring // 2) + 2, *one.shape[1:]), jnp.float32),
        compiler_params=params(),
        cost_estimate=effort(16),
        name="schur_piece",
    )(place, one, two)


def low_products(count, place, colloc, factor, blocks, earlier=()):
    rows = colloc.shape[0] // count
    before = earlier[0].shape[0] // 2 if earlier else 0
    flat = [v for pair in blocks for v in pair] + list(earlier)
    n = 2 * len(blocks)
    return pl.pallas_call(
        functools.partial(low_kernel, count, before),
        in_specs=[IN_SMEM] + [IN_VMEM] * (2 + len(flat)),
        out_specs=[IN_VMEM] * count,
        out_shape=[jax.ShapeDtypeStruct((2 * before + n, rows, LANES), jnp.float32)] * count,
        scratch_shapes=[
            pltpu.VMEM(factor.shape, jnp.bfloat16),
            pltpu.VMEM(factor.shape, jnp.bfloat16),
            pltpu.VMEM((n, count, rows, LANES), jnp.float32),
        ],
        compiler_params=params(30),
        cost_estimate=effort(24 * n),
        name="low_products",
    )(place, colloc, factor, *flat)


def pair_table(ring):
    half = ring // 2
    owners = {}
    for z in range(ring):
        for x in range(2):
            me, across = 2 * z + x, 2 * z + 1 - x

            def back(t):
                return 2 * ((z - t) % ring) + x

            pairs = [(me, me)] + [(me, back(t)) for t in range(1, half)]
            pairs += [(across, back(t)) for t in range(1, half)]
            pairs += [(me, across), (me, back(half)), (across, back(half))]
            for slot, pair in enumerate(pairs):
                owners.setdefault((max(pair), min(pair)), []).append((me, slot))
    return owners, 2 * half + 2


def pick(value, axis, index):
    return lax.dynamic_index_in_dim(value, index, axis, keepdims=False)


def ring_step(value, ring, chosen=None):
    steps = [(2 * z + x, 2 * ((z + 1) % ring) + x) for z in range(ring) for x in range(2)]
    return lax.ppermute(value, "dev", [s for s in steps if chosen is None or chosen(s[1] // 2)])


def swap(value, axis, bit, chosen=None):
    steps = [(i, i ^ bit) for i in range(lax.axis_size(axis))]
    return lax.ppermute(value, axis, [s for s in steps if chosen is None or chosen(s[1] // 2)])


def after(value, *first):
    return lax.optimization_barrier((value, *first))[0]


def exchanged(parts):
    return [parts[0]] + [swap(v, "grp", k) for k, v in enumerate(parts) if k]


def halved(parts):
    own, bit, between = [parts[0]], 1, []
    while len(parts) > 1:
        received = [swap(v, "grp", bit) for v in parts[1::2]]
        own.append(received[0])
        parts = [parts[0]] + [v + w for v, w in zip(parts[2::2], received[1:])]
        between += parts[1:]
        bit *= 2
    return own, between


def coded(colloc_rows, factor_rows):
    width = max(colloc_rows.shape[1], factor_rows.shape[1])
    width += -width % LANES
    factor_rows = factor_rows * SCALE
    parts = (colloc_rows.astype(jnp.float32) * VALUE_SCALE, factor_rows * jnp.abs(factor_rows))
    return jnp.stack([padded(v.astype(jnp.float16), width) for v in parts])


def padded(value, width):
    return jnp.pad(value, ((0, 0), (0, width - value.shape[1])))


def narrow(value):
    return (value.astype(jnp.float32) * jnp.float32(1.0 / VALUE_SCALE)).astype(jnp.bfloat16)


def widen(value):
    value = value.astype(jnp.float32)
    root = jnp.sqrt(jnp.abs(value)) * jnp.float32(1.0 / SCALE)
    return jnp.where(value < 0.0, -root, root)


def on_grid(colloc, block_colloc, factor, block_factor):
    ring, count = lax.axis_size("dev") // 2, lax.axis_size("grp")
    half = ring // 2
    dev_index, grp_index = lax.axis_index("dev"), lax.axis_index("grp")
    own_z = dev_index // 2
    place = jnp.stack([dev_index, lax.rem(grp_index, 2), grp_index, 2 * ring]).astype(jnp.int32)

    def is_upper(t):
        return lax.rem(own_z - t + ring, ring) >= half

    def step(v):
        return ring_step(v, ring)

    def cross(v):
        return swap(v, "dev", 1)

    own = coded(block_colloc, block_factor)
    width = own.shape[2]

    def opened(v):
        return narrow(v[0]), widen(v[1])

    along, across = [own], [cross(own)]
    for t in range(1, half):
        along.append(step(along[-1]))
        across.append(cross(along[-1]))
    next_upper = is_upper(-1)
    first = step(pick(along[-1], 0, jnp.where(next_upper, 0, 1)))
    second = step(after(pick(along[-1], 0, jnp.where(next_upper, 1, 0)), first))

    open_along = [opened(v) for v in along]
    open_across = [opened(across[0])]
    wide_colloc, wide_factor = padded(colloc, width), padded(factor, width)
    open_along[0] = after(open_along[0], wide_colloc)
    middle = [v for pair in open_along[1:] for v in pair]
    done = head_products(
        ring, place, open_along[0][0], open_across[0][0], open_along[0][1], open_across[0][1], *middle
    )
    last = after(first, done)
    keep, send = far_products(
        ring,
        place,
        done,
        open_along[0][0],
        open_across[0][0],
        open_along[0][1],
        open_across[0][1],
        narrow(last),
        widen(last),
    )
    total = keep + swap(send, "grp", 1)
    bit = 2
    while 2 * bit < count:
        total = total + swap(total, "grp", bit)
        bit *= 2
    other = swap(total, "grp", bit)

    across_first = cross(after(first, send))

    def low_parts(chosen, earlier=()):
        return low_products(count, place, wide_colloc, wide_factor, chosen, earlier)

    soon = [open_along[0], open_across[0], *open_along[1:]]
    parts_soon = low_parts(after(soon, total))

    piece = schur_piece(ring, place, total, after(other, across[1:], parts_soon))
    hops, crossed, pairs = [piece], [cross(piece)], []
    for r in range(1, ring):
        due = (second,) if r == 1 else (across_first,) if r == 2 else tuple(crossed[: r - 1])
        hops.append(after(step(hops[-1]), *due))
        pairs.append((swap(hops[r - 1], "grp", 1), swap(crossed[r - 1], "grp", 1)))
        crossed.append(cross(hops[-1]))
    pairs.append((swap(hops[-1], "grp", 1), swap(crossed[-1], "grp", 1)))
    across_second = cross(after(second, crossed[-1]))
    far_along = [(step(after(first, hops[-1])), None)]
    pieces = [v for hop, over, pair in zip(hops, crossed, pairs) for v in (hop, pair[0], over, pair[1])]

    def joined(t, one, two):
        upper = is_upper(t - half)
        return narrow(jnp.where(upper, one, two)), widen(jnp.where(upper, two, one))

    far_along[0] = (far_along[0][0], step(after(second, hops[-1])))
    far_across = [(across_first, across_second)]
    held = after([v for t in range(1, half) for v in (across[t],)] + [first, second], crossed[-2])
    early = [opened(v) for v in held[:-2]] + [joined(half, *held[-2:])]
    parts_early = low_parts(early, parts_soon)
    sums_early, between = halved(parts_early)
    pieces[0] = after(pieces[0], parts_early, across_first)
    quarter = ring // 2
    rows, *one, start = factor_first(ring, quarter, place, pieces)
    seconds = [far_across[0][1]]
    for t in range(half + 1, ring):
        if t > half + 1:
            far_along.append(tuple(step(v) for v in far_along[-1]))
        seconds.append(step(after(seconds[-1], start)))
    start = after(start, between)
    rows, *two, start = factor_more(place, start, rows, quarter, LANES // 2)
    far_across += [(cross(after(one_half, start)), v) for (one_half, _), v in zip(far_along, seconds[1:])]
    rows, *three, start = factor_more(place, start, rows, quarter, LANES // 2)
    start = after(start, sums_early)
    far_along, far_across = after((far_along, far_across), start)
    late = [joined(half + t, *v) for t, v in enumerate(far_across)]
    late += [joined(half + 1 + t, *v) for t, v in enumerate(far_along)]
    parts_late = low_parts(late)
    sums_late = exchanged(parts_late)
    factor_out, *four = factor_more(place, after(start, parts_late), rows, 2 * ring - 3 * quarter, LANES)
    sums = after([sums_early, sums_late], factor_out)
    places_early = [0, 1] + [2 * t for t in range(1, half)] + [2 * t + 1 for t in range(1, half)] + [2 * half]
    places_late = [2 * t + 1 for t in range(half, ring)] + [2 * t for t in range(half + 1, ring)]
    panel = solve_panel(ring, place, [places_early, places_late], sums, [one, two, three, four])
    return factor_out, panel[None]


def whole_kernel(place_ref, schur_ref, below_ref, rows_ref, panel_ref, low_ref, high_part, low_part, inverse_high, inverse_low):
    blocks = schur_ref.shape[0] // LANES

    def block_at(i, j):
        return schur_ref[part(i), part(j)]

    factor_columns(blocks, blocks, block_at, low_ref, high_part, low_part, (inverse_high, inverse_low), None)
    for j in range(blocks):
        own = below_ref[:, part(j)]
        if j:
            done = part(0, j)
            own = own - dot3(split(panel_ref[:, done]), (high_part[part(j), done], low_part[part(j), done]))
        panel_ref[:, part(j)] = dot3(split(own), (inverse_high[part(j), :], inverse_low[part(j), :]))
    band = rows_ref.shape[0]
    start = pl.multiple_of(place_ref[0] * band, SUBS)
    rows_ref[...] = low_ref[pl.ds(start, band), :]


def factor_whole(place, schur, below, band):
    size = schur.shape[0]
    return pl.pallas_call(
        whole_kernel,
        in_specs=[IN_SMEM, IN_VMEM, IN_VMEM],
        out_specs=[IN_VMEM, IN_VMEM],
        out_shape=[
            jax.ShapeDtypeStruct((band, size), jnp.float32),
            jax.ShapeDtypeStruct(below.shape, jnp.float32),
        ],
        scratch_shapes=[
            pltpu.VMEM((size, size), jnp.float32),
            pltpu.VMEM((size, size), jnp.bfloat16),
            pltpu.VMEM((size, size), jnp.bfloat16),
            pltpu.VMEM((size, LANES), jnp.bfloat16),
            pltpu.VMEM((size, LANES), jnp.bfloat16),
        ],
        compiler_params=params(30),
        name="cholesky_whole",
    )(place, schur, below)


def on_any(colloc, block_colloc, factor, block_factor):
    grp_count, grp_index, dev_index = lax.axis_size("grp"), lax.axis_index("grp"), lax.axis_index("dev")
    band = block_colloc.shape[0]
    width = band * lax.axis_size("dev")
    points = jnp.concatenate([block_colloc, colloc], axis=0)
    earlier = jnp.concatenate([block_factor, factor], axis=0)
    dims = (((1,), (1,)), ((), ()))
    gram = lax.dot_general(
        points, lax.all_gather(block_colloc, "dev", axis=0, tiled=True), dims, preferred_element_type=jnp.float32
    )
    update = lax.dot_general(
        earlier,
        lax.all_gather(block_factor, "dev", axis=0, tiled=True),
        dims,
        precision=lax.Precision.HIGHEST,
        preferred_element_type=jnp.float32,
    )
    gram_low = lax.psum_scatter(gram[band:], "grp", scatter_dimension=0, tiled=True)
    update_low = lax.psum_scatter(update[band:], "grp", scatter_dimension=0, tiled=True)
    below = gram_low * gram_low - update_low
    slice_width = width // grp_count
    row = dev_index * band + lax.broadcasted_iota(jnp.int32, (band, slice_width), 0)
    col = grp_index * slice_width + lax.broadcasted_iota(jnp.int32, (band, slice_width), 1)
    gram_slice = lax.psum_scatter(gram[:band], "grp", scatter_dimension=1, tiled=True)
    update_slice = lax.psum_scatter(update[:band], "grp", scatter_dimension=1, tiled=True)
    damping = jnp.where(row == col, jnp.float32(DAMPING), jnp.float32(0.0))
    piece = gram_slice * gram_slice + damping - update_slice
    slab = lax.all_gather(piece, "grp", axis=1, tiled=True)
    schur = lax.all_gather(slab, "dev", axis=0, tiled=True)
    place = jnp.reshape(dev_index, (1,)).astype(jnp.int32)
    factor_rows, panel_rows = factor_whole(place, schur, below, band)
    return factor_rows, panel_rows[None]


def on_device(colloc, block_colloc, factor, block_factor):
    devices, count = lax.axis_size("dev"), lax.axis_size("grp")
    gridded = devices % 4 == 0 and devices >= 8 and block_colloc.shape[0] == LANES and count >= 2 and count & (count - 1) == 0
    form = on_grid if gridded else on_any
    return form(colloc, block_colloc, factor, block_factor)


def solution(mesh):
    placed = (P("dev", "grp"), P("dev", "grp"), P("dev", "grp"), P("dev", "grp"))
    return jax.shard_map(
        on_device,
        mesh=mesh,
        in_specs=placed,
        out_specs=(P("dev", None), P("dev", "grp", None)),
        check_vma=False,
    )
```

```python
import functools
import jax
import jax.numpy as jnp
from jax import lax
from jax.sharding import PartitionSpec as P
from jax.experimental import pallas as pl
from jax.experimental.pallas import tpu as pltpu

DAMPING = 0.0625
SCALE = 896.0
VALUE_SCALE = 16384.0
LANES = 128
SUBS = 8
NT = ((1,), (1,))


def split(value):
    high = value.astype(jnp.bfloat16)
    low = (value - high.astype(jnp.float32)).astype(jnp.bfloat16)
    return high, low


def dot3(left, right):
    (left_high, left_low), (right_high, right_low) = left, right
    return lax.dot_general(
        jnp.concatenate([left_high, left_high, left_low], axis=1),
        jnp.concatenate([right_high, right_low, right_high], axis=1),
        (NT, ((), ())),
        preferred_element_type=jnp.float32,
    )


def reciprocal(value):
    return pl.reciprocal(value, approx=True)


def over_lanes(value, column):
    return jnp.broadcast_to(value[:, column : column + 1], (SUBS, LANES))


def over_subs(value, row):
    return jnp.broadcast_to(value[row : row + 1, :], (SUBS, LANES))


def tree_sum(values):
    while len(values) > 1:
        values = [a + b for a, b in zip(values[::2], values[1::2])] + values[len(values) // 2 * 2 :]
    return values[0]


def factor_block(block):
    lane = lax.broadcasted_iota(jnp.int32, (SUBS, LANES), 1)
    sub = lax.broadcasted_iota(jnp.int32, (SUBS, LANES), 0)
    strips = LANES // SUBS
    rows = [block[SUBS * s : SUBS * (s + 1), :] for s in range(strips)]
    upper, inverse = [], []
    for s in range(strips):
        first = SUBS * s
        pivots = (lane >= first) & (lane < first + SUBS)
        own = rows[s]
        unit = jnp.where(lane - first == sub, 1.0, jnp.where(pivots, 0.0, own))
        columns = [over_lanes(own, first + k) for k in range(SUBS)]
        kept_own, kept_unit, diagonal = own, unit, None
        for k in range(0, SUBS, 2):
            one, two = sub == k, sub == k + 1
            both = one | two
            a, b, c = over_subs(columns[k], k), over_subs(columns[k + 1], k), over_subs(columns[k + 1], k + 1)
            det = a * c - b * b
            share = reciprocal(det)
            lead = jnp.where(one, c, jnp.where(two, -b, columns[k + 1] * b - columns[k] * c)) * share
            trail = jnp.where(one, -b, jnp.where(two, a, columns[k] * b - columns[k + 1] * a)) * share

            def swept(value):
                return jnp.where(both, 0.0, value) + (lead * over_subs(value, k) + trail * over_subs(value, k + 1))

            inverse_a = reciprocal(a)
            ratio = b * inverse_a
            second = det * inverse_a
            if k == 0:
                diagonal = jnp.where(two, second, a)
            else:
                diagonal = jnp.where(one, a, jnp.where(two, second, diagonal))
            kept_own = jnp.where(one, own, jnp.where(two, own - ratio * over_subs(own, k), kept_own))
            kept_unit = jnp.where(one, unit, jnp.where(two, unit - ratio * over_subs(unit, k), kept_unit))
            for q in range(k + 2, SUBS):
                columns[q] = swept(columns[q])
            own, unit = swept(own), swept(unit)
        root = lax.rsqrt(diagonal)
        upper.append(jnp.where(lane >= first + sub, kept_own * root, 0.0))
        inverse.append(jnp.where(lane <= first + sub, kept_unit * root, 0.0))
        spread = [over_subs(unit, k) for k in range(SUBS)]
        for i in range(s + 1, strips):
            change = tree_sum([over_lanes(rows[i], first + k) * spread[k] for k in range(SUBS)])
            rows[i] = jnp.where(pivots, 0.0, rows[i]) - change
    return jnp.concatenate(upper, axis=0), jnp.concatenate(inverse, axis=0)


def part(j, n=1):
    return slice(j * LANES, (j + n) * LANES)


def factor_columns(count, total, block_at, low_ref, high_ref, low_part_ref, inverse_refs, rest_ref):
    zero = jnp.zeros((LANES, LANES), jnp.float32)

    def held(rows, first, n):
        return high_ref[rows, part(first, n)], low_part_ref[rows, part(first, n)]

    def column_at(i, n):
        value = jnp.concatenate([block_at(m, i) for m in range(i, total)], axis=0)
        return value - dot3(held(part(i, total - i), 0, n), held(part(i), 0, n)) if n else value

    diagonal = block_at(0, 0)
    for j in range(count):
        below = slice((j + 1) * LANES, total * LANES)
        if j + 1 < total:
            ahead = column_at(j, j)[LANES:]
        if j + 1 < count:
            next_diagonal = block_at(j + 1, j + 1)
            if j:
                next_diagonal = next_diagonal - dot3(held(part(j + 1), 0, j), held(part(j + 1), 0, j))
        elif rest_ref is not None:
            remainder = [column_at(i, j) for i in range(count, total)]
        upper, inverse = factor_block(diagonal)
        inverse_parts = split(inverse)
        for ref, value in zip(inverse_refs, inverse_parts):
            ref[part(j), :] = value
        low_ref[part(j), part(j)] = upper.T
        for i in range(j):
            low_ref[part(i), part(j)] = zero
        if j + 1 < total:
            column = dot3(split(ahead), inverse_parts)
            low_ref[below, part(j)] = column
            column_parts = split(column)
            high_ref[below, part(j)], low_part_ref[below, part(j)] = column_parts
        if j + 1 < count:
            first = tuple(v[:LANES] for v in column_parts)
            diagonal = next_diagonal - dot3(first, first)
    for i in range(count, total):
        value = remainder[i - count] - dot3(held(part(i, total - i), count - 1, 1), held(part(i), count - 1, 1))
        rest_ref[part(i - count, total - i), part(i - count)] = value


def first_kernel(ring, count, place_ref, *refs):
    devices = 2 * ring
    pieces = refs[: 2 * devices]
    rows_ref, high_ref, low_part_ref, inverse_high, inverse_low, rest_ref, schur, low_ref, arrived = refs[2 * devices :]
    dev_index, side = place_ref[0], place_ref[1]
    own_z, own_x = dev_index // 2, lax.rem(dev_index, 2)
    half_rows = LANES // 2
    copies = []
    for r in range(ring):
        for q in range(2):
            who = 2 * lax.rem(own_z - r + ring, ring) + lax.rem(own_x + q, 2)
            for other in range(2):
                at = pl.multiple_of(lax.rem(side + other, 2) * half_rows, half_rows)
                number = 2 * (2 * r + q) + other
                copies.append(
                    pltpu.make_async_copy(
                        pieces[number], schur.at[who, :, pl.ds(at, half_rows), :], arrived.at[number]
                    )
                )
    for copy in copies:
        copy.start()
    for copy in copies:
        copy.wait()
    owners, _ = pair_table(ring)

    def block_at(i, j):
        return tree_sum([schur[who, slot] for who, slot in owners[i, j]])

    factor_columns(count, devices, block_at, low_ref, high_ref, low_part_ref, (inverse_high, inverse_low), rest_ref)
    start = pl.multiple_of(dev_index * LANES, LANES)
    rows_ref[...] = low_ref[pl.ds(start, LANES), :]


def more_kernel(count, place_ref, start_ref, rows_ref, out_ref, high_ref, low_part_ref, inverse_high, inverse_low, *refs):
    rest_ref, low_ref = refs if len(refs) == 2 else (None, *refs)
    total = start_ref.shape[0] // LANES
    done = rows_ref.shape[1]
    skipped = place_ref[3] - total

    def block_at(i, j):
        return start_ref[part(i), part(j)]

    factor_columns(count, total, block_at, low_ref, high_ref, low_part_ref, (inverse_high, inverse_low), rest_ref)
    out_ref[:, :done] = rows_ref[...]
    row = (place_ref[0] - skipped) * LANES
    at = pl.multiple_of(jnp.maximum(row, 0), LANES)
    out_ref[:, done:] = jnp.where(row >= 0, low_ref[pl.ds(at, LANES), :], 0.0)


def solve_kernel(ring, groups, place_ref, *refs):
    sums = refs[: sum(summands for _, summands in groups)]
    *parts, panel_ref, held = refs[len(sums) :]
    blocks = 2 * ring
    own_z, own_x = place_ref[0] // 2, lax.rem(place_ref[0], 2)
    for places, summands in groups:
        group, sums = sums[:summands], sums[summands:]
        for n, place in enumerate(places):
            who = 2 * lax.rem(own_z - place // 2 + ring, ring) + lax.rem(own_x + place % 2, 2)
            gram_sum = tree_sum([ref[n] for ref in group])
            held[who] = gram_sum * gram_sum - tree_sum([ref[len(places) + n] for ref in group])
    below = jnp.concatenate([held[i] for i in range(blocks)], axis=1)
    columns = []
    while parts:
        group, parts = parts[:4], parts[4:]
        columns += [(group, n, len(columns)) for n in range(group[0].shape[1] // LANES)]
    for j in range(blocks):
        (high, low, inverse_high, inverse_low), n, skip = columns[j]
        value = dot3(split(below[:, :LANES]), (inverse_high[part(n), :], inverse_low[part(n), :]))
        panel_ref[:, part(j)] = value
        if j + 1 < blocks:
            rest = slice((j + 1 - skip) * LANES, (blocks - skip) * LANES)
            below = below[:, LANES:] - dot3(split(value), (high[rest, part(n)], low[rest, part(n)]))


def gram_of(left, right):
    return lax.dot_general(left, right, (NT, ((), ())), preferred_element_type=jnp.float32)


def head_kernel(ring, place_ref, own, across, own_f, across_f, *refs):
    half = ring // 2
    middle, out_ref = refs[:-1], refs[-1]
    own_z, first_x = place_ref[0] // 2, lax.rem(place_ref[0], 2) == 0
    full = 2 * half - 1
    own_parts, across_parts = split(own_f[...]), split(across_f[...])
    out_ref[0] = gram_of(own[...], own[...])
    out_ref[full] = dot3(own_parts, own_parts)
    for t in range(1, half):
        right, right_parts = middle[2 * t - 2][...], split(middle[2 * t - 1][...])
        values = gram_of(own[...], right), gram_of(across[...], right)
        values += dot3(own_parts, right_parts), dot3(across_parts, right_parts)
        slots = t, half - 1 + t, full + t, full + half - 1 + t
        for slot, value in zip(slots, values):
            out_ref[slot] = jnp.where(own_z >= t, value, value.T)

    @pl.when(first_x)
    def _():
        out_ref[2 * full] = gram_of(across[...], own[...])

    @pl.when(jnp.logical_not(first_x))
    def _():
        out_ref[2 * full] = dot3(own_parts, across_parts)


def far_kernel(ring, place_ref, done, own, across, own_f, across_f, far, far_f, keep_ref, send_ref, held):
    half = ring // 2
    n = done.shape[0]
    rows = LANES // 2
    own_z, side = place_ref[0] // 2, place_ref[1]

    @pl.when(own_z >= half)
    def _():
        for m, left in enumerate((own, across)):
            held[m] = gram_of(left[...], far[...])

    @pl.when(own_z < half)
    def _():
        right = split(far_f[...])
        for m, left in enumerate((own_f, across_f)):
            held[m] = dot3(split(left[...]), right).T

    for ref, at in ((keep_ref, side * rows), (send_ref, (1 - side) * rows)):
        here = pl.ds(pl.multiple_of(at, rows), rows)
        ref[:n] = done[:, here, :]
        ref[n:] = held[:, here, :]


def piece_kernel(ring, place_ref, one_ref, two_ref, out_ref):
    half = ring // 2
    full = 2 * half - 1
    dev_index, side = place_ref[0], place_ref[1]
    _, rows, width = out_ref.shape
    row = lax.broadcasted_iota(jnp.int32, (rows, width), 0) + side * rows
    col = lax.broadcasted_iota(jnp.int32, (rows, width), 1)
    for n in range(full):
        gram_sum = one_ref[n] + two_ref[n]
        value = gram_sum * gram_sum - (one_ref[full + n] + two_ref[full + n])
        out_ref[n] = value + jnp.where(row == col, DAMPING, 0.0) if n == 0 else value
    squared = lax.rem(dev_index, 2) == 0, dev_index // 2 >= half, dev_index // 2 >= half
    for n, is_gram in enumerate(squared):
        value = one_ref[2 * full + n] + two_ref[2 * full + n]
        out_ref[full + n] = jnp.where(is_gram, value * value, -value)


def low_kernel(count, before, place_ref, colloc, factor, *refs):
    blocks = (len(refs) - count - 3 - (count if before else 0)) // 2
    high, low, held = refs[-3:]
    outs = refs[-3 - count : -3]
    earlier = refs[2 * blocks : 2 * blocks + count] if before else ()
    rows = colloc.shape[0] // count
    high[...], low[...] = split(factor[...])
    right = jnp.concatenate([refs[2 * n][...] for n in range(blocks)], axis=0)
    value = gram_of(colloc[...], right)
    for n in range(blocks):
        held[n] = value[:, part(n)].reshape(count, rows, LANES)
    right = jnp.concatenate([refs[2 * n + 1][...] for n in range(blocks)], axis=0)
    value = dot3((high[...], low[...]), split(right))
    for n in range(blocks):
        held[blocks + n] = value[:, part(n)].reshape(count, rows, LANES)
    for k, ref in enumerate(outs):
        for n in range(before):
            ref[n] = earlier[k][n]
            ref[before + blocks + n] = earlier[k][before + n]
        for n in range(blocks):
            ref[before + n] = held[n, place_ref[2] ^ k]
            ref[2 * before + blocks + n] = held[blocks + n, place_ref[2] ^ k]


IN_VMEM = pl.BlockSpec(memory_space=pltpu.VMEM)
IN_SMEM = pl.BlockSpec(memory_space=pltpu.SMEM)
ANYWHERE = pl.BlockSpec(memory_space=pl.ANY)


def params(mebibytes=16):
    return pltpu.CompilerParams(vmem_limit_bytes=mebibytes * 1024 * 1024)


def effort(steps):
    return pl.CostEstimate(flops=steps * 40_000_000, bytes_accessed=0, transcendentals=0)


def factor_shapes(count, total):
    part_shape = jax.ShapeDtypeStruct((total * LANES, count * LANES), jnp.bfloat16)
    inverse_shape = jax.ShapeDtypeStruct((count * LANES, LANES), jnp.bfloat16)
    return [part_shape, part_shape, inverse_shape, inverse_shape]


def factor_first(ring, count, place, pieces):
    blocks = 2 * ring
    slots = pieces[0].shape[0]
    left = (blocks - count) * LANES
    return pl.pallas_call(
        functools.partial(first_kernel, ring, count),
        in_specs=[IN_SMEM] + [ANYWHERE] * len(pieces),
        out_specs=[IN_VMEM] * 6,
        out_shape=[jax.ShapeDtypeStruct((LANES, count * LANES), jnp.float32)]
        + factor_shapes(count, blocks)
        + [jax.ShapeDtypeStruct((left, left), jnp.float32)],
        scratch_shapes=[
            pltpu.VMEM((blocks, slots, LANES, LANES), jnp.float32),
            pltpu.VMEM((blocks * LANES, count * LANES), jnp.float32),
            pltpu.SemaphoreType.DMA((len(pieces),)),
        ],
        compiler_params=params(),
        cost_estimate=effort(count * LANES),
        name="cholesky_first",
    )(place, *pieces)


def factor_more(place, start, rows, count, steps):
    total = start.shape[0] // LANES
    rest = [jax.ShapeDtypeStruct(((total - count) * LANES,) * 2, jnp.float32)] if count < total else []
    return pl.pallas_call(
        functools.partial(more_kernel, count),
        in_specs=[IN_SMEM, IN_VMEM, IN_VMEM],
        out_specs=[IN_VMEM] * (5 + len(rest)),
        out_shape=[jax.ShapeDtypeStruct((LANES, rows.shape[1] + count * LANES), jnp.float32)]
        + factor_shapes(count, total)
        + rest,
        scratch_shapes=[pltpu.VMEM((total * LANES, count * LANES), jnp.float32)],
        compiler_params=params(),
        cost_estimate=effort(count * steps),
        name="cholesky_more",
    )(place, start, rows)


def solve_panel(ring, place, groups, sums, factors):
    rows, blocks = sums[0][0].shape[1], 2 * ring
    flat = [v for group in sums for v in group]
    groups = [(places, len(group)) for places, group in zip(groups, sums)]
    return pl.pallas_call(
        functools.partial(solve_kernel, ring, groups),
        in_specs=[IN_SMEM] + [IN_VMEM] * (len(flat) + 4 * len(factors)),
        out_specs=IN_VMEM,
        out_shape=jax.ShapeDtypeStruct((rows, blocks * LANES), jnp.float32),
        scratch_shapes=[pltpu.VMEM((blocks, rows, LANES), jnp.float32)],
        compiler_params=params(),
        cost_estimate=effort(LANES),
        name="panel_solve",
    )(place, *flat, *(v for group in factors for v in group))


def head_products(ring, place, *operands):
    return pl.pallas_call(
        functools.partial(head_kernel, ring),
        in_specs=[IN_SMEM] + [IN_VMEM] * len(operands),
        out_specs=IN_VMEM,
        out_shape=jax.ShapeDtypeStruct((4 * (ring // 2) - 1, LANES, LANES), jnp.float32),
        compiler_params=params(),
        cost_estimate=effort(64),
        name="head_products",
    )(place, *operands)


def far_products(ring, place, done, *operands):
    shape = (done.shape[0] + 2, LANES // 2, LANES)
    return pl.pallas_call(
        functools.partial(far_kernel, ring),
        in_specs=[IN_SMEM] + [IN_VMEM] * (1 + len(operands)),
        out_specs=[IN_VMEM] * 2,
        out_shape=[jax.ShapeDtypeStruct(shape, jnp.float32)] * 2,
        scratch_shapes=[pltpu.VMEM((2, LANES, LANES), jnp.float32)],
        compiler_params=params(),
        cost_estimate=effort(32),
        name="far_products",
    )(place, done, *operands)


def schur_piece(ring, place, one, two):
    return pl.pallas_call(
        functools.partial(piece_kernel, ring),
        in_specs=[IN_SMEM] + [IN_VMEM] * 2,
        out_specs=IN_VMEM,
        out_shape=jax.ShapeDtypeStruct((2 * (ring // 2) + 2, *one.shape[1:]), jnp.float32),
        compiler_params=params(),
        cost_estimate=effort(16),
        name="schur_piece",
    )(place, one, two)


def low_products(count, place, colloc, factor, blocks, earlier=()):
    rows = colloc.shape[0] // count
    before = earlier[0].shape[0] // 2 if earlier else 0
    flat = [v for pair in blocks for v in pair] + list(earlier)
    n = 2 * len(blocks)
    return pl.pallas_call(
        functools.partial(low_kernel, count, before),
        in_specs=[IN_SMEM] + [IN_VMEM] * (2 + len(flat)),
        out_specs=[IN_VMEM] * count,
        out_shape=[jax.ShapeDtypeStruct((2 * before + n, rows, LANES), jnp.float32)] * count,
        scratch_shapes=[
            pltpu.VMEM(factor.shape, jnp.bfloat16),
            pltpu.VMEM(factor.shape, jnp.bfloat16),
            pltpu.VMEM((n, count, rows, LANES), jnp.float32),
        ],
        compiler_params=params(30),
        cost_estimate=effort(24 * n),
        name="low_products",
    )(place, colloc, factor, *flat)


def pair_table(ring):
    half = ring // 2
    owners = {}
    for z in range(ring):
        for x in range(2):
            me, across = 2 * z + x, 2 * z + 1 - x

            def back(t):
                return 2 * ((z - t) % ring) + x

            pairs = [(me, me)] + [(me, back(t)) for t in range(1, half)]
            pairs += [(across, back(t)) for t in range(1, half)]
            pairs += [(me, across), (me, back(half)), (across, back(half))]
            for slot, pair in enumerate(pairs):
                owners.setdefault((max(pair), min(pair)), []).append((me, slot))
    return owners, 2 * half + 2


def pick(value, axis, index):
    return lax.dynamic_index_in_dim(value, index, axis, keepdims=False)


def ring_step(value, ring, chosen=None):
    steps = [(2 * z + x, 2 * ((z + 1) % ring) + x) for z in range(ring) for x in range(2)]
    return lax.ppermute(value, "dev", [s for s in steps if chosen is None or chosen(s[1] // 2)])


def swap(value, axis, bit, chosen=None):
    steps = [(i, i ^ bit) for i in range(lax.axis_size(axis))]
    return lax.ppermute(value, axis, [s for s in steps if chosen is None or chosen(s[1] // 2)])


def after(value, *first):
    return lax.optimization_barrier((value, *first))[0]


def exchanged(parts):
    return [parts[0]] + [swap(v, "grp", k) for k, v in enumerate(parts) if k]


def halved(parts):
    own, bit, between = [parts[0]], 1, []
    while len(parts) > 1:
        received = [swap(v, "grp", bit) for v in parts[1::2]]
        own.append(received[0])
        parts = [parts[0]] + [v + w for v, w in zip(parts[2::2], received[1:])]
        between += parts[1:]
        bit *= 2
    return own, between


def coded(colloc_rows, factor_rows):
    width = max(colloc_rows.shape[1], factor_rows.shape[1])
    width += -width % LANES
    factor_rows = factor_rows * SCALE
    parts = (colloc_rows.astype(jnp.float32) * VALUE_SCALE, factor_rows * jnp.abs(factor_rows))
    return jnp.stack([padded(v.astype(jnp.float16), width) for v in parts])


def padded(value, width):
    return jnp.pad(value, ((0, 0), (0, width - value.shape[1])))


def narrow(value):
    return (value.astype(jnp.float32) * jnp.float32(1.0 / VALUE_SCALE)).astype(jnp.bfloat16)


def widen(value):
    value = value.astype(jnp.float32)
    root = jnp.sqrt(jnp.abs(value)) * jnp.float32(1.0 / SCALE)
    return jnp.where(value < 0.0, -root, root)


def on_grid(colloc, block_colloc, factor, block_factor):
    ring, count = lax.axis_size("dev") // 2, lax.axis_size("grp")
    half = ring // 2
    dev_index, grp_index = lax.axis_index("dev"), lax.axis_index("grp")
    own_z = dev_index // 2
    place = jnp.stack([dev_index, lax.rem(grp_index, 2), grp_index, 2 * ring]).astype(jnp.int32)

    def is_upper(t):
        return lax.rem(own_z - t + ring, ring) >= half

    def step(v):
        return ring_step(v, ring)

    def cross(v):
        return swap(v, "dev", 1)

    own = coded(block_colloc, block_factor)
    width = own.shape[2]

    def opened(v):
        return narrow(v[0]), widen(v[1])

    along, across = [own], [cross(own)]
    for t in range(1, half):
        along.append(step(along[-1]))
        across.append(cross(along[-1]))
    next_upper = is_upper(-1)
    first = step(pick(along[-1], 0, jnp.where(next_upper, 0, 1)))
    second = step(after(pick(along[-1], 0, jnp.where(next_upper, 1, 0)), first))

    open_along = [opened(v) for v in along]
    open_across = [opened(across[0])]
    wide_colloc, wide_factor = padded(colloc, width), padded(factor, width)
    open_along[0] = after(open_along[0], wide_colloc)
    middle = [v for pair in open_along[1:] for v in pair]
    done = head_products(
        ring, place, open_along[0][0], open_across[0][0], open_along[0][1], open_across[0][1], *middle
    )
    last = after(first, done)
    keep, send = far_products(
        ring,
        place,
        done,
        open_along[0][0],
        open_across[0][0],
        open_along[0][1],
        open_across[0][1],
        narrow(last),
        widen(last),
    )
    total = keep + swap(send, "grp", 1)
    bit = 2
    while 2 * bit < count:
        total = total + swap(total, "grp", bit)
        bit *= 2
    other = swap(total, "grp", bit)

    across_first = cross(after(first, send))

    def low_parts(chosen, earlier=()):
        return low_products(count, place, wide_colloc, wide_factor, chosen, earlier)

    soon = [open_along[0], open_across[0], *open_along[1:]]
    parts_soon = low_parts(after(soon, total))

    piece = schur_piece(ring, place, total, after(other, across[1:], parts_soon))
    hops, crossed, pairs = [piece], [cross(piece)], []
    for r in range(1, ring):
        due = (second,) if r == 1 else (across_first,) if r == 2 else tuple(crossed[: r - 1])
        hops.append(after(step(hops[-1]), *due))
        pairs.append((swap(hops[r - 1], "grp", 1), swap(crossed[r - 1], "grp", 1)))
        crossed.append(cross(hops[-1]))
    pairs.append((swap(hops[-1], "grp", 1), swap(crossed[-1], "grp", 1)))
    across_second = cross(after(second, crossed[-1]))
    far_along = [(step(after(first, hops[-1])), None)]
    pieces = [v for hop, over, pair in zip(hops, crossed, pairs) for v in (hop, pair[0], over, pair[1])]

    def joined(t, one, two):
        upper = is_upper(t - half)
        return narrow(jnp.where(upper, one, two)), widen(jnp.where(upper, two, one))

    far_along[0] = (far_along[0][0], step(after(second, hops[-1])))
    far_across = [(across_first, across_second)]
    held = after([v for t in range(1, half) for v in (across[t],)] + [first, second], crossed[-2])
    early = [opened(v) for v in held[:-2]] + [joined(half, *held[-2:])]
    parts_early = low_parts(early, parts_soon)
    sums_early, between = halved(parts_early)
    pieces[0] = after(pieces[0], parts_early, across_first)
    rows, *one, start = factor_first(ring, ring, place, pieces)
    far_across = [(across_first, across_second)]
    for t in range(half + 1, ring):
        if t > half + 1:
            far_along.append(tuple(step(v) for v in far_along[-1]))
        far_across.append((cross(after(far_along[-1][0], start)), step(after(far_across[-1][1], start))))
    factor_out, *two = factor_more(place, after(start, between), rows, ring, LANES)
    far_along, far_across = after((far_along, far_across), factor_out, sums_early)
    late = [joined(half + t, *v) for t, v in enumerate(far_across)]
    late += [joined(half + 1 + t, *v) for t, v in enumerate(far_along)]
    sums_late, _ = halved(low_parts(late))
    sums = [sums_early, sums_late]
    places_early = [0, 1] + [2 * t for t in range(1, half)] + [2 * t + 1 for t in range(1, half)] + [2 * half]
    places_late = [2 * t + 1 for t in range(half, ring)] + [2 * t for t in range(half + 1, ring)]
    panel = solve_panel(ring, place, [places_early, places_late], sums, [one, two])
    return factor_out, panel[None]


def whole_kernel(place_ref, schur_ref, below_ref, rows_ref, panel_ref, low_ref, high_part, low_part, inverse_high, inverse_low):
    blocks = schur_ref.shape[0] // LANES

    def block_at(i, j):
        return schur_ref[part(i), part(j)]

    factor_columns(blocks, blocks, block_at, low_ref, high_part, low_part, (inverse_high, inverse_low), None)
    for j in range(blocks):
        own = below_ref[:, part(j)]
        if j:
            done = part(0, j)
            own = own - dot3(split(panel_ref[:, done]), (high_part[part(j), done], low_part[part(j), done]))
        panel_ref[:, part(j)] = dot3(split(own), (inverse_high[part(j), :], inverse_low[part(j), :]))
    band = rows_ref.shape[0]
    start = pl.multiple_of(place_ref[0] * band, SUBS)
    rows_ref[...] = low_ref[pl.ds(start, band), :]


def factor_whole(place, schur, below, band):
    size = schur.shape[0]
    return pl.pallas_call(
        whole_kernel,
        in_specs=[IN_SMEM, IN_VMEM, IN_VMEM],
        out_specs=[IN_VMEM, IN_VMEM],
        out_shape=[
            jax.ShapeDtypeStruct((band, size), jnp.float32),
            jax.ShapeDtypeStruct(below.shape, jnp.float32),
        ],
        scratch_shapes=[
            pltpu.VMEM((size, size), jnp.float32),
            pltpu.VMEM((size, size), jnp.bfloat16),
            pltpu.VMEM((size, size), jnp.bfloat16),
            pltpu.VMEM((size, LANES), jnp.bfloat16),
            pltpu.VMEM((size, LANES), jnp.bfloat16),
        ],
        compiler_params=params(30),
        name="cholesky_whole",
    )(place, schur, below)


def on_any(colloc, block_colloc, factor, block_factor):
    grp_count, grp_index, dev_index = lax.axis_size("grp"), lax.axis_index("grp"), lax.axis_index("dev")
    band = block_colloc.shape[0]
    width = band * lax.axis_size("dev")
    points = jnp.concatenate([block_colloc, colloc], axis=0)
    earlier = jnp.concatenate([block_factor, factor], axis=0)
    dims = (((1,), (1,)), ((), ()))
    gram = lax.dot_general(
        points, lax.all_gather(block_colloc, "dev", axis=0, tiled=True), dims, preferred_element_type=jnp.float32
    )
    update = lax.dot_general(
        earlier,
        lax.all_gather(block_factor, "dev", axis=0, tiled=True),
        dims,
        precision=lax.Precision.HIGHEST,
        preferred_element_type=jnp.float32,
    )
    gram_low = lax.psum_scatter(gram[band:], "grp", scatter_dimension=0, tiled=True)
    update_low = lax.psum_scatter(update[band:], "grp", scatter_dimension=0, tiled=True)
    below = gram_low * gram_low - update_low
    slice_width = width // grp_count
    row = dev_index * band + lax.broadcasted_iota(jnp.int32, (band, slice_width), 0)
    col = grp_index * slice_width + lax.broadcasted_iota(jnp.int32, (band, slice_width), 1)
    gram_slice = lax.psum_scatter(gram[:band], "grp", scatter_dimension=1, tiled=True)
    update_slice = lax.psum_scatter(update[:band], "grp", scatter_dimension=1, tiled=True)
    damping = jnp.where(row == col, jnp.float32(DAMPING), jnp.float32(0.0))
    piece = gram_slice * gram_slice + damping - update_slice
    slab = lax.all_gather(piece, "grp", axis=1, tiled=True)
    schur = lax.all_gather(slab, "dev", axis=0, tiled=True)
    place = jnp.reshape(dev_index, (1,)).astype(jnp.int32)
    factor_rows, panel_rows = factor_whole(place, schur, below, band)
    return factor_rows, panel_rows[None]


def on_device(colloc, block_colloc, factor, block_factor):
    devices, count = lax.axis_size("dev"), lax.axis_size("grp")
    gridded = devices % 4 == 0 and devices >= 8 and block_colloc.shape[0] == LANES and count >= 2 and count & (count - 1) == 0
    form = on_grid if gridded else on_any
    return form(colloc, block_colloc, factor, block_factor)


def solution(mesh):
    placed = (P("dev", "grp"), P("dev", "grp"), P("dev", "grp"), P("dev", "grp"))
    return jax.shard_map(
        on_device,
        mesh=mesh,
        in_specs=placed,
        out_specs=(P("dev", None), P("dev", "grp", None)),
        check_vma=False,
    )
```

```python
import functools
import jax
import jax.numpy as jnp
from jax import lax
from jax.sharding import PartitionSpec as P
from jax.experimental import pallas as pl
from jax.experimental.pallas import tpu as pltpu

DAMPING = 0.0625
SCALE = 896.0
VALUE_SCALE = 16384.0
LANES = 128
SUBS = 8
NT = ((1,), (1,))


def split(value):
    high = value.astype(jnp.bfloat16)
    low = (value - high.astype(jnp.float32)).astype(jnp.bfloat16)
    return high, low


def dot3(left, right):
    (left_high, left_low), (right_high, right_low) = left, right
    return lax.dot_general(
        jnp.concatenate([left_high, left_high, left_low], axis=1),
        jnp.concatenate([right_high, right_low, right_high], axis=1),
        (NT, ((), ())),
        preferred_element_type=jnp.float32,
    )


def reciprocal(value):
    return pl.reciprocal(value, approx=True)


def over_lanes(value, column):
    return jnp.broadcast_to(value[:, column : column + 1], (SUBS, LANES))


def over_subs(value, row):
    return jnp.broadcast_to(value[row : row + 1, :], (SUBS, LANES))


def tree_sum(values):
    while len(values) > 1:
        values = [a + b for a, b in zip(values[::2], values[1::2])] + values[len(values) // 2 * 2 :]
    return values[0]


def factor_block(block):
    lane = lax.broadcasted_iota(jnp.int32, (SUBS, LANES), 1)
    sub = lax.broadcasted_iota(jnp.int32, (SUBS, LANES), 0)
    strips = LANES // SUBS
    rows = [block[SUBS * s : SUBS * (s + 1), :] for s in range(strips)]
    upper, inverse = [], []
    for s in range(strips):
        first = SUBS * s
        pivots = (lane >= first) & (lane < first + SUBS)
        own = rows[s]
        unit = jnp.where(lane - first == sub, 1.0, jnp.where(pivots, 0.0, own))
        columns = [over_lanes(own, first + k) for k in range(SUBS)]
        kept_own, kept_unit, diagonal = own, unit, None
        for k in range(0, SUBS, 2):
            one, two = sub == k, sub == k + 1
            both = one | two
            a, b, c = over_subs(columns[k], k), over_subs(columns[k + 1], k), over_subs(columns[k + 1], k + 1)
            det = a * c - b * b
            share = reciprocal(det)
            lead = jnp.where(one, c, jnp.where(two, -b, columns[k + 1] * b - columns[k] * c)) * share
            trail = jnp.where(one, -b, jnp.where(two, a, columns[k] * b - columns[k + 1] * a)) * share

            def swept(value):
                return jnp.where(both, 0.0, value) + (lead * over_subs(value, k) + trail * over_subs(value, k + 1))

            inverse_a = reciprocal(a)
            ratio = b * inverse_a
            second = det * inverse_a
            if k == 0:
                diagonal = jnp.where(two, second, a)
            else:
                diagonal = jnp.where(one, a, jnp.where(two, second, diagonal))
            kept_own = jnp.where(one, own, jnp.where(two, own - ratio * over_subs(own, k), kept_own))
            kept_unit = jnp.where(one, unit, jnp.where(two, unit - ratio * over_subs(unit, k), kept_unit))
            for q in range(k + 2, SUBS):
                columns[q] = swept(columns[q])
            own, unit = swept(own), swept(unit)
        root = lax.rsqrt(diagonal)
        upper.append(jnp.where(lane >= first + sub, kept_own * root, 0.0))
        inverse.append(jnp.where(lane <= first + sub, kept_unit * root, 0.0))
        spread = [over_subs(unit, k) for k in range(SUBS)]
        for i in range(s + 1, strips):
            change = tree_sum([over_lanes(rows[i], first + k) * spread[k] for k in range(SUBS)])
            rows[i] = jnp.where(pivots, 0.0, rows[i]) - change
    return jnp.concatenate(upper, axis=0), jnp.concatenate(inverse, axis=0)


def part(j, n=1):
    return slice(j * LANES, (j + n) * LANES)


def factor_columns(count, total, block_at, low_ref, high_ref, low_part_ref, inverse_refs, rest_ref):
    zero = jnp.zeros((LANES, LANES), jnp.float32)

    def held(rows, first, n):
        return high_ref[rows, part(first, n)], low_part_ref[rows, part(first, n)]

    def column_at(i, n):
        value = jnp.concatenate([block_at(m, i) for m in range(i, total)], axis=0)
        return value - dot3(held(part(i, total - i), 0, n), held(part(i), 0, n)) if n else value

    diagonal = block_at(0, 0)
    for j in range(count):
        below = slice((j + 1) * LANES, total * LANES)
        if j + 1 < total:
            ahead = column_at(j, j)[LANES:]
        if j + 1 < count:
            next_diagonal = block_at(j + 1, j + 1)
            if j:
                next_diagonal = next_diagonal - dot3(held(part(j + 1), 0, j), held(part(j + 1), 0, j))
        elif rest_ref is not None:
            remainder = [column_at(i, j) for i in range(count, total)]
        upper, inverse = factor_block(diagonal)
        inverse_parts = split(inverse)
        for ref, value in zip(inverse_refs, inverse_parts):
            ref[part(j), :] = value
        low_ref[part(j), part(j)] = upper.T
        for i in range(j):
            low_ref[part(i), part(j)] = zero
        if j + 1 < total:
            column = dot3(split(ahead), inverse_parts)
            low_ref[below, part(j)] = column
            column_parts = split(column)
            high_ref[below, part(j)], low_part_ref[below, part(j)] = column_parts
        if j + 1 < count:
            first = tuple(v[:LANES] for v in column_parts)
            diagonal = next_diagonal - dot3(first, first)
    for i in range(count, total):
        value = remainder[i - count] - dot3(held(part(i, total - i), count - 1, 1), held(part(i), count - 1, 1))
        rest_ref[part(i - count, total - i), part(i - count)] = value


def first_kernel(ring, count, place_ref, *refs):
    devices = 2 * ring
    pieces = refs[: 2 * devices]
    rows_ref, high_ref, low_part_ref, inverse_high, inverse_low, rest_ref, schur, low_ref, arrived = refs[2 * devices :]
    dev_index, side = place_ref[0], place_ref[1]
    own_z, own_x = dev_index // 2, lax.rem(dev_index, 2)
    half_rows = LANES // 2
    copies = []
    for r in range(ring):
        for q in range(2):
            who = 2 * lax.rem(own_z - r + ring, ring) + lax.rem(own_x + q, 2)
            for other in range(2):
                at = pl.multiple_of(lax.rem(side + other, 2) * half_rows, half_rows)
                number = 2 * (2 * r + q) + other
                copies.append(
                    pltpu.make_async_copy(
                        pieces[number], schur.at[who, :, pl.ds(at, half_rows), :], arrived.at[number]
                    )
                )
    for copy in copies:
        copy.start()
    for copy in copies:
        copy.wait()
    owners, _ = pair_table(ring)

    def block_at(i, j):
        return tree_sum([schur[who, slot] for who, slot in owners[i, j]])

    factor_columns(count, devices, block_at, low_ref, high_ref, low_part_ref, (inverse_high, inverse_low), rest_ref)
    start = pl.multiple_of(dev_index * LANES, LANES)
    rows_ref[...] = low_ref[pl.ds(start, LANES), :]


def more_kernel(count, place_ref, start_ref, rows_ref, out_ref, high_ref, low_part_ref, inverse_high, inverse_low, *refs):
    rest_ref, low_ref = refs if len(refs) == 2 else (None, *refs)
    total = start_ref.shape[0] // LANES
    done = rows_ref.shape[1]
    skipped = place_ref[3] - total

    def block_at(i, j):
        return start_ref[part(i), part(j)]

    factor_columns(count, total, block_at, low_ref, high_ref, low_part_ref, (inverse_high, inverse_low), rest_ref)
    out_ref[:, :done] = rows_ref[...]
    row = (place_ref[0] - skipped) * LANES
    at = pl.multiple_of(jnp.maximum(row, 0), LANES)
    out_ref[:, done:] = jnp.where(row >= 0, low_ref[pl.ds(at, LANES), :], 0.0)


def solve_kernel(ring, groups, place_ref, *refs):
    sums = refs[: sum(summands for _, summands in groups)]
    *parts, panel_ref, held = refs[len(sums) :]
    blocks = 2 * ring
    own_z, own_x = place_ref[0] // 2, lax.rem(place_ref[0], 2)
    for places, summands in groups:
        group, sums = sums[:summands], sums[summands:]
        for n, place in enumerate(places):
            who = 2 * lax.rem(own_z - place // 2 + ring, ring) + lax.rem(own_x + place % 2, 2)
            gram_sum = tree_sum([ref[n] for ref in group])
            held[who] = gram_sum * gram_sum - tree_sum([ref[len(places) + n] for ref in group])
    below = jnp.concatenate([held[i] for i in range(blocks)], axis=1)
    columns = []
    while parts:
        group, parts = parts[:4], parts[4:]
        columns += [(group, n, len(columns)) for n in range(group[0].shape[1] // LANES)]
    for j in range(blocks):
        (high, low, inverse_high, inverse_low), n, skip = columns[j]
        value = dot3(split(below[:, :LANES]), (inverse_high[part(n), :], inverse_low[part(n), :]))
        panel_ref[:, part(j)] = value
        if j + 1 < blocks:
            rest = slice((j + 1 - skip) * LANES, (blocks - skip) * LANES)
            below = below[:, LANES:] - dot3(split(value), (high[rest, part(n)], low[rest, part(n)]))


def gram_of(left, right):
    return lax.dot_general(left, right, (NT, ((), ())), preferred_element_type=jnp.float32)


def head_kernel(ring, place_ref, own, across, own_f, across_f, *refs):
    half = ring // 2
    middle, out_ref = refs[:-1], refs[-1]
    own_z, first_x = place_ref[0] // 2, lax.rem(place_ref[0], 2) == 0
    full = 2 * half - 1
    own_parts, across_parts = split(own_f[...]), split(across_f[...])
    out_ref[0] = gram_of(own[...], own[...])
    out_ref[full] = dot3(own_parts, own_parts)
    for t in range(1, half):
        right, right_parts = middle[2 * t - 2][...], split(middle[2 * t - 1][...])
        values = gram_of(own[...], right), gram_of(across[...], right)
        values += dot3(own_parts, right_parts), dot3(across_parts, right_parts)
        slots = t, half - 1 + t, full + t, full + half - 1 + t
        for slot, value in zip(slots, values):
            out_ref[slot] = jnp.where(own_z >= t, value, value.T)

    @pl.when(first_x)
    def _():
        out_ref[2 * full] = gram_of(across[...], own[...])

    @pl.when(jnp.logical_not(first_x))
    def _():
        out_ref[2 * full] = dot3(own_parts, across_parts)


def far_kernel(ring, place_ref, done, own, across, own_f, across_f, far, far_f, keep_ref, send_ref, held):
    half = ring // 2
    n = done.shape[0]
    rows = LANES // 2
    own_z, side = place_ref[0] // 2, place_ref[1]

    @pl.when(own_z >= half)
    def _():
        for m, left in enumerate((own, across)):
            held[m] = gram_of(left[...], far[...])

    @pl.when(own_z < half)
    def _():
        right = split(far_f[...])
        for m, left in enumerate((own_f, across_f)):
            held[m] = dot3(split(left[...]), right).T

    for ref, at in ((keep_ref, side * rows), (send_ref, (1 - side) * rows)):
        here = pl.ds(pl.multiple_of(at, rows), rows)
        ref[:n] = done[:, here, :]
        ref[n:] = held[:, here, :]


def piece_kernel(ring, place_ref, one_ref, two_ref, out_ref):
    half = ring // 2
    full = 2 * half - 1
    dev_index, side = place_ref[0], place_ref[1]
    _, rows, width = out_ref.shape
    row = lax.broadcasted_iota(jnp.int32, (rows, width), 0) + side * rows
    col = lax.broadcasted_iota(jnp.int32, (rows, width), 1)
    for n in range(full):
        gram_sum = one_ref[n] + two_ref[n]
        value = gram_sum * gram_sum - (one_ref[full + n] + two_ref[full + n])
        out_ref[n] = value + jnp.where(row == col, DAMPING, 0.0) if n == 0 else value
    squared = lax.rem(dev_index, 2) == 0, dev_index // 2 >= half, dev_index // 2 >= half
    for n, is_gram in enumerate(squared):
        value = one_ref[2 * full + n] + two_ref[2 * full + n]
        out_ref[full + n] = jnp.where(is_gram, value * value, -value)


def low_kernel(count, before, place_ref, colloc, factor, *refs):
    blocks = (len(refs) - count - 3 - (count if before else 0)) // 2
    high, low, held = refs[-3:]
    outs = refs[-3 - count : -3]
    earlier = refs[2 * blocks : 2 * blocks + count] if before else ()
    rows = colloc.shape[0] // count
    high[...], low[...] = split(factor[...])
    right = jnp.concatenate([refs[2 * n][...] for n in range(blocks)], axis=0)
    value = gram_of(colloc[...], right)
    for n in range(blocks):
        held[n] = value[:, part(n)].reshape(count, rows, LANES)
    right = jnp.concatenate([refs[2 * n + 1][...] for n in range(blocks)], axis=0)
    value = dot3((high[...], low[...]), split(right))
    for n in range(blocks):
        held[blocks + n] = value[:, part(n)].reshape(count, rows, LANES)
    for k, ref in enumerate(outs):
        for n in range(before):
            ref[n] = earlier[k][n]
            ref[before + blocks + n] = earlier[k][before + n]
        for n in range(blocks):
            ref[before + n] = held[n, place_ref[2] ^ k]
            ref[2 * before + blocks + n] = held[blocks + n, place_ref[2] ^ k]


IN_VMEM = pl.BlockSpec(memory_space=pltpu.VMEM)
IN_SMEM = pl.BlockSpec(memory_space=pltpu.SMEM)
ANYWHERE = pl.BlockSpec(memory_space=pl.ANY)


def params(mebibytes=16):
    return pltpu.CompilerParams(vmem_limit_bytes=mebibytes * 1024 * 1024)


def effort(steps):
    return pl.CostEstimate(flops=steps * 40_000_000, bytes_accessed=0, transcendentals=0)


def factor_shapes(count, total):
    part_shape = jax.ShapeDtypeStruct((total * LANES, count * LANES), jnp.bfloat16)
    inverse_shape = jax.ShapeDtypeStruct((count * LANES, LANES), jnp.bfloat16)
    return [part_shape, part_shape, inverse_shape, inverse_shape]


def factor_first(ring, count, place, pieces):
    blocks = 2 * ring
    slots = pieces[0].shape[0]
    left = (blocks - count) * LANES
    return pl.pallas_call(
        functools.partial(first_kernel, ring, count),
        in_specs=[IN_SMEM] + [ANYWHERE] * len(pieces),
        out_specs=[IN_VMEM] * 6,
        out_shape=[jax.ShapeDtypeStruct((LANES, count * LANES), jnp.float32)]
        + factor_shapes(count, blocks)
        + [jax.ShapeDtypeStruct((left, left), jnp.float32)],
        scratch_shapes=[
            pltpu.VMEM((blocks, slots, LANES, LANES), jnp.float32),
            pltpu.VMEM((blocks * LANES, count * LANES), jnp.float32),
            pltpu.SemaphoreType.DMA((len(pieces),)),
        ],
        compiler_params=params(),
        cost_estimate=effort(count * LANES),
        name="cholesky_first",
    )(place, *pieces)


def factor_more(place, start, rows, count, steps):
    total = start.shape[0] // LANES
    rest = [jax.ShapeDtypeStruct(((total - count) * LANES,) * 2, jnp.float32)] if count < total else []
    return pl.pallas_call(
        functools.partial(more_kernel, count),
        in_specs=[IN_SMEM, IN_VMEM, IN_VMEM],
        out_specs=[IN_VMEM] * (5 + len(rest)),
        out_shape=[jax.ShapeDtypeStruct((LANES, rows.shape[1] + count * LANES), jnp.float32)]
        + factor_shapes(count, total)
        + rest,
        scratch_shapes=[pltpu.VMEM((total * LANES, count * LANES), jnp.float32)],
        compiler_params=params(),
        cost_estimate=effort(count * steps),
        name="cholesky_more",
    )(place, start, rows)


def solve_panel(ring, place, groups, sums, factors):
    rows, blocks = sums[0][0].shape[1], 2 * ring
    flat = [v for group in sums for v in group]
    groups = [(places, len(group)) for places, group in zip(groups, sums)]
    return pl.pallas_call(
        functools.partial(solve_kernel, ring, groups),
        in_specs=[IN_SMEM] + [IN_VMEM] * (len(flat) + 4 * len(factors)),
        out_specs=IN_VMEM,
        out_shape=jax.ShapeDtypeStruct((rows, blocks * LANES), jnp.float32),
        scratch_shapes=[pltpu.VMEM((blocks, rows, LANES), jnp.float32)],
        compiler_params=params(),
        cost_estimate=effort(LANES),
        name="panel_solve",
    )(place, *flat, *(v for group in factors for v in group))


def head_products(ring, place, *operands):
    return pl.pallas_call(
        functools.partial(head_kernel, ring),
        in_specs=[IN_SMEM] + [IN_VMEM] * len(operands),
        out_specs=IN_VMEM,
        out_shape=jax.ShapeDtypeStruct((4 * (ring // 2) - 1, LANES, LANES), jnp.float32),
        compiler_params=params(),
        cost_estimate=effort(64),
        name="head_products",
    )(place, *operands)


def far_products(ring, place, done, *operands):
    shape = (done.shape[0] + 2, LANES // 2, LANES)
    return pl.pallas_call(
        functools.partial(far_kernel, ring),
        in_specs=[IN_SMEM] + [IN_VMEM] * (1 + len(operands)),
        out_specs=[IN_VMEM] * 2,
        out_shape=[jax.ShapeDtypeStruct(shape, jnp.float32)] * 2,
        scratch_shapes=[pltpu.VMEM((2, LANES, LANES), jnp.float32)],
        compiler_params=params(),
        cost_estimate=effort(32),
        name="far_products",
    )(place, done, *operands)


def schur_piece(ring, place, one, two):
    return pl.pallas_call(
        functools.partial(piece_kernel, ring),
        in_specs=[IN_SMEM] + [IN_VMEM] * 2,
        out_specs=IN_VMEM,
        out_shape=jax.ShapeDtypeStruct((2 * (ring // 2) + 2, *one.shape[1:]), jnp.float32),
        compiler_params=params(),
        cost_estimate=effort(16),
        name="schur_piece",
    )(place, one, two)


def low_products(count, place, colloc, factor, blocks, earlier=()):
    rows = colloc.shape[0] // count
    before = earlier[0].shape[0] // 2 if earlier else 0
    flat = [v for pair in blocks for v in pair] + list(earlier)
    n = 2 * len(blocks)
    return pl.pallas_call(
        functools.partial(low_kernel, count, before),
        in_specs=[IN_SMEM] + [IN_VMEM] * (2 + len(flat)),
        out_specs=[IN_VMEM] * count,
        out_shape=[jax.ShapeDtypeStruct((2 * before + n, rows, LANES), jnp.float32)] * count,
        scratch_shapes=[
            pltpu.VMEM(factor.shape, jnp.bfloat16),
            pltpu.VMEM(factor.shape, jnp.bfloat16),
            pltpu.VMEM((n, count, rows, LANES), jnp.float32),
        ],
        compiler_params=params(30),
        cost_estimate=effort(24 * n),
        name="low_products",
    )(place, colloc, factor, *flat)


def pair_table(ring):
    half = ring // 2
    owners = {}
    for z in range(ring):
        for x in range(2):
            me, across = 2 * z + x, 2 * z + 1 - x

            def back(t):
                return 2 * ((z - t) % ring) + x

            pairs = [(me, me)] + [(me, back(t)) for t in range(1, half)]
            pairs += [(across, back(t)) for t in range(1, half)]
            pairs += [(me, across), (me, back(half)), (across, back(half))]
            for slot, pair in enumerate(pairs):
                owners.setdefault((max(pair), min(pair)), []).append((me, slot))
    return owners, 2 * half + 2


def pick(value, axis, index):
    return lax.dynamic_index_in_dim(value, index, axis, keepdims=False)


def ring_step(value, ring, chosen=None):
    steps = [(2 * z + x, 2 * ((z + 1) % ring) + x) for z in range(ring) for x in range(2)]
    return lax.ppermute(value, "dev", [s for s in steps if chosen is None or chosen(s[1] // 2)])


def swap(value, axis, bit, chosen=None):
    steps = [(i, i ^ bit) for i in range(lax.axis_size(axis))]
    return lax.ppermute(value, axis, [s for s in steps if chosen is None or chosen(s[1] // 2)])


def after(value, *first):
    return lax.optimization_barrier((value, *first))[0]


def exchanged(parts):
    return [parts[0]] + [swap(v, "grp", k) for k, v in enumerate(parts) if k]


def halved(parts):
    own, bit, between = [parts[0]], 1, []
    while len(parts) > 1:
        received = [swap(v, "grp", bit) for v in parts[1::2]]
        own.append(received[0])
        parts = [parts[0]] + [v + w for v, w in zip(parts[2::2], received[1:])]
        between += parts[1:]
        bit *= 2
    return own, between


def coded(colloc_rows, factor_rows):
    width = max(colloc_rows.shape[1], factor_rows.shape[1])
    width += -width % LANES
    factor_rows = factor_rows * SCALE
    parts = (colloc_rows.astype(jnp.float32) * VALUE_SCALE, factor_rows * jnp.abs(factor_rows))
    return jnp.stack([padded(v.astype(jnp.float16), width) for v in parts])


def padded(value, width):
    return jnp.pad(value, ((0, 0), (0, width - value.shape[1])))


def narrow(value):
    return (value.astype(jnp.float32) * jnp.float32(1.0 / VALUE_SCALE)).astype(jnp.bfloat16)


def widen(value):
    value = value.astype(jnp.float32)
    root = jnp.sqrt(jnp.abs(value)) * jnp.float32(1.0 / SCALE)
    return jnp.where(value < 0.0, -root, root)


def on_grid(colloc, block_colloc, factor, block_factor):
    ring, count = lax.axis_size("dev") // 2, lax.axis_size("grp")
    half = ring // 2
    dev_index, grp_index = lax.axis_index("dev"), lax.axis_index("grp")
    own_z = dev_index // 2
    place = jnp.stack([dev_index, lax.rem(grp_index, 2), grp_index, 2 * ring]).astype(jnp.int32)

    def is_upper(t):
        return lax.rem(own_z - t + ring, ring) >= half

    def step(v):
        return ring_step(v, ring)

    def cross(v):
        return swap(v, "dev", 1)

    own = coded(block_colloc, block_factor)
    width = own.shape[2]

    def opened(v):
        return narrow(v[0]), widen(v[1])

    along, across = [own], [cross(own)]
    for t in range(1, half):
        along.append(step(along[-1]))
        across.append(cross(along[-1]))
    next_upper = is_upper(-1)
    first = step(pick(along[-1], 0, jnp.where(next_upper, 0, 1)))
    second = step(after(pick(along[-1], 0, jnp.where(next_upper, 1, 0)), first))

    open_along = [opened(v) for v in along]
    open_across = [opened(across[0])]
    wide_colloc, wide_factor = padded(colloc, width), padded(factor, width)
    open_along[0] = after(open_along[0], wide_colloc)
    middle = [v for pair in open_along[1:] for v in pair]
    done = head_products(
        ring, place, open_along[0][0], open_across[0][0], open_along[0][1], open_across[0][1], *middle
    )
    last = after(first, done)
    keep, send = far_products(
        ring,
        place,
        done,
        open_along[0][0],
        open_across[0][0],
        open_along[0][1],
        open_across[0][1],
        narrow(last),
        widen(last),
    )
    total = keep + swap(send, "grp", 1)
    bit = 2
    while 2 * bit < count:
        total = total + swap(total, "grp", bit)
        bit *= 2
    other = swap(total, "grp", bit)

    across_first = cross(after(first, send))

    def low_parts(chosen, earlier=()):
        return low_products(count, place, wide_colloc, wide_factor, chosen, earlier)

    soon = [open_along[0], open_across[0], *open_along[1:]]
    parts_soon = low_parts(after(soon, total))

    piece = schur_piece(ring, place, total, after(other, across[1:], parts_soon))
    hops, crossed, pairs = [piece], [cross(piece)], []
    for r in range(1, ring):
        due = (second,) if r == 1 else (across_first,) if r == 2 else tuple(crossed[: r - 1])
        hops.append(after(step(hops[-1]), *due))
        pairs.append((swap(hops[r - 1], "grp", 1), swap(crossed[r - 1], "grp", 1)))
        crossed.append(cross(hops[-1]))
    pairs.append((swap(hops[-1], "grp", 1), swap(crossed[-1], "grp", 1)))
    across_second = cross(-after(second, crossed[-1]))
    far_along = [(step(-after(first, hops[-1])), None)]
    pieces = [v for hop, over, pair in zip(hops, crossed, pairs) for v in (hop, pair[0], over, pair[1])]

    def joined(t, one, two):
        upper = is_upper(t - half)
        return narrow(jnp.where(upper, one, two)), widen(jnp.where(upper, two, one))

    far_along[0] = (far_along[0][0], step(-after(second, hops[-1])))
    far_across = [(across_first, across_second)]
    held = after([v for t in range(1, half) for v in (across[t],)] + [first, second], crossed[-2])
    early = [opened(v) for v in held[:-2]] + [joined(half, *held[-2:])]
    parts_early = low_parts(early, parts_soon)
    sums_early, between = halved(parts_early)
    pieces[0] = after(pieces[0], parts_early, across_first)
    rows, *one, start = factor_first(ring, ring, place, pieces)
    far_across = [(across_first, across_second)]
    for t in range(half + 1, ring):
        if t > half + 1:
            far_along.append(tuple(step(v) for v in far_along[-1]))
        far_across.append((cross(after(far_along[-1][0], start)), step(after(far_across[-1][1], start))))
    factor_out, *two = factor_more(place, after(start, between), rows, ring, LANES)
    far_along, far_across = after((far_along, far_across), factor_out, sums_early)
    late = [joined(half, far_across[0][0], -far_across[0][1])]
    late += [joined(half + 1 + t, -v[0], -v[1]) for t, v in enumerate(far_across[1:])]
    late += [joined(half + 1 + t, -v[0], -v[1]) for t, v in enumerate(far_along)]
    sums_late, _ = halved(low_parts(late))
    sums = [sums_early, sums_late]
    places_early = [0, 1] + [2 * t for t in range(1, half)] + [2 * t + 1 for t in range(1, half)] + [2 * half]
    places_late = [2 * t + 1 for t in range(half, ring)] + [2 * t for t in range(half + 1, ring)]
    panel = solve_panel(ring, place, [places_early, places_late], sums, [one, two])
    return factor_out, panel[None]


def whole_kernel(place_ref, schur_ref, below_ref, rows_ref, panel_ref, low_ref, high_part, low_part, inverse_high, inverse_low):
    blocks = schur_ref.shape[0] // LANES

    def block_at(i, j):
        return schur_ref[part(i), part(j)]

    factor_columns(blocks, blocks, block_at, low_ref, high_part, low_part, (inverse_high, inverse_low), None)
    for j in range(blocks):
        own = below_ref[:, part(j)]
        if j:
            done = part(0, j)
            own = own - dot3(split(panel_ref[:, done]), (high_part[part(j), done], low_part[part(j), done]))
        panel_ref[:, part(j)] = dot3(split(own), (inverse_high[part(j), :], inverse_low[part(j), :]))
    band = rows_ref.shape[0]
    start = pl.multiple_of(place_ref[0] * band, SUBS)
    rows_ref[...] = low_ref[pl.ds(start, band), :]


def factor_whole(place, schur, below, band):
    size = schur.shape[0]
    return pl.pallas_call(
        whole_kernel,
        in_specs=[IN_SMEM, IN_VMEM, IN_VMEM],
        out_specs=[IN_VMEM, IN_VMEM],
        out_shape=[
            jax.ShapeDtypeStruct((band, size), jnp.float32),
            jax.ShapeDtypeStruct(below.shape, jnp.float32),
        ],
        scratch_shapes=[
            pltpu.VMEM((size, size), jnp.float32),
            pltpu.VMEM((size, size), jnp.bfloat16),
            pltpu.VMEM((size, size), jnp.bfloat16),
            pltpu.VMEM((size, LANES), jnp.bfloat16),
            pltpu.VMEM((size, LANES), jnp.bfloat16),
        ],
        compiler_params=params(30),
        name="cholesky_whole",
    )(place, schur, below)


def on_any(colloc, block_colloc, factor, block_factor):
    grp_count, grp_index, dev_index = lax.axis_size("grp"), lax.axis_index("grp"), lax.axis_index("dev")
    band = block_colloc.shape[0]
    width = band * lax.axis_size("dev")
    points = jnp.concatenate([block_colloc, colloc], axis=0)
    earlier = jnp.concatenate([block_factor, factor], axis=0)
    dims = (((1,), (1,)), ((), ()))
    gram = lax.dot_general(
        points, lax.all_gather(block_colloc, "dev", axis=0, tiled=True), dims, preferred_element_type=jnp.float32
    )
    update = lax.dot_general(
        earlier,
        lax.all_gather(block_factor, "dev", axis=0, tiled=True),
        dims,
        precision=lax.Precision.HIGHEST,
        preferred_element_type=jnp.float32,
    )
    gram_low = lax.psum_scatter(gram[band:], "grp", scatter_dimension=0, tiled=True)
    update_low = lax.psum_scatter(update[band:], "grp", scatter_dimension=0, tiled=True)
    below = gram_low * gram_low - update_low
    slice_width = width // grp_count
    row = dev_index * band + lax.broadcasted_iota(jnp.int32, (band, slice_width), 0)
    col = grp_index * slice_width + lax.broadcasted_iota(jnp.int32, (band, slice_width), 1)
    gram_slice = lax.psum_scatter(gram[:band], "grp", scatter_dimension=1, tiled=True)
    update_slice = lax.psum_scatter(update[:band], "grp", scatter_dimension=1, tiled=True)
    damping = jnp.where(row == col, jnp.float32(DAMPING), jnp.float32(0.0))
    piece = gram_slice * gram_slice + damping - update_slice
    slab = lax.all_gather(piece, "grp", axis=1, tiled=True)
    schur = lax.all_gather(slab, "dev", axis=0, tiled=True)
    place = jnp.reshape(dev_index, (1,)).astype(jnp.int32)
    factor_rows, panel_rows = factor_whole(place, schur, below, band)
    return factor_rows, panel_rows[None]


def on_device(colloc, block_colloc, factor, block_factor):
    devices, count = lax.axis_size("dev"), lax.axis_size("grp")
    gridded = devices % 4 == 0 and devices >= 8 and block_colloc.shape[0] == LANES and count >= 2 and count & (count - 1) == 0
    form = on_grid if gridded else on_any
    return form(colloc, block_colloc, factor, block_factor)


def solution(mesh):
    placed = (P("dev", "grp"), P("dev", "grp"), P("dev", "grp"), P("dev", "grp"))
    return jax.shard_map(
        on_device,
        mesh=mesh,
        in_specs=placed,
        out_specs=(P("dev", None), P("dev", "grp", None)),
        check_vma=False,
    )
```
